32 devices in a mesh: dp: 4 (over y, x), seq: 2 (over core), head: 4 (over z).
Axes of the slice: x: 2, y: 2, z: 4, core: 2. Of those that a mesh axis runs over, the one named last changes fastest.
Arguments:
- x_in: bfloat16 [8, 1024, 1536], P('dp', 'seq'), may hold values from -6 to 6
- d_out: bfloat16 [8, 1024, 1536], P('dp', 'seq'), may hold values from -6 to 6
- log_decay: float32 [8, 1024, 48], P('dp', 'seq', 'head'), may hold values from -1 to 0
- routes: int32 [8, 1024, 6], P('dp', 'seq'), may hold values from 0 to 15, all different within a row; in each aligned block of 128 rows (0 to 127, 128 to 255, ..., all dimensions but the last counted through in order) at most 96 rows name the same one
- norm1_gain: float32 [1536], replicated, may hold values from 0.5 to 1.5
- w_in_zx: bfloat16 [2, 1536, 3072], P(None, None, 'head'), may hold values from -0.15625 to 0.15625
- w_in_bc: bfloat16 [1536, 256], replicated, may hold values from -0.0390625 to 0.0390625
- w_in_dt: bfloat16 [1536, 48], P(None, 'head'), may hold values from -0.15625 to 0.15625
- dt_bias: float32 [48], P('head'), may hold values from -1 to 1
- conv_x: float32 [4, 3072], P(None, 'head'), may hold values from -3 to 3
- conv_x_bias: float32 [3072], P('head'), may hold values from -1.5 to 1.5
- conv_bc: float32 [4, 256], replicated, may hold values from -3 to 3
- conv_bc_bias: float32 [256], replicated, may hold values from -0.25 to 0.25
- skip_d: float32 [48], P('head'), may hold values from 0.5 to 1.5
- gate_norm_gain: float32 [3072], P('head'), may hold values from 0.5 to 1.5
- w_out: bfloat16 [3072, 1536], P('head'), may hold values from -0.109375 to 0.109375
- norm2_gain: float32 [1536], replicated, may hold values from 0.5 to 1.5
- router: bfloat16 [1536, 16], replicated, may hold values from -0.078125 to 0.078125
- w_expert_gu: bfloat16 [16, 1536, 1024], P(('seq', 'head')), may hold values from -0.15625 to 0.15625
- w_expert_down: bfloat16 [16, 512, 1536], P(('seq', 'head')), may hold values from -0.25 to 0.25
- w_shared_gu: bfloat16 [2, 1536, 1024], P(None, None, 'head'), may hold values from -0.15625 to 0.15625
- w_shared_down: bfloat16 [1024, 1536], P('head'), may hold values from -0.1875 to 0.1875
Outputs:
- layer_out: bfloat16 [8, 1024, 1536], P('dp', 'seq')
- d_input: bfloat16 [8, 1024, 1536], P('dp', 'seq')
- grad_norm1_gain: float32 [1536], replicated
- grad_w_in_zx: float32 [2, 1536, 3072], P(None, ('dp', 'seq'), 'head')
- grad_w_in_bc: float32 [1536, 256], replicated
- grad_w_in_dt: float32 [1536, 48], P(('dp', 'seq'), 'head')
- grad_dt_bias: float32 [48], replicated
- grad_conv_x: float32 [4, 3072], replicated
- grad_conv_x_bias: float32 [3072], replicated
- grad_conv_bc: float32 [4, 256], replicated
- grad_conv_bc_bias: float32 [256], replicated
- grad_skip_d: float32 [48], replicated
- grad_gate_norm_gain: float32 [3072], replicated
- grad_w_out: float32 [3072, 1536], P('head', ('dp', 'seq'))
- grad_norm2_gain: float32 [1536], replicated
- grad_router: float32 [1536, 16], replicated
- grad_expert_gu: float32 [16, 1536, 1024], P(('seq', 'head'), 'dp')
- grad_expert_down: float32 [16, 512, 1536], P(('seq', 'head'), None, 'dp')
- grad_shared_gu: float32 [2, 1536, 1024], P(None, ('dp', 'seq'), 'head')
- grad_shared_down: float32 [1024, 1536], P('head', ('dp', 'seq'))
The draws below stay inside these ranges and needn't reach their ends.
Inputs may be any that keep to these rules, and one draw needn't show every extreme that they name: `routes`: in each aligned block of 128 positions (sequence by sequence, in order), no expert is named by more than 96 positions; each position names 6 different experts.
All inputs are finite; a program needn't handle non-finite values.
Results may differ from the reference program's by a relative error of at most 0.015.
The reference program's roundings to bfloat16 on the way (of `normed_one`, `conv_in`, `conv_act`, `gated_low`, `normed_two`, `shared_act`, `expert_act` and `expert_out`) count: a program that leaves them out, or rounds other values in their place, can miss the bound.
Values may be sent and summed in bfloat16 or wider, within the bound.
No kernel may reach another device: no remote copies, remote signals or barrier semaphores. Data moves between devices by JAX's collectives and lax.ppermute only.
A program may use at most 384 MiB of HBM per device.

```python
import math
from functools import partial
import jax
import jax.numpy as jnp
import numpy as np
from jax import lax

D = 1536
HEADS = 48
HDIM = 64
STATE = 128
CONV = 4
BLOCK = 256
FFE = 512
FFS = 1024
TOPK = 6
SEQUENCE_LENGTH = 1024
TOK_DEV = 512
BATCH_ROWS = 8
INNER = 3072
EXPERTS = 16
ROWS = 128
CAP = 96


def draw_log_decay(key, part):
    random_keys = jax.random.split(key, 7)
    slow_share = 0.5
    slow_heads = jax.random.uniform(random_keys[0], (HEADS,)) < slow_share
    slow_rate = 0.15 / SEQUENCE_LENGTH * jnp.exp(jax.random.uniform(random_keys[1], (HEADS,), minval=0.0, maxval=math.log(2.0)))
    fast_rate = jnp.exp(-jax.random.uniform(random_keys[2], (HEADS,), minval=math.log(8.0), maxval=math.log(40.0)))
    head_speed = jnp.where(slow_heads, slow_rate, fast_rate)
    span_count = SEQUENCE_LENGTH // TOK_DEV
    device_multiplier = jnp.exp(jax.random.uniform(random_keys[3], (BATCH_ROWS, span_count, 1, HEADS), minval=-0.5, maxval=0.5))
    device_multiplier = jnp.broadcast_to(device_multiplier, (BATCH_ROWS, span_count, TOK_DEV, HEADS)).reshape(BATCH_ROWS, SEQUENCE_LENGTH, HEADS)
    token_multiplier = jax.random.uniform(random_keys[4], (BATCH_ROWS, SEQUENCE_LENGTH, HEADS), minval=0.5, maxval=1.5)
    surge_position = jax.random.randint(random_keys[5], (BATCH_ROWS, 2), 0, SEQUENCE_LENGTH)
    surge_strike = jnp.any(jnp.arange(SEQUENCE_LENGTH)[None, :, None] == surge_position[:, None, :], axis=-1)
    surge_falloff = jnp.log(jax.random.uniform(random_keys[6], (BATCH_ROWS, SEQUENCE_LENGTH, 1), minval=0.6, maxval=0.8))
    final_result = -head_speed * device_multiplier * token_multiplier + jnp.where(surge_strike[..., None], surge_falloff, 0.0)
    return final_result.astype(jnp.float32)


def levels(rng, shape, cuts, smallest, largest):
    level = 1.0
    for position, shards_of in cuts:
        draws = jax.random.uniform(jax.random.fold_in(jax.random.fold_in(rng, 6), position), (shards_of,), jnp.float32, smallest / len(cuts), largest / len(cuts))
        level = level * jnp.repeat(jnp.exp(draws), shape[position] // shards_of).reshape((-1,) + (1,) * (len(shape) - 1 - position))
    return level


def assign_block(stream_key, own, number, rows, number_of, top, limit, slope):
    order = jax.random.permutation(stream_key, number_of)
    packed, common = portions_of(number_of, rows * top, limit, slope, True), portions_of(number_of, rows * top, limit, slope, False)
    places = jnp.arange(number_of)

    def named(lengths, turn):
        used = int((lengths > 0).sum())
        fixed = max(1, used // 4)
        shifted = fixed + (places - fixed + turn * (used - fixed)) % max(1, number_of - fixed)
        return jnp.zeros((number_of,), jnp.int32).at[order[jnp.where(places < fixed, places, shifted)]].set(jnp.asarray(lengths, jnp.int32))

    lengths = jnp.where(number % 4 == 0, named(packed, number // 4), named(common, number - number // 4 - 1))
    mixed = jax.random.permutation(jax.random.fold_in(own, 3), number_of)
    source_of, receiver = mixed[0:number_of // 2 * 2:2], mixed[1:number_of // 2 * 2:2]
    room = jnp.minimum(lengths[source_of] - 1, limit - lengths[receiver]) // 2
    room = jnp.where((source_of == order[0]) | (receiver == order[0]) | (lengths[receiver] == 0), 0, jnp.maximum(room, 0))
    shifted = jax.random.randint(jax.random.fold_in(own, 4), (number_of // 2,), 0, 1 << 20) % (room + 1)
    lengths = lengths.at[source_of].add(-shifted).at[receiver].add(shifted)
    members = jnp.searchsorted(jnp.cumsum(lengths), jnp.arange(rows * top), side="right").astype(jnp.int32)
    table = members.reshape(top, rows).T
    table = table[jax.random.permutation(jax.random.fold_in(own, 1), rows)]
    turn = jax.random.randint(jax.random.fold_in(own, 2), (rows, 1), 0, top)
    return jnp.take_along_axis(table, (jnp.arange(top)[None, :] + turn) % top, axis=1)


def portions_of(number_of, total, most, lean, full):
    portions = [(1 << 20) // math.isqrt(standing ** lean) + 1 for standing in range(1, number_of + 1)]
    largest = most if full else min(most, max(-(-total // number_of), total * portions[0] // sum(portions)))
    least = 1 if total - largest >= number_of - 1 else 0
    counts, rest = [largest] + [least] * (number_of - 1), total - largest - least * (number_of - 1)
    while rest > 0:
        candidates = [i for i in range(1, number_of) if counts[i] < largest] or [i for i in range(1, number_of) if counts[i] < most]
        pool, left = sum([portions[i] for i in candidates]), rest
        for i in candidates:
            addition = min(most - counts[i], max(1, left * portions[i] // pool), rest)
            counts[i] = counts[i] + addition
            rest = rest - addition
    return np.array(counts)


def noise(key, dims, width, reach, cuts=(), kind=jnp.bfloat16):
    entries = width * jax.random.normal(key, dims, jnp.float32)
    if cuts:
        entries = entries * levels(key, dims, cuts, -0.22, 0.18)
    return jnp.clip(entries, -reach, reach).astype(kind)


def setup_inputs(seed: int = 0) -> dict:
    seeds = jax.random.split(jax.random.key(seed), 23)
    x_in = noise(seeds[0], (BATCH_ROWS, SEQUENCE_LENGTH, D), 1.0, 6.0, ((0, 4), (1, 2)))
    d_out = noise(seeds[1], (BATCH_ROWS, SEQUENCE_LENGTH, D), 1.0, 6.0, ((0, 4), (1, 2)))
    log_decay = draw_log_decay(jax.random.fold_in(seeds[22], 71), 0)
    routes_keys = jax.random.split(jax.random.fold_in(seeds[3], 1), BATCH_ROWS * SEQUENCE_LENGTH // ROWS)
    routes_turns = jax.random.permutation(jax.random.fold_in(seeds[3], 3), BATCH_ROWS * SEQUENCE_LENGTH // ROWS)
    routes = jax.vmap(lambda own, number: assign_block(jax.random.fold_in(seeds[3], 2), own, number, ROWS, EXPERTS, TOPK, CAP, 1))(routes_keys, routes_turns).reshape((BATCH_ROWS, SEQUENCE_LENGTH, TOPK))
    norm1_gain = jnp.clip(1.0 + 0.1 * jax.random.normal(seeds[4], (D,), jnp.float32), 0.5, 1.5)
    w_in_zx = noise(seeds[5], (2, D, INNER), D ** -0.5, 0.15625, ((2, 4),))
    w_in_bc = noise(seeds[6], (D, 2 * STATE), (16 * D) ** -0.5, 0.0390625)
    w_in_dt = noise(seeds[7], (D, HEADS), D ** -0.5, 0.15625, ((1, 4),))
    dt_bias = jnp.clip(jax.random.uniform(seeds[8], (HEADS,), jnp.float32, -1.0, 1.0) * levels(seeds[8], (HEADS,), ((0, 4),), -0.4, 0.0), -1.0, 1.0)
    conv_x = noise(seeds[9], (CONV, INNER), CONV ** -0.5, 3.0, ((1, 4),), jnp.float32)
    conv_x_bias = noise(seeds[10], (INNER,), 0.3, 1.5, ((0, 4),), jnp.float32)
    conv_bc = noise(seeds[11], (CONV, 2 * STATE), CONV ** -0.5, 3.0, (), jnp.float32)
    conv_bc_bias = noise(seeds[12], (2 * STATE,), 0.05, 0.25, (), jnp.float32)
    skip_d = jnp.clip(0.5 + 1.0 * jax.random.uniform(seeds[13], (HEADS,), jnp.float32) ** levels(seeds[13], (HEADS,), ((0, 4),), -0.2, 0.2), 0.5, 1.5)
    gate_norm_gain = jnp.clip(1.0 + 0.1 * jax.random.normal(seeds[14], (INNER,), jnp.float32), 0.5, 1.5)
    w_out = noise(seeds[15], (INNER, D), INNER ** -0.5, 0.109375, ((0, 4),))
    norm2_gain = jnp.clip(1.0 + 0.1 * jax.random.normal(seeds[16], (D,), jnp.float32), 0.5, 1.5)
    router = noise(seeds[17], (D, EXPERTS), (4 * D) ** -0.5, 0.078125)
    w_expert_gu = noise(seeds[18], (EXPERTS, D, 2 * FFE), D ** -0.5, 0.15625, ((0, 8),))
    w_expert_down = noise(seeds[19], (EXPERTS, FFE, D), FFE ** -0.5, 0.25, ((0, 8),))
    w_shared_gu = noise(seeds[20], (2, D, FFS), D ** -0.5, 0.15625, ((2, 4),))
    w_shared_down = noise(seeds[21], (FFS, D), FFS ** -0.5, 0.1875, ((0, 4),))
    return {"x_in": x_in, "d_out": d_out, "log_decay": log_decay, "routes": routes, "norm1_gain": norm1_gain, "w_in_zx": w_in_zx, "w_in_bc": w_in_bc, "w_in_dt": w_in_dt, "dt_bias": dt_bias, "conv_x": conv_x, "conv_x_bias": conv_x_bias, "conv_bc": conv_bc, "conv_bc_bias": conv_bc_bias, "skip_d": skip_d, "gate_norm_gain": gate_norm_gain, "w_out": w_out, "norm2_gain": norm2_gain, "router": router, "w_expert_gu": w_expert_gu, "w_expert_down": w_expert_down, "w_shared_gu": w_shared_gu, "w_shared_down": w_shared_down}


norm_eps = 1e-05
highest = lax.Precision.HIGHEST

@jax.custom_vjp
def low(v):
    return lax.optimization_barrier(v.astype(jnp.bfloat16)).astype(jnp.float32)

@jax.custom_vjp
def low_back(v):
    return v

def low_keep(v):
    return (low(v), None)

def low_pass(kept, grad):
    return (grad,)

def back_keep(v):
    return (v, None)

def back_low(kept, grad):
    return (low(grad),)
low.defvjp(low_keep, low_pass)
low_back.defvjp(back_keep, back_low)

def scan_block(skip_gain, state_now, pieces):
    input_x, map_b, map_c, step_block, decay_block = pieces
    within = jnp.cumsum(decay_block, axis=0)
    block_len = decay_block.shape[0]
    causal = (jnp.arange(block_len)[:, None] >= jnp.arange(block_len)[None, :])[:, :, None]
    pair_gaps = within[:, None, :] - within[None, :, :]
    decays = jnp.where(causal, jnp.exp(jnp.where(causal, pair_gaps, 0.0)), 0.0)
    scores = jnp.dot(map_c, map_b.T, precision=highest)
    scaled = input_x * step_block[:, :, None]
    inside = jnp.einsum('tsh,shp->thp', decays * scores[:, :, None], scaled, precision=highest)
    carried = jnp.exp(within)[:, :, None] * jnp.einsum('tn,hpn->thp', map_c, state_now, precision=highest)
    final_result = inside + carried + skip_gain[None, :, None] * input_x
    tail_decay = jnp.exp(within[-1][None, :] - within)
    new_state = jnp.exp(within[-1])[:, None, None] * state_now + jnp.einsum('sh,shp,sn->hpn', tail_decay, scaled, map_b, precision=highest)
    return (new_state, final_result)

def expert_apply(pieces):
    weight_gu, weight_down, rows_in = pieces
    rows_in = low_back(rows_in)
    expert_gu = low_back(jnp.dot(rows_in, weight_gu, precision=highest))
    expert_act = low(jax.nn.silu(expert_gu[:, :FFE]) * expert_gu[:, FFE:])
    return low_back(low(jnp.dot(expert_act, weight_down, precision=highest)))

def forward(input_wide, weights, decay, route):
    gain_one, w_zx, w_bc, w_dt, bias_dt, conv_xw, conv_xb, conv_bw, conv_bb, skip_gain, gain_gate, w_mix, gain_two, w_router, w_egu, w_edown, w_sgu, w_sdown = weights
    scale_one = lax.rsqrt(lax.optimization_barrier(jnp.mean(input_wide * input_wide, axis=-1, keepdims=True)) + norm_eps)
    normed_one = low(input_wide * scale_one * gain_one)
    gate_z = low_back(jnp.dot(normed_one, w_zx[0], precision=highest))
    x_part = low_back(low(jnp.dot(normed_one, w_zx[1], precision=highest)))
    bc_part = low(jnp.dot(normed_one, w_bc, precision=highest))
    step_raw = jnp.dot(normed_one, w_dt, precision=highest)
    conv_in = jnp.concatenate([x_part, bc_part], axis=-1)
    padded = jnp.pad(conv_in, ((CONV - 1, 0), (0, 0)))
    conv_weight = jnp.concatenate([conv_xw, conv_bw], axis=1)
    conv_pre = jnp.concatenate([conv_xb, conv_bb])[None, :]
    for offset in range(CONV):
        conv_pre = conv_pre + conv_weight[offset] * padded[offset:offset + SEQUENCE_LENGTH]
    conv_act = low(jax.nn.silu(conv_pre))
    input_x = conv_act[:, :INNER].reshape(SEQUENCE_LENGTH, HEADS, HDIM)
    map_b = conv_act[:, INNER:INNER + STATE]
    map_c = conv_act[:, INNER + STATE:]
    step_size = jax.nn.softplus(step_raw + bias_dt)
    blocks = SEQUENCE_LENGTH // BLOCK
    pieces = (input_x.reshape(blocks, BLOCK, HEADS, HDIM), map_b.reshape(blocks, BLOCK, STATE), map_c.reshape(blocks, BLOCK, STATE), step_size.reshape(blocks, BLOCK, HEADS), decay.reshape(blocks, BLOCK, HEADS))
    start_state = jnp.zeros((HEADS, HDIM, STATE), jnp.float32)
    _, scanned = lax.scan(jax.checkpoint(partial(scan_block, skip_gain)), start_state, pieces)
    gated = scanned.reshape(SEQUENCE_LENGTH, INNER) * jax.nn.silu(gate_z)
    gate_scale = lax.rsqrt(lax.optimization_barrier(jnp.mean(gated * gated, axis=-1, keepdims=True)) + norm_eps)
    gated_low = low(gated * gain_gate)
    mix_proj = low_back(jnp.dot(gated_low, w_mix, precision=highest))
    hidden = input_wide + mix_proj * gate_scale
    scale_two = lax.rsqrt(lax.optimization_barrier(jnp.mean(hidden * hidden, axis=-1, keepdims=True)) + norm_eps)
    normed_two = low(hidden * scale_two * gain_two)
    shared_gu = low_back(jnp.einsum('td,cdf->ctf', normed_two, w_sgu, precision=highest))
    shared_act = low(jax.nn.silu(shared_gu[0]) * shared_gu[1])
    shared_out = jnp.dot(shared_act, w_sdown, precision=highest)
    logits = jnp.dot(normed_two, w_router, precision=highest)
    picked = jnp.take_along_axis(logits, route, axis=1)
    gate_weights = jax.nn.softmax(picked, axis=-1)
    flat_routes = route.reshape(-1)
    route_hits = (flat_routes[:, None] == jnp.arange(EXPERTS, dtype=jnp.int32)[None, :]).astype(jnp.int32)
    slot_ranks = lax.optimization_barrier(jnp.sum((jnp.cumsum(route_hits, axis=0) - route_hits) * route_hits, axis=1))
    slot_count = SEQUENCE_LENGTH // ROWS * CAP
    slot_pos = flat_routes * slot_count + slot_ranks
    filled = jnp.zeros((EXPERTS * slot_count,), jnp.int32).at[slot_pos].set(jnp.arange(SEQUENCE_LENGTH * TOPK, dtype=jnp.int32) + 1)
    row_pick = jnp.where(filled > 0, (filled - 1) // TOPK + 1, 0)
    rows_pad = jnp.concatenate([jnp.zeros((1, D), jnp.float32), normed_two], axis=0)
    rows_in = rows_pad[row_pick].reshape(EXPERTS, slot_count, D)
    expert_out = lax.map(jax.checkpoint(expert_apply), (w_egu, w_edown, rows_in))
    assigned = expert_out.reshape(EXPERTS * slot_count, D)[slot_pos].reshape(SEQUENCE_LENGTH, TOPK, D)
    routed = lax.optimization_barrier(jnp.sum(gate_weights[:, :, None] * assigned, axis=1))
    return hidden + shared_out + routed

def reference(x_in, d_out, log_decay, routes, norm1_gain, w_in_zx, w_in_bc, w_in_dt, dt_bias, conv_x, conv_x_bias, conv_bc, conv_bc_bias, skip_d, gate_norm_gain, w_out, norm2_gain, router, w_expert_gu, w_expert_down, w_shared_gu, w_shared_down):
    weights = tuple((array_in.astype(jnp.float32) for array_in in (norm1_gain, w_in_zx, w_in_bc, w_in_dt, dt_bias, conv_x, conv_x_bias, conv_bc, conv_bc_bias, skip_d, gate_norm_gain, w_out, norm2_gain, router, w_expert_gu, w_expert_down, w_shared_gu, w_shared_down)))

    def one_sequence(totals, pieces):
        input_seq, grad_seq, decay_seq, route_seq = pieces

        def run_layer(input_value, weight_value):
            return forward(input_value, weight_value, decay_seq, route_seq)
        final_result, pull_back = jax.vjp(run_layer, input_seq.astype(jnp.float32), weights)
        input_grad, weight_grads = pull_back(grad_seq.astype(jnp.float32))
        totals = jax.tree.map(jnp.add, totals, weight_grads)
        return (totals, (final_result.astype(jnp.bfloat16), input_grad.astype(jnp.bfloat16)))
    zero_grads = jax.tree.map(jnp.zeros_like, weights)
    totals, (outputs, input_grads) = lax.scan(one_sequence, zero_grads, (x_in, d_out, log_decay, routes))
    return (outputs, input_grads, totals[0], totals[1], totals[2], totals[3], totals[4], totals[5], totals[6], totals[7], totals[8], totals[9], totals[10], totals[11], totals[12], totals[13], totals[14], totals[15], totals[16], totals[17])
```

```python
import jax
import jax.numpy as jnp
from jax import lax
from jax.sharding import PartitionSpec as P

BLOCK = 256


norm_eps = 1e-05
highest = lax.Precision.HIGHEST


def shifted(array, axis, by):
    count = lax.axis_size(axis)
    pairs = [(i, i + by) for i in range(count) if 0 <= i + by < count]
    return lax.ppermute(array, axis, pairs)


def prefix(part, axis, combine, identity):
    place = lax.axis_index(axis)
    gathered = jax.tree.map(lambda a: lax.all_gather(a, axis), part)
    state = jax.tree.map(lambda a, e: jnp.zeros_like(a) + jnp.asarray(e, a.dtype), part, identity)

    def one(lap, state):
        return combine(
            state, jax.tree.map(lambda a: lax.dynamic_index_in_dim(a, lap, 0, False), gathered)
        )

    return lax.fori_loop(0, place, one, state)


def prefix_2(array, axis, combine, identity):
    count, place = (lax.axis_size(axis), lax.axis_index(axis))
    everything = jax.tree.map(
        lambda part, kind: lax.all_gather(part.astype(kind), axis),
        array,
        jax.tree.map(lambda a: jnp.bfloat16 if a.dtype == jnp.float32 else a.dtype, array),
    )
    start = jax.tree.map(
        lambda part, zero: jnp.broadcast_to(jnp.asarray(zero, part.dtype), part.shape),
        array,
        identity,
    )

    def lap(k, before):
        at = count - 1 - k
        reached = at > place
        new = combine(
            before, jax.tree.map(lambda part, own: part[at].astype(own.dtype), everything, array)
        )
        return jax.tree.map(lambda a, b: jnp.where(reached, a, b), new, before)

    return lax.fori_loop(0, count, lap, start)


def silu_slope(argument):
    sigma = jax.nn.sigmoid(argument)
    return sigma * (1.0 + argument * (1.0 - sigma))


def running_sum(values):
    count = values.shape[2]
    lower = (jnp.arange(count)[:, None] >= jnp.arange(count)[None, :]).astype(jnp.float32)
    return jnp.einsum("ts,bksh->bkth", lower, values, precision=highest)


def sum_shares(part):
    count = lax.axis_size("head")
    batch_size, tokens, width = part.shape
    pieces = part.reshape(batch_size, count, tokens // count, width)
    got = lax.all_to_all(pieces, "head", split_axis=1, concat_axis=1, tiled=True)
    return jnp.sum(got.astype(jnp.float32), axis=1)


def gather_shares(share):
    count = lax.axis_size("head")
    batch_size, rows, width = share.shape
    copies = jnp.broadcast_to(share[:, None], (batch_size, count, rows, width))
    got = lax.all_to_all(copies, "head", split_axis=1, concat_axis=1, tiled=True)
    return got.reshape(batch_size, count * rows, width)


def around(array, by):
    count = lax.axis_size("seq")
    if by % count == 0:
        return array
    return lax.ppermute(array, "seq", [(i, (i + by) % count) for i in range(count)])


def spread_last(local_part, rank_index, part_count):
    local_width = local_part.shape[-1]
    full_array = jnp.zeros(local_part.shape[:-1] + (local_width * part_count,), jnp.float32)
    return lax.dynamic_update_slice_in_dim(
        full_array, local_part, rank_index * local_width, local_part.ndim - 1
    )


def block_states(scaled, map_b, within, block_total):
    tail_decay = jnp.exp(block_total[:, :, None, :] - within)
    return jnp.einsum("bksh,bkshp,bksn->bkhpn", tail_decay, scaled, map_b, precision=highest)


def leaving_state(states, before, block_total, device_total):
    weights_out = jnp.exp(device_total[:, None, :] - before - block_total)
    return jnp.einsum("bjh,bjhpn->bhpn", weights_out, states, precision=highest)


def scan_output(scaled, map_b, map_c, within, before, block_total, states, entering):
    block_len = within.shape[2]
    causal = (jnp.arange(block_len)[:, None] >= jnp.arange(block_len)[None, :])[
        None, None, :, :, None
    ]
    pair_gaps = within[:, :, :, None, :] - within[:, :, None, :, :]
    decays = jnp.where(causal, jnp.exp(jnp.where(causal, pair_gaps, 0.0)), 0.0)
    scores = jnp.einsum("bkqn,bksn->bkqs", map_c, map_b, precision=highest)
    inside = jnp.einsum("bkqsh,bkshp->bkqhp", decays * scores[..., None], scaled, precision=highest)
    after_block = before + block_total
    block_count = before.shape[1]
    earlier = (jnp.arange(block_count)[:, None] > jnp.arange(block_count)[None, :])[
        None, :, :, None
    ]
    gap_spans = before[:, :, None, :] - after_block[:, None, :, :]
    link_weights = jnp.where(earlier, jnp.exp(jnp.where(earlier, gap_spans, 0.0)), 0.0)
    starting = jnp.exp(before)[..., None, None] * entering[:, None] + jnp.einsum(
        "bkjh,bjhpn->bkhpn", link_weights, states, precision=highest
    )
    carried = (
        jnp.einsum("bkqn,bkhpn->bkqhp", map_c, starting, precision=highest)
        * jnp.exp(within)[..., None]
    )
    return inside + carried


def chain_forward(earlier, later):
    return (earlier[0] * later[0], later[0][..., None, None] * earlier[1] + later[1])


def chain_backward(earlier, later):
    return (earlier[0] * later[0], later[1] + later[0][..., None, None] * earlier[1])


def local(
    x_in,
    d_out,
    log_decay,
    routes,
    norm1_gain,
    w_in_zx,
    w_in_bc,
    w_in_dt,
    dt_bias,
    conv_x,
    conv_x_bias,
    conv_bc,
    conv_bc_bias,
    skip_d,
    gate_norm_gain,
    w_out,
    norm2_gain,
    router,
    w_expert_gu,
    w_expert_down,
    w_shared_gu,
    w_shared_down,
):
    f32, bf16 = jnp.float32, jnp.bfloat16
    batch_size, tokens, model_width = x_in.shape
    inner_dev = w_in_zx.shape[2]
    heads_dev = w_in_dt.shape[1]
    head_size = inner_dev // heads_dev
    state_size = w_in_bc.shape[1] // 2
    conv_taps = conv_x.shape[0]
    experts_dev = w_expert_gu.shape[0]
    expert_ff = w_expert_down.shape[1]
    head_count = lax.axis_size("head")
    seq_count = lax.axis_size("seq")
    head_rank = lax.axis_index("head")
    seq_rank = lax.axis_index("seq")
    inner_all = inner_dev * head_count
    experts_all = experts_dev * seq_count * head_count
    share_rows = tokens // head_count
    share_start = head_rank * share_rows
    blocks = tokens // BLOCK

    def blockify(array_in):
        return array_in.reshape((batch_size, blocks, BLOCK) + array_in.shape[2:])

    def own_share(array):
        return lax.dynamic_slice_in_dim(array, share_start, share_rows, 1)

    grads_in = [around(d_out, k) for k in range(seq_count)]
    input_wide = x_in.astype(f32)
    scale_one = lax.rsqrt(jnp.mean(input_wide * input_wide, axis=-1, keepdims=True) + norm_eps)
    normed_one = (input_wide * scale_one * norm1_gain).astype(bf16)
    proj_zx = jnp.einsum("btd,cdk->cbtk", normed_one, w_in_zx, preferred_element_type=f32)
    gate_z = proj_zx[0]
    bc_proj = jnp.einsum("btd,dn->btn", normed_one, w_in_bc, preferred_element_type=f32)
    step_raw = jnp.einsum("btd,dh->bth", normed_one, w_in_dt, preferred_element_type=f32)
    conv_in = jnp.concatenate([proj_zx[1], bc_proj], axis=-1).astype(bf16)
    edge_rows = shifted(conv_in[:, tokens - (conv_taps - 1) :, :], "seq", 1)
    padded = jnp.concatenate([edge_rows, conv_in], axis=1).astype(f32)
    conv_weight = jnp.concatenate([conv_x, conv_bc], axis=1)
    conv_bias = jnp.concatenate([conv_x_bias, conv_bc_bias])
    conv_pre = jnp.broadcast_to(conv_bias, padded[:, :tokens].shape)
    for offset in range(conv_taps):
        conv_pre = conv_pre + conv_weight[offset] * padded[:, offset : offset + tokens, :]
    conv_act = jax.nn.silu(conv_pre).astype(bf16)
    input_x = (
        conv_act[..., :inner_dev].astype(f32).reshape(batch_size, tokens, heads_dev, head_size)
    )
    input_b = conv_act[..., inner_dev : inner_dev + state_size].astype(f32)
    input_c = conv_act[..., inner_dev + state_size :].astype(f32)
    step_size = jax.nn.softplus(step_raw + dt_bias)
    within = running_sum(log_decay.reshape(batch_size, blocks, BLOCK, heads_dev))
    block_total = within[:, :, -1, :]
    before = [jnp.zeros_like(block_total[:, 0])]
    for k in range(blocks - 1):
        before.append(before[-1] + block_total[:, k])
    before = jnp.stack(before, axis=1)
    device_total = jnp.sum(block_total, axis=1)
    device_decay = jnp.exp(device_total)
    scaled = blockify(input_x * step_size[..., None])
    b_blocks = blockify(input_b)
    states = block_states(scaled, b_blocks, within, block_total)
    leaving = leaving_state(states, before, block_total, device_total)
    identity = (jnp.ones_like(device_decay), jnp.zeros_like(leaving))
    if seq_count == 2:
        entering = shifted(leaving, "seq", 1)
    else:
        _, entering = prefix((device_decay, leaving), "seq", chain_forward, identity)
    scanned = scan_output(
        scaled, b_blocks, blockify(input_c), within, before, block_total, states, entering
    )
    mixed = scanned.reshape(batch_size, tokens, heads_dev, head_size) + skip_d[:, None] * input_x
    mixed_flat = mixed.reshape(batch_size, tokens, inner_dev)
    z_silu = jax.nn.silu(gate_z)
    gated = mixed_flat * z_silu
    squares = jnp.sum(gated * gated, axis=-1)
    gated_low = (gated * gate_norm_gain).astype(bf16)
    partial_out = jnp.einsum("btk,kd->btd", gated_low, w_out, preferred_element_type=f32)

    mix_out = sum_shares(partial_out.astype(bf16))
    squares = sum_shares(squares[..., None])[..., 0]
    gate_scale = lax.rsqrt(squares / inner_all + norm_eps)[..., None]
    hidden = own_share(x_in).astype(f32) + mix_out * gate_scale
    scale_two = lax.rsqrt(jnp.mean(hidden * hidden, axis=-1, keepdims=True) + norm_eps)
    normed_share = (hidden * scale_two * norm2_gain).astype(bf16)
    normed_two = gather_shares(normed_share)

    expert_ids = jnp.arange(experts_all, dtype=jnp.int32)
    used = jnp.any(routes[..., None] == expert_ids, axis=2)
    logits = jnp.einsum("btd,de->bte", normed_two, router, preferred_element_type=f32)
    top = jnp.max(jnp.where(used, logits, -jnp.inf), axis=-1, keepdims=True)
    powers = jnp.where(used, jnp.exp(jnp.where(used, logits - top, 0.0)), 0.0)
    gates = powers / jnp.sum(powers, axis=-1, keepdims=True)
    gates_across = jnp.transpose(gates, (0, 2, 1))

    shared_gu = jnp.einsum("btd,cdf->cbtf", normed_two, w_shared_gu, preferred_element_type=f32)
    shared_act = (jax.nn.silu(shared_gu[0]) * shared_gu[1]).astype(bf16)
    shared_out = jnp.einsum("btf,fd->btd", shared_act, w_shared_down, preferred_element_type=f32)
    shared_push = jnp.einsum("btd,fd->btf", d_out, w_shared_down, preferred_element_type=f32)
    shared_gu_grad = jnp.stack(
        [
            shared_push * shared_gu[1] * silu_slope(shared_gu[0]),
            shared_push * jax.nn.silu(shared_gu[0]),
        ]
    ).astype(bf16)
    shared_dx = jnp.einsum(
        "cbtf,cdf->btd", shared_gu_grad, w_shared_gu, preferred_element_type=f32
    )
    grad_shared_down = jnp.einsum(
        "btf,btd->df", shared_act, d_out, preferred_element_type=f32
    )
    grad_shared_gu = jnp.einsum(
        "btd,cbtf->dcf", normed_two, shared_gu_grad, preferred_element_type=f32
    )

    first_expert = (seq_rank * head_count + head_rank) * experts_dev
    ffn_out, ffn_dx = shared_out, shared_dx
    pushes = []
    grad_expert_gu = grad_expert_down = 0.0
    for k in range(seq_count):
        rows = around(normed_two, k)
        grads = grads_in[k]
        weights = lax.dynamic_slice_in_dim(around(gates_across, k), first_expert, experts_dev, 1)
        weights = jnp.transpose(weights, (1, 0, 2))[..., None]
        expert_gu = jnp.einsum("btd,edf->ebtf", rows, w_expert_gu, preferred_element_type=f32)
        gate_part, up_part = expert_gu[..., :expert_ff], expert_gu[..., expert_ff:]
        expert_act = (jax.nn.silu(gate_part) * up_part).astype(bf16)
        expert_out = jnp.einsum(
            "ebtf,efd->ebtd", expert_act, w_expert_down, preferred_element_type=f32
        ).astype(bf16)
        push = (weights * grads.astype(f32)).astype(bf16)
        act_push = jnp.einsum("ebtd,efd->ebtf", push, w_expert_down, preferred_element_type=f32)
        gu_grad = jnp.concatenate(
            [act_push * up_part * silu_slope(gate_part), act_push * jax.nn.silu(gate_part)],
            axis=-1,
        ).astype(bf16)
        expert_dx = jnp.einsum(
            "ebtf,edf->ebtd", gu_grad, w_expert_gu, preferred_element_type=f32
        ).astype(bf16)
        gate_push = jnp.sum(grads.astype(f32) * expert_out.astype(f32), axis=-1)
        routed = jnp.sum(weights * expert_out.astype(f32), axis=0)
        routed_dx = jnp.sum(expert_dx.astype(f32), axis=0)
        grad_expert_down = grad_expert_down + jnp.einsum(
            "ebtf,ebtd->edf", expert_act, push, preferred_element_type=f32
        )
        grad_expert_gu = grad_expert_gu + jnp.einsum(
            "btd,ebtf->edf", rows, gu_grad, preferred_element_type=f32
        )
        if k == 0:
            ffn_out, ffn_dx = ffn_out + routed, ffn_dx + routed_dx
        else:
            ffn_out = ffn_out + around(routed.astype(bf16), -k).astype(f32)
            ffn_dx = ffn_dx + around(routed_dx.astype(bf16), -k).astype(f32)
        pushes.append(around(gate_push, -k))

    pushes = jnp.stack(pushes + pushes)
    pushes = lax.dynamic_slice_in_dim(pushes, (seq_count - seq_rank) % seq_count, seq_count, 0)
    pushes = pushes.reshape(seq_count * experts_dev * batch_size, head_count, share_rows)
    pushes = lax.all_to_all(pushes, "head", split_axis=1, concat_axis=1, tiled=True)
    pushes = pushes.reshape(seq_count, experts_dev, batch_size, head_count, share_rows)
    pushes = jnp.transpose(pushes, (2, 4, 0, 3, 1)).reshape(batch_size, share_rows, experts_all)
    gates_share = own_share(gates)
    logit_grad = gates_share * (pushes - jnp.sum(gates_share * pushes, axis=-1, keepdims=True))
    grad_router = jnp.einsum(
        "brd,bre->de",
        normed_share,
        logit_grad,
        precision=highest,
        preferred_element_type=f32,
    )

    ffn_share = sum_shares(ffn_out.astype(bf16))
    layer_out = gather_shares((hidden + ffn_share).astype(bf16))

    normed_two_grad = sum_shares(ffn_dx.astype(bf16)) + jnp.einsum(
        "bre,de->brd", logit_grad, router.astype(f32), precision=highest
    )
    gained_two = normed_two_grad * norm2_gain
    hidden_grad = own_share(d_out).astype(f32) + scale_two * (
        gained_two
        - hidden * scale_two * scale_two * jnp.mean(gained_two * hidden, axis=-1, keepdims=True)
    )
    grad_norm_two = jnp.sum(normed_two_grad * hidden * scale_two, axis=(0, 1))
    scale_push = jnp.sum(hidden_grad * mix_out, axis=-1)
    squares_grad = -0.5 * scale_push * gate_scale[..., 0] ** 3 / inner_all
    squares_grad = gather_shares(squares_grad[..., None])
    out_push = gather_shares((hidden_grad * gate_scale).astype(bf16))

    gated_grad_low = jnp.einsum("btd,kd->btk", out_push, w_out, preferred_element_type=f32)
    grad_w_out = jnp.einsum("btk,btd->dk", gated_low, out_push, preferred_element_type=f32)
    gated_grad = gated_grad_low * gate_norm_gain + 2.0 * gated * squares_grad
    grad_gate_gain = jnp.sum(gated_grad_low * gated, axis=(0, 1))
    mixed_grad = (gated_grad * z_silu).reshape(batch_size, tokens, heads_dev, head_size)
    z_grad = (gated_grad * mixed_flat * silu_slope(gate_z)).astype(bf16)
    grad_skip = jnp.sum(mixed_grad * input_x, axis=(0, 1, 3))
    device_cum = jnp.exp(before[:, :, None, :] + within).reshape(batch_size, tokens, heads_dev)
    entering_grad = jnp.einsum(
        "bth,bthp,btn->bhpn", device_cum, mixed_grad, input_c, precision=highest
    )
    if seq_count == 2:
        leaving_grad = shifted(entering_grad.astype(bf16), "seq", -1).astype(f32)
    else:
        _, leaving_grad = prefix_2((device_decay, entering_grad), "seq", chain_backward, identity)

    def mixer_local(x_value, b_value, c_value, step_value):
        scaled_value = blockify(x_value * step_value[..., None])
        b_value_blocks = blockify(b_value)
        state_value = block_states(scaled_value, b_value_blocks, within, block_total)
        outputs = scan_output(
            scaled_value,
            b_value_blocks,
            blockify(c_value),
            within,
            before,
            block_total,
            state_value,
            entering,
        )
        return (
            outputs.reshape(x_value.shape),
            leaving_state(state_value, before, block_total, device_total),
        )

    _, pull_back = jax.vjp(mixer_local, input_x, input_b, input_c, step_size)
    x_grad, b_grad, c_grad, step_grad = pull_back((mixed_grad, leaving_grad))
    x_grad = x_grad + skip_d[:, None] * mixed_grad
    raw_grad = step_grad * jax.nn.sigmoid(step_raw + dt_bias)
    grad_dt_bias = jnp.sum(raw_grad, axis=(0, 1))
    act_grad = jnp.concatenate(
        [x_grad.reshape(batch_size, tokens, inner_dev), b_grad, c_grad], axis=-1
    )
    pre_grad = act_grad * silu_slope(conv_pre)
    grad_conv = jnp.stack(
        [
            jnp.sum(pre_grad * padded[:, offset : offset + tokens, :], axis=(0, 1))
            for offset in range(conv_taps)
        ]
    )
    grad_conv_bias = jnp.sum(pre_grad, axis=(0, 1))
    next_rows = shifted(pre_grad[:, : conv_taps - 1, :], "seq", -1)
    extended = jnp.concatenate([pre_grad, next_rows], axis=1)
    in_grad = sum(
        conv_weight[conv_taps - 1 - k] * extended[:, k : k + tokens, :] for k in range(conv_taps)
    )
    x_in_grad = in_grad[..., :inner_dev].astype(bf16)
    bc_grad = in_grad[..., inner_dev:]
    zx_grad = jnp.concatenate([z_grad, x_in_grad], axis=-1)
    grad_w_zx = jnp.einsum("btd,btk->dk", normed_one, zx_grad, preferred_element_type=f32)
    grad_w_bc = jnp.einsum(
        "btd,btn->dn", normed_one, bc_grad.astype(bf16), preferred_element_type=f32
    )
    grad_w_dt = jnp.einsum(
        "btd,bth->dh", normed_one, raw_grad.astype(bf16), preferred_element_type=f32
    )
    normed_one_grad = jnp.einsum(
        "btk,dk->btd", z_grad, w_in_zx[0], preferred_element_type=f32
    ) + jnp.einsum("btk,dk->btd", x_in_grad, w_in_zx[1], preferred_element_type=f32)
    small_grad = jnp.concatenate([bc_grad, raw_grad], axis=-1).astype(bf16)
    small_weight = jnp.concatenate([w_in_bc, w_in_dt], axis=-1)
    normed_one_grad = normed_one_grad + jnp.einsum(
        "btn,dn->btd", small_grad, small_weight, preferred_element_type=f32
    )
    normed_one_grad = sum_shares(normed_one_grad.astype(bf16))
    gained_one = normed_one_grad * norm1_gain
    input_share, scale_share = own_share(input_wide), own_share(scale_one)
    input_grad = hidden_grad + scale_share * (
        gained_one
        - input_share
        * scale_share
        * scale_share
        * jnp.mean(gained_one * input_share, axis=-1, keepdims=True)
    )
    grad_norm_one = jnp.sum(normed_one_grad * input_share * scale_share, axis=(0, 1))
    d_input = gather_shares(input_grad.astype(bf16))
    small_sums = lax.psum(
        (
            grad_norm_one,
            grad_norm_two,
            grad_router,
            grad_w_bc,
            grad_conv[:, inner_dev:],
            grad_conv_bias[inner_dev:],
            spread_last(grad_conv[:, :inner_dev], head_rank, head_count),
            spread_last(grad_conv_bias[:inner_dev], head_rank, head_count),
            spread_last(grad_gate_gain, head_rank, head_count),
            spread_last(grad_dt_bias, head_rank, head_count),
            spread_last(grad_skip, head_rank, head_count),
        ),
        ("dp", "seq", "head"),
    )

    def scattered(array, axes):
        return lax.psum_scatter(
            array.astype(bf16), axes, scatter_dimension=0, tiled=True
        ).astype(f32)

    grad_zx = scattered(grad_w_zx, ("dp", "seq"))
    grad_zx = jnp.stack([grad_zx[:, :inner_dev], grad_zx[:, inner_dev:]])
    grad_out = scattered(grad_w_out, ("dp", "seq")).T
    grad_gu = scattered(grad_shared_gu.reshape(model_width, -1), ("dp", "seq"))
    grad_gu = jnp.transpose(grad_gu.reshape(grad_gu.shape[0], 2, -1), (1, 0, 2))
    grad_down = scattered(grad_shared_down, ("dp", "seq")).T
    grad_dt = scattered(grad_w_dt, ("dp", "seq"))
    expert_gu_sum = lax.psum_scatter(
        grad_expert_gu.astype(bf16), "dp", scatter_dimension=1, tiled=True
    ).astype(f32)
    expert_down_sum = lax.psum_scatter(
        grad_expert_down.astype(bf16), "dp", scatter_dimension=1, tiled=True
    ).astype(f32)
    expert_down_sum = jnp.transpose(expert_down_sum, (0, 2, 1))
    return (
        layer_out,
        d_input,
        small_sums[0],
        grad_zx,
        small_sums[3],
        grad_dt,
        small_sums[9],
        small_sums[6],
        small_sums[7],
        small_sums[4],
        small_sums[5],
        small_sums[10],
        small_sums[8],
        grad_out,
        small_sums[1],
        small_sums[2],
        expert_gu_sum,
        expert_down_sum,
        grad_gu,
        grad_down,
    )


def solution(mesh):
    placed = (
        P("dp", "seq", None),
        P("dp", "seq", None),
        P("dp", "seq", "head"),
        P("dp", "seq", None),
        P(),
        P(None, None, "head"),
        P(),
        P(None, "head"),
        P("head"),
        P(None, "head"),
        P("head"),
        P(),
        P(),
        P("head"),
        P("head"),
        P("head", None),
        P(),
        P(),
        P(("seq", "head"), None, None),
        P(("seq", "head"), None, None),
        P(None, None, "head"),
        P("head", None),
    )
    return jax.shard_map(
        local,
        mesh=mesh,
        in_specs=placed,
        out_specs=(
            P("dp", "seq", None),
            P("dp", "seq", None),
            P(),
            P(None, ("dp", "seq"), "head"),
            P(),
            P(("dp", "seq"), "head"),
            P(),
            P(),
            P(),
            P(),
            P(),
            P(),
            P(),
            P("head", ("dp", "seq")),
            P(),
            P(),
            P(("seq", "head"), "dp", None),
            P(("seq", "head"), None, "dp"),
            P(None, ("dp", "seq"), "head"),
            P("head", ("dp", "seq")),
        ),
        check_vma=False,
    )
```

```python
import jax
import jax.numpy as jnp
from jax import lax
from jax.experimental import pallas as pl
from jax.experimental.pallas import tpu as pltpu
from jax.sharding import PartitionSpec as P

BLOCK = 256
ROWS = 256

bf16, f32 = jnp.bfloat16, jnp.float32
norm_eps = 1e-05
highest = lax.Precision.HIGHEST


def dot_nn(a, b):
    return lax.dot_general(a, b, (((1,), (0,)), ((), ())), preferred_element_type=f32)


def dot_nt(a, b):
    return lax.dot_general(a, b, (((1,), (1,)), ((), ())), preferred_element_type=f32)


def dot_tn(a, b):
    return lax.dot_general(a, b, (((0,), (0,)), ((), ())), preferred_element_type=f32)


def lower_mask(count, flip=False):
    rows = lax.broadcasted_iota(jnp.int32, (count, count), 0)
    columns = lax.broadcasted_iota(jnp.int32, (count, count), 1)
    return columns >= rows if flip else rows >= columns


def sum_down(values):
    lower = lower_mask(values.shape[0]).astype(f32)
    return jnp.dot(lower, values, precision=highest, preferred_element_type=f32)


def sum_right(values):
    upper = lower_mask(values.shape[1], True).astype(f32)
    return jnp.dot(values, upper, precision=highest, preferred_element_type=f32)


def first_half(rows, width=128):
    return lax.broadcasted_iota(jnp.int32, (rows, width), 1) < width // 2


def per_channel(values, head_size):
    rows, heads = values.shape
    left = first_half(rows, 2 * head_size)
    return jnp.concatenate(
        [jnp.where(left, values[:, h : h + 1], values[:, h + 1 : h + 2]) for h in range(0, heads, 2)],
        axis=1,
    )


def joined(ref):
    return ref[...].reshape(-1, ref.shape[-1])


def softplus(v):
    return jnp.maximum(v, 0.0) + jnp.log1p(jnp.exp(-jnp.abs(v)))


def scan_kernel(cin, edge, taps, raw, bias, decay, decay_t, act_ref, y_ref, start_ref, leave_ref, buf, prev, state):
    heads = decay.shape[1]
    block = BLOCK
    inner = y_ref.shape[2]
    size = state.shape[0]
    head_size = inner // heads
    pair = 2 * head_size
    count = 4

    @pl.when(pl.program_id(1) == 0)
    def _():
        prev[...] = edge[...]
        state[...] = jnp.zeros_like(state)

    buf[0:8, :] = prev[...]
    buf[8 : 8 + block, :] = joined(cin).astype(f32)
    pre = taps[4:5, :] + sum(taps[k : k + 1, :] * buf[5 + k : 5 + k + block, :] for k in range(count))
    prev[...] = buf[block : block + 8, :]
    act = (pre * jax.nn.sigmoid(pre)).astype(bf16)
    act_ref[...] = act.reshape(act_ref.shape)
    map_b, map_c = act[:, inner : inner + size], act[:, inner + size :]
    step = softplus(joined(raw) + bias[...])
    scaled = act[:, :inner].astype(f32) * per_channel(step, head_size)
    within, across = sum_down(decay[...]), sum_right(decay_t[...])
    grown = per_channel(jnp.exp(within), head_size)
    tail = per_channel(jnp.exp(within[block - 1 :, :] - within), head_size)
    before = state[...]
    start_ref[...] = before
    carried = grown * dot_nn(map_c, before.astype(bf16))
    scores = dot_nt(map_c, map_b)
    causal = lower_mask(block)
    low = scaled.astype(bf16)
    left = first_half(block, pair)
    for h in range(0, heads, 2):
        columns = slice(h * head_size, h * head_size + pair)
        halves = []
        for a in (h, h + 1):
            gap = jnp.where(causal, within[:, a : a + 1] - across[a : a + 1, :], -1e30)
            halves.append(dot_nn((jnp.exp(gap) * scores).astype(bf16), low[:, columns]))
        y_pair = carried[:, columns] + jnp.where(left, halves[0], halves[1])
        y_ref[:, :, columns] = y_pair.reshape(y_ref.shape[:2] + (pair,))
    after = grown[block - 1 :, :] * before + dot_tn(map_b, (scaled * tail).astype(bf16))
    state[...] = after
    leave_ref[...] = after


def gate_kernel(y, act_in, z, decay, lead, entering, skip, gain, w_out, mixed_ref, low_ref, squares_ref, out_ref):
    heads = decay.shape[1]
    inner = y.shape[2]
    size = entering.shape[0]
    grown = per_channel(jnp.exp(sum_down(decay[...])), inner // heads) * lead[...]
    act = joined(act_in)
    map_c = act[:, inner + size :]
    carried = grown * dot_nn(map_c, entering[...].astype(bf16))
    mixed = joined(y) + carried + skip[...] * act[:, :inner].astype(f32)
    gate = joined(z)
    gated = mixed * (gate * jax.nn.sigmoid(gate))
    mixed_ref[...] = mixed.astype(bf16).reshape(mixed_ref.shape)
    low = (gated * gain[...]).astype(bf16)
    low_ref[...] = low.reshape(low_ref.shape)
    squares = jnp.sum(gated * gated, axis=1, keepdims=True)
    squares_ref[...] = jnp.broadcast_to(squares, (BLOCK, squares_ref.shape[2])).reshape(squares_ref.shape)
    out_ref[...] = dot_nn(low, w_out[...]).astype(bf16).reshape(out_ref.shape)


def gate_back_kernel(push, w_out, mixed_in, z, act_in, decay, lead, slope_in, gain, dy_ref, dz_ref, enter_ref, sums_ref):
    heads = decay.shape[1]
    inner = mixed_in.shape[2]
    size = enter_ref.shape[0]
    mixed = joined(mixed_in).astype(f32)
    act = joined(act_in)
    gate = joined(z)
    sigma = jax.nn.sigmoid(gate)
    silu = gate * sigma
    gated = mixed * silu
    low_grad = dot_nt(joined(push), w_out[...])
    gated_grad = low_grad * gain[...] + 2.0 * gated * joined(slope_in)
    dy = gated_grad * silu
    dy_ref[...] = dy.astype(bf16).reshape(dy_ref.shape)
    dz_ref[...] = (gated_grad * mixed * (sigma + silu * (1.0 - sigma))).astype(bf16).reshape(dz_ref.shape)
    grown = per_channel(jnp.exp(sum_down(decay[...])), inner // heads) * lead[...]
    part = dot_tn(act[:, inner + size :], (grown * dy).astype(bf16))
    gain_sum = jnp.sum(low_grad * gated, axis=0, keepdims=True)
    skip_sum = jnp.sum(dy * act[:, :inner].astype(f32), axis=0, keepdims=True)

    @pl.when(pl.program_id(1) == 0)
    def _():
        enter_ref[...] = jnp.zeros_like(enter_ref)

    @pl.when((pl.program_id(0) == 0) & (pl.program_id(1) == 0))
    def _():
        sums_ref[...] = jnp.zeros_like(sums_ref)

    enter_ref[...] += part
    sums_ref[0:1, :] += gain_sum
    sums_ref[1:2, :] += skip_sum


def scan_back_kernel(cin, cin_before, edge, taps, raw, bias, decay, decay_t, act_in, dy_in, start, lead, entering, leave_grad, skip,
                     in_ref, head_ref, tail_ref, taps_ref, buf, nextp, state_grad):
    heads = decay.shape[1]
    block = BLOCK
    inner = dy_in.shape[2]
    width = taps.shape[1]
    size = state_grad.shape[0]
    head_size = inner // heads
    pair = 2 * head_size
    count = 4
    turn, turns = pl.program_id(1), pl.num_programs(1)

    @pl.when(turn == 0)
    def _():
        state_grad[...] = leave_grad[...]
        nextp[...] = jnp.zeros_like(nextp)

    @pl.when((pl.program_id(0) == 0) & (turn == 0))
    def _():
        taps_ref[...] = jnp.zeros_like(taps_ref)

    buf[8 : 8 + block, :] = joined(cin).astype(f32)

    @pl.when(turn == turns - 1)
    def _():
        buf[0:8, :] = edge[...]

    @pl.when(turn < turns - 1)
    def _():
        buf[0:8, :] = cin_before[...].astype(f32)[8:, :]

    pre = taps[4:5, :] + sum(taps[k : k + 1, :] * buf[5 + k : 5 + k + block, :] for k in range(count))
    sigma = jax.nn.sigmoid(pre)
    slope = sigma * (1.0 + pre * (1.0 - sigma))
    act = joined(act_in)
    map_b, map_c = act[:, inner : inner + size], act[:, inner + size :]
    value = act[:, :inner].astype(f32)
    raw_full = joined(raw) + bias[...]
    step = per_channel(softplus(raw_full), head_size)
    scaled = value * step
    low = scaled.astype(bf16)
    dy_low = joined(dy_in)
    dy = dy_low.astype(f32)
    within, across = sum_down(decay[...]), sum_right(decay_t[...])
    grown = per_channel(jnp.exp(within), head_size)
    tail = per_channel(jnp.exp(within[block - 1 :, :] - within), head_size)
    before = (start[...] + lead[...] * entering[...]).astype(bf16)
    after_grad = state_grad[...]
    after_low = after_grad.astype(bf16)
    grown_dy = (grown * dy).astype(bf16)
    c_grad = dot_nt(grown_dy, before)
    b_grad = dot_nt((tail * scaled).astype(bf16), after_low)
    scaled_grad = tail * dot_nn(map_b, after_low)
    state_grad[...] = grown[block - 1 :, :] * after_grad + dot_tn(map_c, grown_dy)
    scores_t = dot_nt(map_b, map_c)
    causal_t = lower_mask(block, True)
    left = first_half(block, pair)
    zero = jnp.zeros((block, pair), bf16)
    scores_grad_t = jnp.zeros((block, block), f32)
    parts = []
    for h in range(0, heads, 2):
        columns = slice(h * head_size, h * head_size + pair)
        dy_pair, low_pair = dy_low[:, columns], low[:, columns]
        halves = []
        for a in (h, h + 1):
            gap = jnp.where(causal_t, across[a : a + 1, :] - within[:, a : a + 1], -1e30)
            fade = jnp.exp(gap)
            own = jnp.where(left, low_pair, zero) if a == h else jnp.where(left, zero, low_pair)
            scores_grad_t = scores_grad_t + fade * dot_nt(own, dy_pair)
            halves.append(dot_nn((fade * scores_t).astype(bf16), dy_pair))
        parts.append(jnp.where(left, halves[0], halves[1]))
    scaled_grad = scaled_grad + jnp.concatenate(parts, axis=1)
    scores_low = scores_grad_t.astype(bf16)
    b_grad = b_grad + dot_nn(scores_low, map_c)
    c_grad = c_grad + dot_tn(scores_low, map_b)
    x_grad = scaled_grad * step + skip[...] * dy
    lanes = in_ref.shape[2] - width
    rows = lax.broadcasted_iota(jnp.int32, (inner, lanes), 0)
    columns = lax.broadcasted_iota(jnp.int32, (inner, lanes), 1)
    member = ((rows >= columns * head_size) & (rows < (columns + 1) * head_size)).astype(bf16)
    step_grad = dot_nn((scaled_grad * value).astype(bf16), member)
    raw_grad = step_grad[:, :heads] * jax.nn.sigmoid(raw_full)
    taps_ref[5:6, :heads] += jnp.sum(raw_grad, axis=0, keepdims=True)
    raw_grad = jnp.concatenate([raw_grad, jnp.zeros((block, lanes - heads), f32)], axis=1)
    in_ref[:, :, width:] = raw_grad.astype(bf16).reshape(in_ref.shape[:2] + (lanes,))
    pre_grad = jnp.concatenate([x_grad, b_grad, c_grad], axis=1) * slope
    for k in range(count):
        taps_ref[k : k + 1, :] += jnp.sum(pre_grad * buf[5 + k : 5 + k + block, :], axis=0, keepdims=True)
    taps_ref[4:5, :] += jnp.sum(pre_grad, axis=0, keepdims=True)
    buf[0:block, :] = pre_grad
    buf[block : block + 8, :] = nextp[...]
    nextp[...] = buf[0:8, :]
    head_ref[...] = buf[0:8, :]
    in_grad = sum(taps[k : k + 1, :] * buf[3 - k : 3 - k + block, :] for k in range(count))
    in_ref[:, :, :width] = in_grad.astype(bf16).reshape(in_ref.shape[:2] + (width,))

    @pl.when(turn == 0)
    def _():
        tail_ref[...] = in_grad[block - 8 :, :]


def params():
    return pltpu.CompilerParams(vmem_limit_bytes=56 * 2**20)


def cost(flops, moved, powers):
    return pl.CostEstimate(flops=int(flops), bytes_accessed=int(moved), transcendentals=int(powers))


def rows_of(share, width, flip=0):
    per = BLOCK // share
    if flip:
        return pl.BlockSpec((per, None, share, width), lambda b, k: (flip - 1 - k, b, 0, 0))
    return pl.BlockSpec((per, None, share, width), lambda b, k: (k, b, 0, 0))


def each(height, width):
    return pl.BlockSpec((None, height, width), lambda b, k: (b, 0, 0))


def only(height, width):
    return pl.BlockSpec((height, width), lambda b, k: (0, 0))


def at_block(height, width, flip=0):
    if flip:
        return pl.BlockSpec((None, None, height, width), lambda b, k: (b, flip - 1 - k, 0, 0))
    return pl.BlockSpec((None, None, height, width), lambda b, k: (b, k, 0, 0))


def in_order(width, flip=0):
    if flip:
        return pl.BlockSpec((None, BLOCK, width), lambda b, k: (b, flip - 1 - k, 0))
    return pl.BlockSpec((None, BLOCK, width), lambda b, k: (b, k, 0))


def made(*shape, kind=bf16):
    return jax.ShapeDtypeStruct(shape, kind)


def scan_forward(cin, edge, taps, raw, bias, decay, decay_t, inner, size):
    shares, batch, share, width = cin.shape
    heads = raw.shape[3]
    tokens = shares * share
    blocks = tokens // BLOCK
    return pl.pallas_call(
        scan_kernel,
        grid=(batch, blocks),
        in_specs=[
            rows_of(share, width),
            each(8, width),
            only(8, width),
            rows_of(share, heads),
            only(1, heads),
            in_order(heads),
            pl.BlockSpec((None, heads, BLOCK), lambda b, k: (b, 0, k)),
        ],
        out_specs=[rows_of(share, width), rows_of(share, inner), at_block(size, inner), each(size, inner)],
        out_shape=[
            made(shares, batch, share, width),
            made(shares, batch, share, inner, kind=f32),
            made(batch, blocks, size, inner, kind=f32),
            made(batch, size, inner, kind=f32),
        ],
        scratch_shapes=[
            pltpu.VMEM((BLOCK + 8, width), f32),
            pltpu.VMEM((8, width), f32),
            pltpu.VMEM((size, inner), f32),
        ],
        compiler_params=params(),
        cost_estimate=cost(
            batch * tokens * inner * (4 * BLOCK + 4 * size), 10 * batch * tokens * inner, batch * tokens * heads * BLOCK
        ),
    )(cin, edge, taps, raw, bias, decay, decay_t)


def gate_forward(y, act, z, decay, lead, entering, skip, gain, w_out):
    shares, batch, share, inner = y.shape
    width, heads, size = act.shape[3], decay.shape[2], entering.shape[1]
    model = w_out.shape[1]
    tokens = shares * share
    return pl.pallas_call(
        gate_kernel,
        grid=(batch, tokens // BLOCK),
        in_specs=[
            rows_of(share, inner),
            rows_of(share, width),
            rows_of(share, inner),
            in_order(heads),
            at_block(1, inner),
            each(size, inner),
            only(1, inner),
            only(1, inner),
            only(inner, model),
        ],
        out_specs=[rows_of(share, inner), rows_of(share, inner), rows_of(share, 128), rows_of(share, model)],
        out_shape=[
            made(shares, batch, share, inner),
            made(shares, batch, share, inner),
            made(shares, batch, share, 128, kind=f32),
            made(shares, batch, share, model),
        ],
        compiler_params=params(),
        cost_estimate=cost(
            2 * batch * tokens * inner * (model + size), batch * tokens * inner * 18, batch * tokens * inner
        ),
    )(y, act, z, decay, lead, entering, skip, gain, w_out)


def gate_backward(push, w_out, mixed, z, act, decay, lead, slope, gain):
    shares, batch, share, inner = mixed.shape
    width, heads, model = act.shape[3], decay.shape[2], w_out.shape[1]
    size = (width - inner) // 2
    tokens = shares * share
    return pl.pallas_call(
        gate_back_kernel,
        grid=(batch, tokens // BLOCK),
        in_specs=[
            rows_of(share, model),
            only(inner, model),
            rows_of(share, inner),
            rows_of(share, inner),
            rows_of(share, width),
            in_order(heads),
            at_block(1, inner),
            rows_of(share, 1),
            only(1, inner),
        ],
        out_specs=[rows_of(share, inner), rows_of(share, inner), each(size, inner), only(8, inner)],
        out_shape=[
            made(shares, batch, share, inner),
            made(shares, batch, share, inner),
            made(batch, size, inner, kind=f32),
            made(8, inner, kind=f32),
        ],
        compiler_params=params(),
        cost_estimate=cost(
            2 * batch * tokens * inner * (model + size), batch * tokens * inner * 18, batch * tokens * inner
        ),
    )(push, w_out, mixed, z, act, decay, lead, slope, gain)


def scan_backward(cin, edge, taps, raw, bias, decay, decay_t, act, dy, start, lead, entering, leave_grad, skip):
    shares, batch, share, width = cin.shape
    heads, inner, size = raw.shape[3], dy.shape[3], entering.shape[1]
    tokens = shares * share
    blocks = tokens // BLOCK
    per = BLOCK // share
    return pl.pallas_call(
        scan_back_kernel,
        grid=(batch, blocks),
        in_specs=[
            rows_of(share, width, blocks),
            pl.BlockSpec(
                (None, None, 16, width),
                lambda b, k: (jnp.maximum((blocks - 1 - k) * per - 1, 0), b, share // 16 - 1, 0),
            ),
            each(8, width),
            only(8, width),
            rows_of(share, heads, blocks),
            only(1, heads),
            in_order(heads, blocks),
            pl.BlockSpec((None, heads, BLOCK), lambda b, k: (b, 0, blocks - 1 - k)),
            rows_of(share, width, blocks),
            rows_of(share, inner, blocks),
            at_block(size, inner, blocks),
            at_block(1, inner, blocks),
            each(size, inner),
            each(size, inner),
            only(1, inner),
        ],
        out_specs=[rows_of(share, width + 128, blocks), each(8, width), each(8, width), only(8, width)],
        out_shape=[
            made(shares, batch, share, width + 128),
            made(batch, 8, width, kind=f32),
            made(batch, 8, width, kind=f32),
            made(8, width, kind=f32),
        ],
        scratch_shapes=[
            pltpu.VMEM((BLOCK + 8, width), f32),
            pltpu.VMEM((8, width), f32),
            pltpu.VMEM((size, inner), f32),
        ],
        compiler_params=params(),
        cost_estimate=cost(
            batch * tokens * inner * (8 * BLOCK + 10 * size), 15 * batch * tokens * inner, batch * tokens * heads * BLOCK
        ),
    )(cin, cin, edge, taps, raw, bias, decay, decay_t, act, dy, start, lead, entering, leave_grad, skip)


def weight_grads(groups, tile, extra=None):
    depth = groups[0][0][0].shape[1]
    rows = groups[0][0][0].shape[0]
    tiles = [group[0][1].shape[1] // tile for group in groups]
    starts = [sum(tiles[:g]) for g in range(len(groups) + 1)]
    terms = max(len(group) for group in groups)
    flat = [array for group in groups for term in group for array in term]
    count = len(flat)

    def kernel(*refs):
        out, turned = refs[-2], refs[-1]
        j = pl.program_id(0)
        place = 0
        for g, group in enumerate(groups):
            mine = refs[place : place + 2 * len(group)]
            place += 2 * len(group)

            @pl.when(j == starts[g])
            def _(mine=mine):
                for t in range(len(mine) // 2):
                    turned[t] = mine[2 * t][...].T

            @pl.when((j >= starts[g]) & (j < starts[g + 1]))
            def _(mine=mine):
                total = sum(dot_nn(turned[t], mine[2 * t + 1][...]) for t in range(len(mine) // 2))
                out[...] = total.astype(bf16)

        if extra is not None:

            @pl.when(j >= starts[-1])
            def _():
                out[...] = refs[count][...]

    specs = []
    for g, group in enumerate(groups):
        for _ in group:
            specs.append(pl.BlockSpec((rows, depth), lambda j: (0, 0), pipeline_mode=pl.Buffered(1)))
            specs.append(
                pl.BlockSpec((rows, tile), lambda j, a=starts[g], n=tiles[g]: (0, jnp.clip(j - a, 0, n - 1)))
            )
    steps = starts[-1]
    if extra is not None:
        flat = flat + [extra]
        specs.append(pl.BlockSpec((depth, tile), lambda j, a=steps: (0, jnp.maximum(j - a, 0))))
        steps += extra.shape[1] // tile
    return pl.pallas_call(
        kernel,
        grid=(steps,),
        in_specs=specs,
        out_specs=pl.BlockSpec((depth, tile), lambda j: (0, j)),
        out_shape=jax.ShapeDtypeStruct((depth, steps * tile), bf16),
        scratch_shapes=[pltpu.VMEM((terms, depth, rows), bf16)],
        compiler_params=params(),
        cost_estimate=cost(2 * terms * rows * depth * tile * steps, 2 * (count * rows * depth + depth * tile * steps), 0),
    )(*flat)


def expert_kernel(shared, x_ref, grad_ref, gates_ref, mine, w_gu, w_down, *refs):
    if shared:
        ws_gu, ws_down, out_ref, dx_ref, logit_ref, act_ref, gu_ref, s_act_ref, s_gu_ref = refs
    else:
        out_ref, dx_ref, logit_ref, act_ref, gu_ref = refs
    x, grad, gates = x_ref[...], grad_ref[...], gates_ref[...]
    wide = grad.astype(f32)

    def back(gate, up, act_push):
        sigma = jax.nn.sigmoid(gate)
        silu = gate * sigma
        slope = sigma + silu * (1.0 - sigma)
        return silu, jnp.concatenate([act_push * up * slope, act_push * silu], axis=1).astype(bf16)

    out = dx = 0.0
    width = w_down.shape[1]
    own = total = 0.0
    for e in range(w_gu.shape[0]):
        weight = jnp.sum(gates * mine[e : e + 1, :], axis=1, keepdims=True)
        both = dot_nn(x, w_gu[e])
        gate, up = both[:, :width], both[:, width:]
        act_push = dot_nt((weight * wide).astype(bf16), w_down[e])
        silu, gu_grad = back(gate, up, act_push)
        act = (silu * up).astype(bf16)
        act_ref[:, e * width : (e + 1) * width] = (weight * act.astype(f32)).astype(bf16)
        gu_ref[:, 2 * e * width : 2 * (e + 1) * width] = gu_grad
        result = dot_nn(act, w_down[e]).astype(bf16).astype(f32)
        push = jnp.sum(wide * result, axis=1, keepdims=True)
        own = own + push * mine[e : e + 1, :]
        total = total + weight * push
        out = out + weight * result
        dx = dx + dot_nt(gu_grad, w_gu[e]).astype(bf16).astype(f32)
    if shared:
        width = ws_down.shape[0]
        gate, up = dot_nn(x, ws_gu[0]), dot_nn(x, ws_gu[1])
        silu, gu_grad = back(gate, up, dot_nt(grad, ws_down[...]))
        act = (silu * up).astype(bf16)
        s_act_ref[...] = act
        s_gu_ref[...] = gu_grad
        out = out + dot_nn(act, ws_down[...])
        dx = dx + dot_nt(gu_grad[:, :width], ws_gu[0]) + dot_nt(gu_grad[:, width:], ws_gu[1])
    out_ref[...] = out.astype(bf16)
    dx_ref[...] = dx.astype(bf16)
    logit_ref[...] = gates * (own - total)


def experts(x, grad, gates, mine, w_gu, w_down, shared=()):
    rows, model = x.shape
    count, _, double = w_gu.shape
    width = double // 2
    every = gates.shape[1]

    def row(columns):
        return pl.BlockSpec((ROWS, columns), lambda i: (i, 0))

    def whole(array):
        zeros = (0,) * array.ndim
        return pl.BlockSpec(array.shape, lambda i: zeros, pipeline_mode=pl.Buffered(1))

    widths = [model, model, every, count * width, count * double]
    hidden = count * width
    if shared:
        ff = shared[1].shape[0]
        hidden += ff
        widths += [ff, 2 * ff]
    return pl.pallas_call(
        lambda *refs: expert_kernel(bool(shared), *refs),
        grid=(rows // ROWS,),
        in_specs=[row(model), row(model), row(every), whole(mine), whole(w_gu), whole(w_down)]
        + [whole(w) for w in shared],
        out_specs=[row(w) for w in widths],
        out_shape=[made(rows, w, kind=f32 if i == 2 else bf16) for i, w in enumerate(widths)],
        compiler_params=params(),
        cost_estimate=cost(
            rows * hidden * model * 12, 6 * hidden * model + rows * (8 * model + 6 * hidden), rows * hidden
        ),
    )(x, grad, gates, mine, w_gu, w_down, *shared)


def shifted(array, axis, by):
    count = lax.axis_size(axis)
    pairs = [(i, i + by) for i in range(count) if 0 <= i + by < count]
    return lax.ppermute(array, axis, pairs)


def prefix(part, axis, combine, identity):
    place = lax.axis_index(axis)
    gathered = jax.tree.map(lambda a: lax.all_gather(a, axis), part)
    state = jax.tree.map(lambda a, e: jnp.zeros_like(a) + jnp.asarray(e, a.dtype), part, identity)

    def one(lap, state):
        return combine(
            state, jax.tree.map(lambda a: lax.dynamic_index_in_dim(a, lap, 0, False), gathered)
        )

    return lax.fori_loop(0, place, one, state)


def prefix_2(array, axis, combine, identity):
    count, place = (lax.axis_size(axis), lax.axis_index(axis))
    everything = jax.tree.map(
        lambda part, kind: lax.all_gather(part.astype(kind), axis),
        array,
        jax.tree.map(lambda a: jnp.bfloat16 if a.dtype == jnp.float32 else a.dtype, array),
    )
    start = jax.tree.map(
        lambda part, zero: jnp.broadcast_to(jnp.asarray(zero, part.dtype), part.shape),
        array,
        identity,
    )

    def lap(k, before):
        at = count - 1 - k
        reached = at > place
        new = combine(
            before, jax.tree.map(lambda part, own: part[at].astype(own.dtype), everything, array)
        )
        return jax.tree.map(lambda a, b: jnp.where(reached, a, b), new, before)

    return lax.fori_loop(0, count, lap, start)


def sum_shares(part):
    got = lax.all_to_all(part, "head", split_axis=0, concat_axis=0, tiled=True)
    return jnp.sum(got.astype(f32), axis=0)


def gather_shares(share):
    copies = jnp.broadcast_to(share[None], (lax.axis_size("head"),) + share.shape)
    return lax.all_to_all(copies, "head", split_axis=0, concat_axis=0, tiled=True)


def relay(parts):
    count, place = lax.axis_size("head"), lax.axis_index("head")

    def passed(array, by):
        return lax.ppermute(
            array, "head", [(i, i + by) for i in range(count) if 0 <= i + by < count]
        )

    up, down = [[p] for p in parts], [[p] for p in parts]
    for _ in range(count - 1):
        for k in range(len(parts)):
            up[k].append(passed(up[k][-1], 1))
            down[k].append(passed(down[k][-1], -1))
    return [
        [p] + [jnp.where(place >= d, up[k][d], down[k][count - d]) for d in range(1, count)]
        for k, p in enumerate(parts)
    ]


def laid(pieces, lists, shares_first=True):
    count, place = lax.axis_size("head"), lax.axis_index("head")
    batch_size = len(lists)
    lead = (count, batch_size) if shares_first else (batch_size, count)
    out = jnp.zeros(lead + pieces.shape[1:], pieces.dtype)
    for b, row in enumerate(lists):
        for d, piece in enumerate(row):
            slot = (place + count - d) % count
            at = (slot, b) if shares_first else (b, slot)
            out = lax.dynamic_update_slice(out, piece[None, None], at + (0,) * piece.ndim)
    return out


def relay_shares(share, *extras, shares_first=True):
    batch_size = share.shape[0]
    lists = relay([share[b] for b in range(batch_size)] + list(extras))
    whole = laid(share, lists[:batch_size], shares_first)
    others = []
    for row in lists[batch_size:]:
        out = jnp.zeros((len(row),) + row[0].shape, row[0].dtype)
        for d, piece in enumerate(row):
            slot = (lax.axis_index("head") + len(row) - d) % len(row)
            out = lax.dynamic_update_index_in_dim(out, piece, slot, 0)
        others.append(out)
    return (whole, *others) if extras else whole


def bits_of(axis):
    count = lax.axis_size(axis)
    return [(1 << k) for k in range(count.bit_length() - 1)]


def across(array, axis, bit):
    return lax.ppermute(array, axis, [(i, i ^ bit) for i in range(lax.axis_size(axis))])


def add_over(array, *axes):
    for axis in axes:
        for bit in bits_of(axis):
            array = array + across(array, axis, bit)
    return array


def join_over(array, dimension, *axes):
    for axis in axes:
        place = lax.axis_index(axis)
        for bit in bits_of(axis):
            other = across(array, axis, bit)
            array = jnp.where(
                (place & bit) == 0,
                jnp.concatenate([array, other], axis=dimension),
                jnp.concatenate([other, array], axis=dimension),
            )
    return array


def tie(*arrays):
    return lax.optimization_barrier(arrays)


def around(array, by):
    count = lax.axis_size("seq")
    if by % count == 0:
        return array
    return lax.ppermute(array, "seq", [(i, (i + by) % count) for i in range(count)])


def spread_last(local_part, rank_index, part_count):
    local_width = local_part.shape[-1]
    full_array = jnp.zeros(local_part.shape[:-1] + (local_width * part_count,), jnp.float32)
    return lax.dynamic_update_slice_in_dim(
        full_array, local_part, rank_index * local_width, local_part.ndim - 1
    )


def chain_forward(earlier, later):
    return (earlier[0] * later[0], later[0] * earlier[1] + later[1])


def chain_backward(earlier, later):
    return (earlier[0] * later[0], later[1] + later[0] * earlier[1])


def local(
    x_in,
    d_out,
    log_decay,
    routes,
    norm1_gain,
    w_in_zx,
    w_in_bc,
    w_in_dt,
    dt_bias,
    conv_x,
    conv_x_bias,
    conv_bc,
    conv_bc_bias,
    skip_d,
    gate_norm_gain,
    w_out,
    norm2_gain,
    router,
    w_expert_gu,
    w_expert_down,
    w_shared_gu,
    w_shared_down,
):
    batch_size, tokens, model_width = x_in.shape
    inner_dev = w_in_zx.shape[2]
    heads_dev = w_in_dt.shape[1]
    head_size = inner_dev // heads_dev
    state_size = w_in_bc.shape[1] // 2
    conv_taps = conv_x.shape[0]
    experts_dev = w_expert_gu.shape[0]
    head_count = lax.axis_size("head")
    seq_count = lax.axis_size("seq")
    head_rank = lax.axis_index("head")
    seq_rank = lax.axis_index("seq")
    inner_all = inner_dev * head_count
    experts_all = experts_dev * seq_count * head_count
    share_rows = tokens // head_count
    rows_all = batch_size * tokens
    conv_width = inner_dev + 2 * state_size
    edge = conv_taps - 1

    def by_share(array):
        array = array.reshape((batch_size, head_count, share_rows) + array.shape[2:])
        return jnp.swapaxes(array, 0, 1)

    def by_position(array):
        return jnp.swapaxes(array, 0, 1).reshape(batch_size, tokens, array.shape[-1])

    def own_share(array):
        return lax.dynamic_index_in_dim(array, head_rank, 0, keepdims=False)

    def flat(array):
        return array.reshape(-1, array.shape[-1])

    def times(a, b):
        return lax.dot_general(a, b, (((a.ndim - 1,), (0,)), ((), ())), preferred_element_type=f32)

    def times_t(a, b):
        return lax.dot_general(a, b, (((a.ndim - 1,), (1,)), ((), ())), preferred_element_type=f32)

    def scattered(array, axes):
        return lax.psum_scatter(array, axes, scatter_dimension=0, tiled=True)

    x_rows, grad_rows = by_share(x_in), by_share(d_out)
    grads_in = [flat(around(grad_rows, k)) for k in range(seq_count)]
    input_wide = x_rows.astype(f32)
    scale_one = lax.rsqrt(jnp.mean(input_wide * input_wide, axis=-1, keepdims=True) + norm_eps)
    normed_one = (input_wide * scale_one * norm1_gain).astype(bf16)
    w_conv = jnp.concatenate([w_in_zx[1], w_in_bc], axis=-1)
    w_step = jnp.pad(w_in_dt, ((0, 0), (0, 128 - heads_dev)))
    w_late = jnp.concatenate([w_conv, w_step], axis=-1)
    conv_in = times(normed_one, w_conv).astype(bf16)
    step_raw = times(normed_one, w_step)[..., :heads_dev]
    gate_z = times(normed_one, w_in_zx[0])
    edge_rows = shifted(conv_in[head_count - 1, :, share_rows - edge :], "seq", 1).astype(f32)
    edge_rows = jnp.pad(edge_rows, ((0, 0), (8 - edge, 0), (0, 0)))
    taps = jnp.concatenate([conv_x, conv_bc], axis=1)
    bias = jnp.concatenate([conv_x_bias, conv_bc_bias])
    taps_bias = jnp.concatenate([taps, bias[None], jnp.zeros((7 - conv_taps, conv_width), f32)])
    decay_across = jnp.transpose(log_decay, (0, 2, 1))
    step_bias = dt_bias[None]
    totals = jnp.sum(log_decay.reshape(batch_size, -1, BLOCK, heads_dev), axis=2)
    before = [jnp.zeros_like(totals[:, 0])]
    for k in range(totals.shape[1]):
        before.append(before[-1] + totals[:, k])
    lead = jnp.repeat(jnp.exp(jnp.stack(before, axis=1)), head_size, axis=-1)
    device_decay, lead = lead[:, -1:], lead[:, :-1, None]
    skip = jnp.repeat(skip_d, head_size)[None]
    gate_gain = gate_norm_gain[None]

    conv_act, scanned, starts, leaving = scan_forward(
        conv_in, edge_rows, taps_bias, step_raw, step_bias, log_decay, decay_across, inner_dev, state_size
    )
    identity = (jnp.ones_like(device_decay), jnp.zeros_like(leaving))
    if seq_count == 2:
        entering = shifted(leaving, "seq", 1)
    else:
        _, entering = prefix((device_decay, leaving), "seq", chain_forward, identity)
    mixed, gated_low, squares, partial_out = gate_forward(
        scanned, conv_act, gate_z, log_decay, lead, entering, skip, gate_gain, w_out
    )

    mix_out = sum_shares(partial_out)
    squares = own_share(add_over(squares[..., 0], "head"))
    gate_scale = lax.rsqrt(squares / inner_all + norm_eps)[..., None]
    hidden = own_share(x_rows).astype(f32) + mix_out * gate_scale
    scale_two = lax.rsqrt(jnp.mean(hidden * hidden, axis=-1, keepdims=True) + norm_eps)
    normed_share = (hidden * scale_two * norm2_gain).astype(bf16)

    expert_ids = jnp.arange(experts_all, dtype=jnp.int32)
    used = jnp.any(own_share(by_share(routes))[..., None] == expert_ids, axis=2)
    logits = times(normed_share, router)
    top = jnp.max(jnp.where(used, logits, -jnp.inf), axis=-1, keepdims=True)
    powers = jnp.where(used, jnp.exp(jnp.where(used, logits - top, 0.0)), 0.0)
    gates = powers / jnp.sum(powers, axis=-1, keepdims=True)
    normed_two, gates = relay_shares(normed_share, flat(gates).T)

    first = (seq_rank * head_count + head_rank) * experts_dev
    mine = (jnp.arange(8)[:, None] + first == expert_ids) & (jnp.arange(8)[:, None] < experts_dev)
    mine = mine.astype(f32)
    ffn_out, ffn_dx, logit_grad = [], [], []
    up_terms, down_terms = [], []
    for k in [*range(1, seq_count), 0]:
        rows = flat(around(normed_two, k))
        weights = flat(jnp.swapaxes(around(gates, k), 1, 2))
        shared = (w_shared_gu, w_shared_down) if k == 0 else ()
        pieces = experts(rows, grads_in[k], weights, mine, w_expert_gu, w_expert_down, shared)
        ffn_out.append(around(pieces[0], -k))
        ffn_dx.append(around(pieces[1], -k))
        logit_grad.append(around(pieces[2], -k))
        down_terms.append((grads_in[k], pieces[3]))
        up_terms.append((rows, pieces[4]))
    shared_terms = [[(rows, pieces[6])], [(grads_in[0], pieces[5])]]
    expert_grads = [
        weight_grads([up_terms[k : k + 2], down_terms[k : k + 2]], 512) for k in range(0, seq_count, 2)
    ]
    if len(expert_grads) > 1:
        expert_grads = [sum(g.astype(f32) for g in expert_grads).astype(bf16)]
    logit_grad = sum(logit_grad).astype(bf16)
    ffn_dx = sum(d.astype(f32) for d in ffn_dx) + times_t(logit_grad, router)
    ffn_dx = ffn_dx.astype(bf16).reshape(normed_two.shape)
    expert_sum = scattered(expert_grads[0], "dp")
    dx_share, _, logit_grad = tie(sum_shares(ffn_dx), expert_grads[0], logit_grad)
    grad_router = lax.dot_general(
        logit_grad, flat(normed_two), (((0,), (0,)), ((), ())), preferred_element_type=f32
    )
    gained_two = dx_share * norm2_gain
    hidden_grad = own_share(grad_rows).astype(f32) + scale_two * (
        gained_two
        - hidden * scale_two * scale_two * jnp.mean(gained_two * hidden, axis=-1, keepdims=True)
    )
    grad_norm_two = jnp.sum(dx_share * hidden * scale_two, axis=(0, 1))
    scale_push = jnp.sum(hidden_grad * mix_out, axis=-1)
    squares_grad = -0.5 * scale_push * gate_scale[..., 0] ** 3 / inner_all
    out_push, squares_grad = relay_shares((hidden_grad * gate_scale).astype(bf16), squares_grad)
    out_push, expert_sum = tie(out_push, expert_sum)
    ffn_low = sum(f.astype(f32) for f in ffn_out).astype(bf16).reshape(normed_two.shape)
    ffn_low, out_push = tie(ffn_low, out_push)
    ffn_share = sum_shares(ffn_low)

    mixed_grad, z_grad, entering_grad, channel_sums = gate_backward(
        out_push, w_out, mixed, gate_z, conv_act, log_decay, lead, squares_grad[..., None], gate_gain
    )
    if seq_count == 2:
        leaving_grad = shifted(entering_grad.astype(bf16), "seq", -1).astype(f32)
    else:
        _, leaving_grad = prefix_2((device_decay, entering_grad), "seq", chain_backward, identity)
    in_grad, first_rows, last_rows, tap_sums = scan_backward(
        conv_in,
        edge_rows,
        taps_bias,
        step_raw,
        step_bias,
        log_decay,
        decay_across,
        conv_act,
        mixed_grad,
        starts,
        lead,
        entering,
        leaving_grad,
        skip,
    )
    early_dx = times_t(z_grad, w_in_zx[0])
    in_grad, ffn_share = tie(in_grad, ffn_share)
    next_rows = shifted(first_rows[:, :edge], "seq", -1)
    late = [
        sum(taps[edge - k] * next_rows[:, k + i - edge] for k in range(conv_taps) if k + i >= edge)
        for i in range(edge)
    ]
    late = last_rows.at[:, 8 - edge :].add(jnp.stack(late, axis=1)).astype(bf16)
    in_grad = in_grad.at[head_count - 1, :, share_rows - 8 :, :conv_width].set(late)
    normed_one_grad = early_dx + times_t(in_grad, w_late)
    grad_norm_one = jnp.sum(normed_one_grad * input_wide * scale_one, axis=(0, 1, 2))
    normed_one_grad = normed_one_grad.astype(bf16)
    dn_share = sum_shares(normed_one_grad)

    def whole(array):
        return spread_last(array, head_rank, head_count).reshape(-1)

    small = [
        grad_norm_two,
        grad_router.reshape(-1),
        whole(tap_sums[:conv_taps, :inner_dev]),
        whole(tap_sums[conv_taps, :inner_dev]),
        whole(channel_sums[0]),
        grad_norm_one,
        tap_sums[:conv_taps, inner_dev:].reshape(-1),
        tap_sums[conv_taps, inner_dev:],
        whole(tap_sums[conv_taps + 1, :heads_dev]),
        whole(jnp.sum(channel_sums[1].reshape(heads_dev, head_size), axis=-1)),
    ]
    sizes = [a.shape[0] for a in small]
    small = jnp.concatenate(small + [jnp.zeros((128 * model_width - sum(sizes),), f32)])
    small = small.reshape(128, model_width).T.astype(bf16)
    grad_late = weight_grads([[(flat(normed_one), flat(in_grad))]], 128, small)
    early_terms = [[(flat(out_push), flat(gated_low))], [(flat(normed_one), flat(z_grad))]]
    grad_early = weight_grads(early_terms + shared_terms, 256)
    late_sum = scattered(grad_late, ("dp", "seq")).astype(f32)
    merged = jnp.concatenate([late_sum[:, inner_dev:conv_width], late_sum[:, conv_width + 128 :]], axis=1)
    merged = add_over(merged, "head")
    merged = join_over(merged, 0, "seq", "dp")
    early_sum = scattered(grad_early, ("dp", "seq"))

    layer_share, dn_share, early_sum = tie((hidden + ffn_share).astype(bf16), dn_share, early_sum)
    early_sum = early_sum.astype(f32)
    layer_out = by_position(gather_shares(layer_share))
    gained_one = dn_share * norm1_gain
    input_share, scale_share = own_share(input_wide), own_share(scale_one)
    input_grad = hidden_grad + scale_share * (
        gained_one
        - input_share
        * scale_share
        * scale_share
        * jnp.mean(gained_one * input_share, axis=-1, keepdims=True)
    )
    d_input = relay_shares(input_grad.astype(bf16), shares_first=False)
    d_input = d_input.reshape(batch_size, tokens, model_width)

    grad_bc = merged[:, : 2 * state_size]
    small = merged[:, 2 * state_size :].T.reshape(-1)
    ends = [sum(sizes[:k]) for k in range(len(sizes) + 1)]
    small = [small[ends[k] : ends[k + 1]] for k in range(len(sizes))]
    expert_sum = expert_sum.astype(f32)
    double = w_expert_gu.shape[2]
    grad_gu = [expert_sum[:, e * double : (e + 1) * double] for e in range(experts_dev)]
    expert_sum = expert_sum[:, experts_dev * double :]
    width = double // 2
    grad_down = [expert_sum[:, e * width : (e + 1) * width].T for e in range(experts_dev)]
    shared_sum = early_sum[:, 2 * inner_dev :]
    ff_dev = w_shared_down.shape[0]
    return (
        layer_out,
        d_input,
        small[5],
        jnp.stack([early_sum[:, inner_dev : 2 * inner_dev], late_sum[:, :inner_dev]]),
        grad_bc,
        late_sum[:, conv_width : conv_width + heads_dev],
        small[8],
        small[2].reshape(conv_taps, inner_all),
        small[3],
        small[6].reshape(conv_taps, 2 * state_size),
        small[7],
        small[9],
        small[4],
        early_sum[:, :inner_dev].T,
        small[0],
        small[1].reshape(experts_all, model_width).T,
        jnp.stack(grad_gu),
        jnp.stack(grad_down),
        jnp.stack([shared_sum[:, :ff_dev], shared_sum[:, ff_dev : 2 * ff_dev]]),
        shared_sum[:, 2 * ff_dev :].T,
    )


def solution(mesh):
    placed = (
        P("dp", "seq", None),
        P("dp", "seq", None),
        P("dp", "seq", "head"),
        P("dp", "seq", None),
        P(),
        P(None, None, "head"),
        P(),
        P(None, "head"),
        P("head"),
        P(None, "head"),
        P("head"),
        P(),
        P(),
        P("head"),
        P("head"),
        P("head", None),
        P(),
        P(),
        P(("seq", "head"), None, None),
        P(("seq", "head"), None, None),
        P(None, None, "head"),
        P("head", None),
    )
    return jax.shard_map(
        local,
        mesh=mesh,
        in_specs=placed,
        out_specs=(
            P("dp", "seq", None),
            P("dp", "seq", None),
            P(),
            P(None, ("dp", "seq"), "head"),
            P(),
            P(("dp", "seq"), "head"),
            P(),
            P(),
            P(),
            P(),
            P(),
            P(),
            P(),
            P("head", ("dp", "seq")),
            P(),
            P(),
            P(("seq", "head"), "dp", None),
            P(("seq", "head"), None, "dp"),
            P(None, ("dp", "seq"), "head"),
            P("head", ("dp", "seq")),
        ),
        check_vma=False,
    )
```

```python
import jax
import jax.numpy as jnp
from jax import lax
from jax.experimental import pallas as pl
from jax.experimental.pallas import tpu as pltpu
from jax.sharding import PartitionSpec as P

BLOCK = 256
ROWS = 256

bf16, f32 = jnp.bfloat16, jnp.float32
norm_eps = 1e-05
highest = lax.Precision.HIGHEST


def dot_nn(a, b):
    return lax.dot_general(a, b, (((1,), (0,)), ((), ())), preferred_element_type=f32)


def dot_nt(a, b):
    return lax.dot_general(a, b, (((1,), (1,)), ((), ())), preferred_element_type=f32)


def dot_tn(a, b):
    return lax.dot_general(a, b, (((0,), (0,)), ((), ())), preferred_element_type=f32)


def lower_mask(count, flip=False):
    rows = lax.broadcasted_iota(jnp.int32, (count, count), 0)
    columns = lax.broadcasted_iota(jnp.int32, (count, count), 1)
    return columns >= rows if flip else rows >= columns


def sum_down(values):
    lower = lower_mask(values.shape[0]).astype(f32)
    return jnp.dot(lower, values, precision=highest, preferred_element_type=f32)


def sum_right(values):
    upper = lower_mask(values.shape[1], True).astype(f32)
    return jnp.dot(values, upper, precision=highest, preferred_element_type=f32)


def first_half(rows, width=128):
    return lax.broadcasted_iota(jnp.int32, (rows, width), 1) < width // 2


def per_channel(values, head_size):
    rows, heads = values.shape
    left = first_half(rows, 2 * head_size)
    return jnp.concatenate(
        [jnp.where(left, values[:, h : h + 1], values[:, h + 1 : h + 2]) for h in range(0, heads, 2)],
        axis=1,
    )


def joined(ref):
    return ref[...].reshape(-1, ref.shape[-1])


def softplus(v):
    return jnp.maximum(v, 0.0) + jnp.log1p(jnp.exp(-jnp.abs(v)))


def scan_kernel(cin, edge, taps, raw, bias, decay, decay_t, act_ref, y_ref, start_ref, leave_ref, buf, prev, state):
    heads = decay.shape[1]
    block = BLOCK
    inner = y_ref.shape[2]
    size = state.shape[0]
    head_size = inner // heads
    pair = 2 * head_size
    count = 4

    @pl.when(pl.program_id(1) == 0)
    def _():
        prev[...] = edge[...]
        state[...] = jnp.zeros_like(state)

    buf[0:8, :] = prev[...]
    buf[8 : 8 + block, :] = joined(cin).astype(f32)
    pre = taps[4:5, :] + sum(taps[k : k + 1, :] * buf[5 + k : 5 + k + block, :] for k in range(count))
    prev[...] = buf[block : block + 8, :]
    act = (pre * jax.nn.sigmoid(pre)).astype(bf16)
    act_ref[...] = act.reshape(act_ref.shape)
    map_b, map_c = act[:, inner : inner + size], act[:, inner + size :]
    step = softplus(joined(raw) + bias[...])
    scaled = act[:, :inner].astype(f32) * per_channel(step, head_size)
    within, across = sum_down(decay[...]), sum_right(decay_t[...])
    grown = per_channel(jnp.exp(within), head_size)
    tail = per_channel(jnp.exp(within[block - 1 :, :] - within), head_size)
    before = state[...]
    start_ref[...] = before
    carried = grown * dot_nn(map_c, before.astype(bf16))
    scores = dot_nt(map_c, map_b)
    causal = lower_mask(block)
    low = scaled.astype(bf16)
    left = first_half(block, pair)
    for h in range(0, heads, 2):
        columns = slice(h * head_size, h * head_size + pair)
        halves = []
        for a in (h, h + 1):
            gap = jnp.where(causal, within[:, a : a + 1] - across[a : a + 1, :], -1e30)
            halves.append(dot_nn((jnp.exp(gap) * scores).astype(bf16), low[:, columns]))
        y_pair = carried[:, columns] + jnp.where(left, halves[0], halves[1])
        y_ref[:, :, columns] = y_pair.reshape(y_ref.shape[:2] + (pair,))
    after = grown[block - 1 :, :] * before + dot_tn(map_b, (scaled * tail).astype(bf16))
    state[...] = after
    leave_ref[...] = after


def gate_kernel(y, act_in, z, decay, lead, entering, skip, gain, w_out, mixed_ref, low_ref, squares_ref, out_ref):
    heads = decay.shape[1]
    inner = y.shape[2]
    size = entering.shape[0]
    grown = per_channel(jnp.exp(sum_down(decay[...])), inner // heads) * lead[...]
    act = joined(act_in)
    map_c = act[:, inner + size :]
    carried = grown * dot_nn(map_c, entering[...].astype(bf16))
    mixed = joined(y) + carried + skip[...] * act[:, :inner].astype(f32)
    gate = joined(z)
    gated = mixed * (gate * jax.nn.sigmoid(gate))
    mixed_ref[...] = mixed.astype(bf16).reshape(mixed_ref.shape)
    low = (gated * gain[...]).astype(bf16)
    low_ref[...] = low.reshape(low_ref.shape)
    squares = jnp.sum(gated * gated, axis=1, keepdims=True)
    squares_ref[...] = jnp.broadcast_to(squares, (BLOCK, squares_ref.shape[2])).reshape(squares_ref.shape)
    out_ref[...] = dot_nn(low, w_out[...]).astype(bf16).reshape(out_ref.shape)


def gate_back_kernel(push, w_out, mixed_in, z, act_in, decay, lead, slope_in, gain, dy_ref, dz_ref, enter_ref, sums_ref):
    heads = decay.shape[1]
    inner = mixed_in.shape[2]
    size = enter_ref.shape[0]
    mixed = joined(mixed_in).astype(f32)
    act = joined(act_in)
    terms = joined(slope_in).astype(f32)
    slope = terms[:, 0:1] + terms[:, 1:2]
    gate = joined(z)
    sigma = jax.nn.sigmoid(gate)
    silu = gate * sigma
    gated = mixed * silu
    low_grad = dot_nt(joined(push), w_out[...])
    gated_grad = low_grad * gain[...] + 2.0 * gated * slope
    dy = gated_grad * silu
    dy_ref[...] = dy.astype(bf16).reshape(dy_ref.shape)
    dz_ref[...] = (gated_grad * mixed * (sigma + silu * (1.0 - sigma))).astype(bf16).reshape(dz_ref.shape)
    grown = per_channel(jnp.exp(sum_down(decay[...])), inner // heads) * lead[...]
    part = dot_tn(act[:, inner + size :], (grown * dy).astype(bf16))
    gain_sum = jnp.sum(low_grad * gated, axis=0, keepdims=True)
    skip_sum = jnp.sum(dy * act[:, :inner].astype(f32), axis=0, keepdims=True)

    @pl.when(pl.program_id(1) == 0)
    def _():
        enter_ref[...] = jnp.zeros_like(enter_ref)

    @pl.when((pl.program_id(0) == 0) & (pl.program_id(1) == 0))
    def _():
        sums_ref[...] = jnp.zeros_like(sums_ref)

    enter_ref[...] += part
    sums_ref[0:1, :] += gain_sum
    sums_ref[1:2, :] += skip_sum


def scan_back_kernel(cin, cin_before, edge, taps, raw, bias, decay, decay_t, act_in, dy_in, start, lead, entering, leave_grad, skip,
                     in_ref, head_ref, tail_ref, taps_ref, buf, nextp, state_grad):
    heads = decay.shape[1]
    block = BLOCK
    inner = dy_in.shape[2]
    width = taps.shape[1]
    size = state_grad.shape[0]
    head_size = inner // heads
    pair = 2 * head_size
    count = 4
    turn, turns = pl.program_id(1), pl.num_programs(1)

    @pl.when(turn == 0)
    def _():
        state_grad[...] = leave_grad[...]
        nextp[...] = jnp.zeros_like(nextp)

    @pl.when((pl.program_id(0) == 0) & (turn == 0))
    def _():
        taps_ref[...] = jnp.zeros_like(taps_ref)

    buf[8 : 8 + block, :] = joined(cin).astype(f32)

    @pl.when(turn == turns - 1)
    def _():
        buf[0:8, :] = edge[...]

    @pl.when(turn < turns - 1)
    def _():
        buf[0:8, :] = cin_before[...].astype(f32)[8:, :]

    pre = taps[4:5, :] + sum(taps[k : k + 1, :] * buf[5 + k : 5 + k + block, :] for k in range(count))
    sigma = jax.nn.sigmoid(pre)
    slope = sigma * (1.0 + pre * (1.0 - sigma))
    act = joined(act_in)
    map_b, map_c = act[:, inner : inner + size], act[:, inner + size :]
    value = act[:, :inner].astype(f32)
    raw_full = joined(raw) + bias[...]
    step = per_channel(softplus(raw_full), head_size)
    scaled = value * step
    low = scaled.astype(bf16)
    dy_low = joined(dy_in)
    dy = dy_low.astype(f32)
    within, across = sum_down(decay[...]), sum_right(decay_t[...])
    grown = per_channel(jnp.exp(within), head_size)
    tail = per_channel(jnp.exp(within[block - 1 :, :] - within), head_size)
    before = (start[...] + lead[...] * entering[...]).astype(bf16)
    after_grad = state_grad[...]
    after_low = after_grad.astype(bf16)
    grown_dy = (grown * dy).astype(bf16)
    c_grad = dot_nt(grown_dy, before)
    b_grad = dot_nt((tail * scaled).astype(bf16), after_low)
    scaled_grad = tail * dot_nn(map_b, after_low)
    state_grad[...] = grown[block - 1 :, :] * after_grad + dot_tn(map_c, grown_dy)
    scores_t = dot_nt(map_b, map_c)
    causal_t = lower_mask(block, True)
    left = first_half(block, pair)
    zero = jnp.zeros((block, pair), bf16)
    scores_grad_t = jnp.zeros((block, block), f32)
    parts = []
    for h in range(0, heads, 2):
        columns = slice(h * head_size, h * head_size + pair)
        dy_pair, low_pair = dy_low[:, columns], low[:, columns]
        halves = []
        for a in (h, h + 1):
            gap = jnp.where(causal_t, across[a : a + 1, :] - within[:, a : a + 1], -1e30)
            fade = jnp.exp(gap)
            own = jnp.where(left, low_pair, zero) if a == h else jnp.where(left, zero, low_pair)
            scores_grad_t = scores_grad_t + fade * dot_nt(own, dy_pair)
            halves.append(dot_nn((fade * scores_t).astype(bf16), dy_pair))
        parts.append(jnp.where(left, halves[0], halves[1]))
    scaled_grad = scaled_grad + jnp.concatenate(parts, axis=1)
    scores_low = scores_grad_t.astype(bf16)
    b_grad = b_grad + dot_nn(scores_low, map_c)
    c_grad = c_grad + dot_tn(scores_low, map_b)
    x_grad = scaled_grad * step + skip[...] * dy
    lanes = in_ref.shape[2] - width
    rows = lax.broadcasted_iota(jnp.int32, (inner, lanes), 0)
    columns = lax.broadcasted_iota(jnp.int32, (inner, lanes), 1)
    member = ((rows >= columns * head_size) & (rows < (columns + 1) * head_size)).astype(bf16)
    step_grad = dot_nn((scaled_grad * value).astype(bf16), member)
    raw_grad = step_grad[:, :heads] * jax.nn.sigmoid(raw_full)
    taps_ref[5:6, :heads] += jnp.sum(raw_grad, axis=0, keepdims=True)
    raw_grad = jnp.concatenate([raw_grad, jnp.zeros((block, lanes - heads), f32)], axis=1)
    in_ref[:, :, width:] = raw_grad.astype(bf16).reshape(in_ref.shape[:2] + (lanes,))
    pre_grad = jnp.concatenate([x_grad, b_grad, c_grad], axis=1) * slope
    for k in range(count):
        taps_ref[k : k + 1, :] += jnp.sum(pre_grad * buf[5 + k : 5 + k + block, :], axis=0, keepdims=True)
    taps_ref[4:5, :] += jnp.sum(pre_grad, axis=0, keepdims=True)
    buf[0:block, :] = pre_grad
    buf[block : block + 8, :] = nextp[...]
    nextp[...] = buf[0:8, :]
    head_ref[...] = buf[0:8, :]
    in_grad = sum(taps[k : k + 1, :] * buf[3 - k : 3 - k + block, :] for k in range(count))
    in_ref[:, :, :width] = in_grad.astype(bf16).reshape(in_ref.shape[:2] + (width,))

    @pl.when(turn == 0)
    def _():
        tail_ref[...] = in_grad[block - 8 :, :]


def params():
    return pltpu.CompilerParams(vmem_limit_bytes=56 * 2**20)


def cost(flops, moved, powers):
    return pl.CostEstimate(flops=int(flops), bytes_accessed=int(moved), transcendentals=int(powers))


def rows_of(share, width, flip=0):
    per = BLOCK // share
    if flip:
        return pl.BlockSpec((per, None, share, width), lambda b, k: (flip - 1 - k, b, 0, 0))
    return pl.BlockSpec((per, None, share, width), lambda b, k: (k, b, 0, 0))


def each(height, width):
    return pl.BlockSpec((None, height, width), lambda b, k: (b, 0, 0))


def only(height, width):
    return pl.BlockSpec((height, width), lambda b, k: (0, 0))


def at_block(height, width, flip=0):
    if flip:
        return pl.BlockSpec((None, None, height, width), lambda b, k: (b, flip - 1 - k, 0, 0))
    return pl.BlockSpec((None, None, height, width), lambda b, k: (b, k, 0, 0))


def in_order(width, flip=0):
    if flip:
        return pl.BlockSpec((None, BLOCK, width), lambda b, k: (b, flip - 1 - k, 0))
    return pl.BlockSpec((None, BLOCK, width), lambda b, k: (b, k, 0))


def made(*shape, kind=bf16):
    return jax.ShapeDtypeStruct(shape, kind)


def scan_forward(cin, edge, taps, raw, bias, decay, decay_t, inner, size):
    shares, batch, share, width = cin.shape
    heads = raw.shape[3]
    tokens = shares * share
    blocks = tokens // BLOCK
    return pl.pallas_call(
        scan_kernel,
        grid=(batch, blocks),
        in_specs=[
            rows_of(share, width),
            each(8, width),
            only(8, width),
            rows_of(share, heads),
            only(1, heads),
            in_order(heads),
            pl.BlockSpec((None, heads, BLOCK), lambda b, k: (b, 0, k)),
        ],
        out_specs=[rows_of(share, width), rows_of(share, inner), at_block(size, inner), each(size, inner)],
        out_shape=[
            made(shares, batch, share, width),
            made(shares, batch, share, inner, kind=f32),
            made(batch, blocks, size, inner, kind=f32),
            made(batch, size, inner, kind=f32),
        ],
        scratch_shapes=[
            pltpu.VMEM((BLOCK + 8, width), f32),
            pltpu.VMEM((8, width), f32),
            pltpu.VMEM((size, inner), f32),
        ],
        compiler_params=params(),
        cost_estimate=cost(
            batch * tokens * inner * (4 * BLOCK + 4 * size), 10 * batch * tokens * inner, batch * tokens * heads * BLOCK
        ),
    )(cin, edge, taps, raw, bias, decay, decay_t)


def gate_forward(y, act, z, decay, lead, entering, skip, gain, w_out):
    shares, batch, share, inner = y.shape
    width, heads, size = act.shape[3], decay.shape[2], entering.shape[1]
    model = w_out.shape[1]
    tokens = shares * share
    return pl.pallas_call(
        gate_kernel,
        grid=(batch, tokens // BLOCK),
        in_specs=[
            rows_of(share, inner),
            rows_of(share, width),
            rows_of(share, inner),
            in_order(heads),
            at_block(1, inner),
            each(size, inner),
            only(1, inner),
            only(1, inner),
            only(inner, model),
        ],
        out_specs=[rows_of(share, inner), rows_of(share, inner), rows_of(share, 128), rows_of(share, model)],
        out_shape=[
            made(shares, batch, share, inner),
            made(shares, batch, share, inner),
            made(shares, batch, share, 128, kind=f32),
            made(shares, batch, share, model),
        ],
        compiler_params=params(),
        cost_estimate=cost(
            2 * batch * tokens * inner * (model + size), batch * tokens * inner * 18, batch * tokens * inner
        ),
    )(y, act, z, decay, lead, entering, skip, gain, w_out)


def gate_backward(push, w_out, mixed, z, act, decay, lead, gain):
    shares, batch, share, inner = mixed.shape
    width, heads, model = act.shape[3], decay.shape[2], w_out.shape[1]
    size = (width - inner) // 2
    tokens = shares * share
    return pl.pallas_call(
        gate_back_kernel,
        grid=(batch, tokens // BLOCK),
        in_specs=[
            rows_of(share, model),
            only(inner, model),
            rows_of(share, inner),
            rows_of(share, inner),
            rows_of(share, width),
            in_order(heads),
            at_block(1, inner),
            pl.BlockSpec((BLOCK // share, None, share, 128), lambda b, k: (k, b, 0, model // 128)),
            only(1, inner),
        ],
        out_specs=[rows_of(share, inner), rows_of(share, inner), each(size, inner), only(8, inner)],
        out_shape=[
            made(shares, batch, share, inner),
            made(shares, batch, share, inner),
            made(batch, size, inner, kind=f32),
            made(8, inner, kind=f32),
        ],
        compiler_params=params(),
        cost_estimate=cost(
            2 * batch * tokens * inner * (model + size), batch * tokens * inner * 18, batch * tokens * inner
        ),
    )(push, w_out, mixed, z, act, decay, lead, push, gain)


def scan_backward(cin, edge, taps, raw, bias, decay, decay_t, act, dy, start, lead, entering, leave_grad, skip):
    shares, batch, share, width = cin.shape
    heads, inner, size = raw.shape[3], dy.shape[3], entering.shape[1]
    tokens = shares * share
    blocks = tokens // BLOCK
    per = BLOCK // share
    return pl.pallas_call(
        scan_back_kernel,
        grid=(batch, blocks),
        in_specs=[
            rows_of(share, width, blocks),
            pl.BlockSpec(
                (None, None, 16, width),
                lambda b, k: (jnp.maximum((blocks - 1 - k) * per - 1, 0), b, share // 16 - 1, 0),
            ),
            each(8, width),
            only(8, width),
            rows_of(share, heads, blocks),
            only(1, heads),
            in_order(heads, blocks),
            pl.BlockSpec((None, heads, BLOCK), lambda b, k: (b, 0, blocks - 1 - k)),
            rows_of(share, width, blocks),
            rows_of(share, inner, blocks),
            at_block(size, inner, blocks),
            at_block(1, inner, blocks),
            each(size, inner),
            each(size, inner),
            only(1, inner),
        ],
        out_specs=[rows_of(share, width + 128, blocks), each(8, width), each(8, width), only(8, width)],
        out_shape=[
            made(shares, batch, share, width + 128),
            made(batch, 8, width, kind=f32),
            made(batch, 8, width, kind=f32),
            made(8, width, kind=f32),
        ],
        scratch_shapes=[
            pltpu.VMEM((BLOCK + 8, width), f32),
            pltpu.VMEM((8, width), f32),
            pltpu.VMEM((size, inner), f32),
        ],
        compiler_params=params(),
        cost_estimate=cost(
            batch * tokens * inner * (8 * BLOCK + 10 * size), 15 * batch * tokens * inner, batch * tokens * heads * BLOCK
        ),
    )(cin, cin, edge, taps, raw, bias, decay, decay_t, act, dy, start, lead, entering, leave_grad, skip)


def end_rows(in_grad, last, following, taps):
    shares, batch, share, width = in_grad.shape
    columns = last.shape[2]

    def kernel(rows, last_ref, next_ref, taps_ref, out_ref, buf):
        for b in range(batch):
            buf[0:8, :] = jnp.zeros((8, columns), f32)
            buf[8:16, :] = next_ref[b]
            added = sum(taps_ref[k : k + 1, :] * buf[3 - k : 11 - k, :] for k in range(4))
            old = rows[b].astype(f32)
            end = jnp.concatenate([last_ref[b] + added, old[8:, columns:]], axis=1)
            out_ref[b] = jnp.concatenate([old[:8], end], axis=0).astype(bf16)

    block = pl.BlockSpec((None, batch, 16, width), lambda i: (shares - 1, 0, share // 16 - 1, 0))

    def whole(array):
        zeros = (0,) * array.ndim
        return pl.BlockSpec(array.shape, lambda i: zeros)

    return pl.pallas_call(
        kernel,
        grid=(1,),
        in_specs=[block, whole(last), whole(following), whole(taps)],
        out_specs=block,
        out_shape=made(*in_grad.shape),
        input_output_aliases={0: 0},
        scratch_shapes=[pltpu.VMEM((16, columns), f32)],
        compiler_params=params(),
        cost_estimate=cost(16 * width * batch, 200 * width * batch, 0),
    )(in_grad, last, following, taps)


def weight_grads(groups, depth, tile, extra=None):
    rows = groups[0][0][0].shape[0]
    tiles = [group[0][1].shape[1] // tile for group in groups]
    starts = [sum(tiles[:g]) for g in range(len(groups) + 1)]
    terms = max(len(group) for group in groups)
    flat = [array for group in groups for term in group for array in term]
    count = len(flat)

    def kernel(*refs):
        out, turned = refs[-2], refs[-1]
        j = pl.program_id(0)
        place = 0
        for g, group in enumerate(groups):
            mine = refs[place : place + 2 * len(group)]
            place += 2 * len(group)

            @pl.when(j == starts[g])
            def _(mine=mine):
                for t in range(len(mine) // 2):
                    turned[t] = mine[2 * t][...].T

            @pl.when((j >= starts[g]) & (j < starts[g + 1]))
            def _(mine=mine):
                total = sum(dot_nn(turned[t], mine[2 * t + 1][...]) for t in range(len(mine) // 2))
                out[...] = total.astype(bf16)

        if extra is not None:

            @pl.when(j >= starts[-1])
            def _():
                out[...] = refs[count][...]

    specs = []
    for g, group in enumerate(groups):
        for _ in group:
            specs.append(pl.BlockSpec((rows, depth), lambda j: (0, 0), pipeline_mode=pl.Buffered(1)))
            specs.append(
                pl.BlockSpec((rows, tile), lambda j, a=starts[g], n=tiles[g]: (0, jnp.clip(j - a, 0, n - 1)))
            )
    steps = starts[-1]
    if extra is not None:
        flat = flat + [extra]
        specs.append(pl.BlockSpec((depth, tile), lambda j, a=steps: (0, jnp.maximum(j - a, 0))))
        steps += extra.shape[1] // tile
    return pl.pallas_call(
        kernel,
        grid=(steps,),
        in_specs=specs,
        out_specs=pl.BlockSpec((depth, tile), lambda j: (0, j)),
        out_shape=jax.ShapeDtypeStruct((depth, steps * tile), bf16),
        scratch_shapes=[pltpu.VMEM((terms, depth, rows), bf16)],
        compiler_params=params(),
        cost_estimate=cost(2 * terms * rows * depth * tile * steps, 2 * (count * rows * depth + depth * tile * steps), 0),
    )(*flat)


def gates_of(gates_ref, mine):
    terms = gates_ref[...].astype(f32)
    every = mine.shape[1]
    return terms[:, :every] + terms[:, every : 2 * every]


def expert_forward_kernel(shared, x_ref, grad_ref, gates_ref, mine, w_gu, w_down, *refs):
    out_ref, logit_ref, both_ref = refs[-3:]
    x = x_ref[...]
    gates = gates_of(gates_ref, mine)
    wide = grad_ref[...].astype(f32)
    out = own = total = 0.0
    width = w_down.shape[1]
    for e in range(w_gu.shape[0]):
        weight = jnp.sum(gates * mine[e : e + 1, :], axis=1, keepdims=True)
        both = dot_nn(x, w_gu[e])
        both_ref[:, 2 * e * width : 2 * (e + 1) * width] = both
        gate, up = both[:, :width], both[:, width:]
        act = (gate * jax.nn.sigmoid(gate) * up).astype(bf16)
        result = dot_nn(act, w_down[e]).astype(bf16).astype(f32)
        push = jnp.sum(wide * result, axis=1, keepdims=True)
        own = own + push * mine[e : e + 1, :]
        total = total + weight * push
        out = out + weight * result
    if shared:
        ws_gu, ws_down = refs[:2]
        first, ff = 2 * w_gu.shape[0] * width, ws_down.shape[0]
        gate, up = dot_nn(x, ws_gu[0]), dot_nn(x, ws_gu[1])
        both_ref[:, first : first + ff] = gate
        both_ref[:, first + ff :] = up
        act = (gate * jax.nn.sigmoid(gate) * up).astype(bf16)
        out = out + dot_nn(act, ws_down[...])
    out_ref[...] = out.astype(bf16)
    logit_ref[...] = gates * (own - total)


def expert_backward_kernel(shared, grad_ref, gates_ref, both_ref, mine, w_gu, w_down, *refs):
    grad = grad_ref[...]
    gates = gates_of(gates_ref, mine)
    wide = grad.astype(f32)
    dx_ref, act_ref, gu_ref = refs[2:5] if shared else refs

    def back(gate, up, act_push):
        sigma = jax.nn.sigmoid(gate)
        silu = gate * sigma
        slope = sigma + silu * (1.0 - sigma)
        gu_grad = jnp.concatenate([act_push * up * slope, act_push * silu], axis=1).astype(bf16)
        return (silu * up).astype(bf16), gu_grad

    dx = 0.0
    width = w_down.shape[1]
    for e in range(w_gu.shape[0]):
        weight = jnp.sum(gates * mine[e : e + 1, :], axis=1, keepdims=True)
        act_push = dot_nt((weight * wide).astype(bf16), w_down[e])
        middle = (2 * e + 1) * width
        gate, up = both_ref[:, middle - width : middle], both_ref[:, middle : middle + width]
        act, gu_grad = back(gate, up, act_push)
        act_ref[:, e * width : (e + 1) * width] = (weight * act.astype(f32)).astype(bf16)
        gu_ref[:, middle - width : middle + width] = gu_grad
        dx = dx + dot_nt(gu_grad, w_gu[e]).astype(bf16).astype(f32)
    if shared:
        ws_gu, ws_down = refs[:2]
        s_act_ref, s_gu_ref = refs[5:]
        first, ff = 2 * w_gu.shape[0] * width, ws_down.shape[0]
        gate, up = both_ref[:, first : first + ff], both_ref[:, first + ff :]
        act, gu_grad = back(gate, up, dot_nt(grad, ws_down[...]))
        s_act_ref[...] = act
        s_gu_ref[...] = gu_grad
        dx = dx + dot_nt(gu_grad[:, :ff], ws_gu[0]) + dot_nt(gu_grad[:, ff:], ws_gu[1])
    dx_ref[...] = dx.astype(bf16)


def by_rows(columns, at=0):
    return pl.BlockSpec((ROWS, columns), lambda i: (i, at))


def kept(array):
    zeros = (0,) * array.ndim
    return pl.BlockSpec(array.shape, lambda i: zeros, pipeline_mode=pl.Buffered(1))


def experts_forward(x, grad, mine, w_gu, w_down, shared=()):
    rows = x.shape[0]
    count, model, double = w_gu.shape
    beside = x.shape[1] - model
    every = mine.shape[1]
    hidden = count * double + (2 * shared[1].shape[0] if shared else 0)
    return pl.pallas_call(
        lambda *refs: expert_forward_kernel(bool(shared), *refs),
        grid=(rows // ROWS,),
        in_specs=[by_rows(model), by_rows(model), by_rows(beside, model // beside)]
        + [kept(w) for w in (mine, w_gu, w_down, *shared)],
        out_specs=[by_rows(model), by_rows(every), by_rows(hidden)],
        out_shape=[made(rows, model), made(rows, every, kind=f32), made(rows, hidden, kind=f32)],
        compiler_params=params(),
        cost_estimate=cost(3 * rows * hidden * model, 3 * hidden * model + rows * (6 * model + 4 * hidden), rows * hidden),
    )(x, grad, x, mine, w_gu, w_down, *shared)


def experts_backward(x, grad, both, mine, w_gu, w_down, shared=()):
    rows = x.shape[0]
    count, model, double = w_gu.shape
    beside = x.shape[1] - model
    hidden = both.shape[1]
    widths = [model, count * double // 2, count * double]
    if shared:
        widths += [shared[1].shape[0], 2 * shared[1].shape[0]]
    return pl.pallas_call(
        lambda *refs: expert_backward_kernel(bool(shared), *refs),
        grid=(rows // ROWS,),
        in_specs=[by_rows(model), by_rows(beside, model // beside), by_rows(hidden)]
        + [kept(w) for w in (mine, w_gu, w_down, *shared)],
        out_specs=[by_rows(w) for w in widths],
        out_shape=[made(rows, w) for w in widths],
        compiler_params=params(),
        cost_estimate=cost(3 * rows * hidden * model, 3 * hidden * model + rows * (4 * model + 7 * hidden), rows * hidden),
    )(grad, x, both, mine, w_gu, w_down, *shared)


def summed(got):
    return sum(got[i].astype(f32) for i in range(got.shape[0]))


def two_terms(values, width):
    high = values.astype(bf16)
    low = (values - high.astype(f32)).astype(bf16)
    terms, room = [high, low], width - 2 * values.shape[1]
    if room:
        terms.append(jnp.zeros((values.shape[0], room), bf16))
    return jnp.concatenate(terms, axis=1)


def after_mix_kernel(inner, got, x, squares, used, gain, router, packed_ref, hidden_ref, mix_ref, scale_ref):
    model = x.shape[1]
    mix = summed(got)
    gate_scale = lax.rsqrt(squares[...] / inner + norm_eps)
    hidden = x[...].astype(f32) + mix * gate_scale
    scale = lax.rsqrt(jnp.mean(hidden * hidden, axis=1, keepdims=True) + norm_eps)
    normed = (hidden * scale * gain[...]).astype(bf16)
    mask = used[...] > 0.0
    logits = jnp.where(mask, dot_nn(normed, router[...]), -1e30)
    powers = jnp.where(mask, jnp.exp(logits - jnp.max(logits, axis=1, keepdims=True)), 0.0)
    gates = powers / jnp.sum(powers, axis=1, keepdims=True)
    packed_ref[:, :model] = normed
    packed_ref[:, model:] = two_terms(gates, packed_ref.shape[1] - model)
    hidden_ref[...] = hidden
    mix_ref[...] = mix
    lane = lax.broadcasted_iota(jnp.int32, scale_ref.shape, 1)
    scale_ref[...] = jnp.where(lane == 0, gate_scale, scale)


def after_ffn_kernel(inner, got, hidden_in, mix, scales, grad, gain, packed_ref, grad_ref, sum_ref):
    model = grad.shape[1]
    dx, hidden = summed(got), hidden_in[...]
    gate_scale, scale = scales[:, 0:1], scales[:, 1:2]
    gained = dx * gain[...]
    mean = jnp.mean(gained * hidden, axis=1, keepdims=True)
    hidden_grad = grad[...].astype(f32) + scale * (gained - hidden * (scale * scale * mean))
    grad_ref[...] = hidden_grad
    push = jnp.sum(hidden_grad * mix[...], axis=1, keepdims=True)
    slope = (-0.5 / inner) * push * gate_scale * gate_scale * gate_scale
    packed_ref[:, :model] = (hidden_grad * gate_scale).astype(bf16)
    packed_ref[:, model:] = two_terms(slope, packed_ref.shape[1] - model)

    @pl.when(pl.program_id(0) == 0)
    def _():
        sum_ref[...] = jnp.zeros_like(sum_ref)

    sum_ref[0:1, :] += jnp.sum(dx * hidden * scale, axis=0, keepdims=True)


def after_proj_kernel(got, x_in, hidden_grad, gain, out_ref):
    dn, x = summed(got), x_in[...].astype(f32)
    scale = lax.rsqrt(jnp.mean(x * x, axis=1, keepdims=True) + norm_eps)
    gained = dn * gain[...]
    mean = jnp.mean(gained * x, axis=1, keepdims=True)
    out_ref[...] = (hidden_grad[...] + scale * (gained - x * (scale * scale * mean))).astype(bf16)


def on_share(kernel, got, rows, wholes, outs, sums=()):
    shares, batch, share, model = got.shape

    def rows_at(width):
        return pl.BlockSpec((None, share, width), lambda b: (b, 0, 0))

    def kept_at(shape):
        return pl.BlockSpec(shape, lambda b: (0, 0))

    return pl.pallas_call(
        kernel,
        grid=(batch,),
        in_specs=[pl.BlockSpec((shares, None, share, model), lambda b: (0, b, 0, 0))]
        + [rows_at(r.shape[2]) for r in rows]
        + [kept_at(w.shape) for w in wholes],
        out_specs=[rows_at(width) for width, _ in outs] + [kept_at(shape) for shape in sums],
        out_shape=[made(batch, share, width, kind=kind) for width, kind in outs]
        + [made(*shape, kind=f32) for shape in sums],
        compiler_params=params(),
        cost_estimate=cost(40 * batch * share * model, 30 * batch * share * model, batch * share),
    )(got, *rows, *wholes)


def shifted(array, axis, by):
    count = lax.axis_size(axis)
    pairs = [(i, i + by) for i in range(count) if 0 <= i + by < count]
    return lax.ppermute(array, axis, pairs)


def prefix(part, axis, combine, identity):
    place = lax.axis_index(axis)
    gathered = jax.tree.map(lambda a: lax.all_gather(a, axis), part)
    state = jax.tree.map(lambda a, e: jnp.zeros_like(a) + jnp.asarray(e, a.dtype), part, identity)

    def one(lap, state):
        return combine(
            state, jax.tree.map(lambda a: lax.dynamic_index_in_dim(a, lap, 0, False), gathered)
        )

    return lax.fori_loop(0, place, one, state)


def prefix_2(array, axis, combine, identity):
    count, place = (lax.axis_size(axis), lax.axis_index(axis))
    everything = jax.tree.map(
        lambda part, kind: lax.all_gather(part.astype(kind), axis),
        array,
        jax.tree.map(lambda a: jnp.bfloat16 if a.dtype == jnp.float32 else a.dtype, array),
    )
    start = jax.tree.map(
        lambda part, zero: jnp.broadcast_to(jnp.asarray(zero, part.dtype), part.shape),
        array,
        identity,
    )

    def lap(k, before):
        at = count - 1 - k
        reached = at > place
        new = combine(
            before, jax.tree.map(lambda part, own: part[at].astype(own.dtype), everything, array)
        )
        return jax.tree.map(lambda a, b: jnp.where(reached, a, b), new, before)

    return lax.fori_loop(0, count, lap, start)


def swap_shares(part):
    return lax.all_to_all(part, "head", split_axis=0, concat_axis=0, tiled=True)


def gather_shares(share):
    copies = jnp.broadcast_to(share[None], (lax.axis_size("head"),) + share.shape)
    return lax.all_to_all(copies, "head", split_axis=0, concat_axis=0, tiled=True)


def relay(part):
    count, place = lax.axis_size("head"), lax.axis_index("head")

    def passed(array, by, start=0):
        pairs = [(i, i + by) for i in range(count) if 0 <= i + by < count]
        pairs = [(i, j) for i, j in pairs if 0 <= i - start * by < count]
        return lax.ppermute(array, "head", pairs)

    if count == 4:
        up, down = passed(part, 1), passed(part, -1)
        far = lax.ppermute(part, "head", [(0, 3), (3, 0)])
        up_two, down_two = passed(up, 1, 1), passed(down, -1, 1)
        return [
            part,
            jnp.where(place >= 1, up, far),
            jnp.where(place >= 2, up_two, down_two),
            jnp.where(place >= 3, far, down),
        ]
    up, down = [part], [part]
    for _ in range(count - 1):
        up.append(passed(up[-1], 1))
        down.append(passed(down[-1], -1))
    return [part] + [jnp.where(place >= d, up[d], down[count - d]) for d in range(1, count)]


def laid(pieces, axis=0):
    count, place = lax.axis_size("head"), lax.axis_index("head")
    shape = pieces[0].shape[:axis] + (count,) + pieces[0].shape[axis:]
    out = jnp.zeros(shape, pieces[0].dtype)
    for d, piece in enumerate(pieces):
        out = lax.dynamic_update_index_in_dim(out, piece, (place + count - d) % count, axis)
    return out


def relay_shares(share, axis=0):
    return laid(relay(share), axis)


def bits_of(axis):
    count = lax.axis_size(axis)
    return [(1 << k) for k in range(count.bit_length() - 1)]


def across(array, axis, bit):
    return lax.ppermute(array, axis, [(i, i ^ bit) for i in range(lax.axis_size(axis))])


def add_over(array, *axes):
    for axis in axes:
        for bit in bits_of(axis):
            array = array + across(array, axis, bit)
    return array


def join_over(array, dimension, *axes):
    for axis in axes:
        place = lax.axis_index(axis)
        for bit in bits_of(axis):
            other = across(array, axis, bit)
            array = jnp.where(
                (place & bit) == 0,
                jnp.concatenate([array, other], axis=dimension),
                jnp.concatenate([other, array], axis=dimension),
            )
    return array


def tie(*arrays):
    return lax.optimization_barrier(arrays)


def around(array, by):
    count = lax.axis_size("seq")
    if by % count == 0:
        return array
    return lax.ppermute(array, "seq", [(i, (i + by) % count) for i in range(count)])


def spread_last(local_part, rank_index, part_count):
    local_width = local_part.shape[-1]
    full_array = jnp.zeros(local_part.shape[:-1] + (local_width * part_count,), jnp.float32)
    return lax.dynamic_update_slice_in_dim(
        full_array, local_part, rank_index * local_width, local_part.ndim - 1
    )


def chain_forward(earlier, later):
    return (earlier[0] * later[0], later[0] * earlier[1] + later[1])


def chain_backward(earlier, later):
    return (earlier[0] * later[0], later[1] + later[0] * earlier[1])


def local(
    x_in,
    d_out,
    log_decay,
    routes,
    norm1_gain,
    w_in_zx,
    w_in_bc,
    w_in_dt,
    dt_bias,
    conv_x,
    conv_x_bias,
    conv_bc,
    conv_bc_bias,
    skip_d,
    gate_norm_gain,
    w_out,
    norm2_gain,
    router,
    w_expert_gu,
    w_expert_down,
    w_shared_gu,
    w_shared_down,
):
    batch_size, tokens, model_width = x_in.shape
    inner_dev = w_in_zx.shape[2]
    heads_dev = w_in_dt.shape[1]
    head_size = inner_dev // heads_dev
    state_size = w_in_bc.shape[1] // 2
    conv_taps = conv_x.shape[0]
    experts_dev = w_expert_gu.shape[0]
    head_count = lax.axis_size("head")
    seq_count = lax.axis_size("seq")
    head_rank = lax.axis_index("head")
    seq_rank = lax.axis_index("seq")
    inner_all = inner_dev * head_count
    experts_all = experts_dev * seq_count * head_count
    share_rows = tokens // head_count
    rows_all = batch_size * tokens
    conv_width = inner_dev + 2 * state_size

    def by_share(array):
        array = array.reshape((batch_size, head_count, share_rows) + array.shape[2:])
        return jnp.swapaxes(array, 0, 1)

    def by_position(array):
        return jnp.swapaxes(array, 0, 1).reshape(batch_size, tokens, array.shape[-1])

    def own_share(array):
        return lax.dynamic_index_in_dim(array, head_rank, 0, keepdims=False)

    def flat(array):
        return array.reshape(-1, array.shape[-1])

    def times(a, b):
        return lax.dot_general(a, b, (((a.ndim - 1,), (0,)), ((), ())), preferred_element_type=f32)

    def times_t(a, b):
        return lax.dot_general(a, b, (((a.ndim - 1,), (1,)), ((), ())), preferred_element_type=f32)

    def scattered(array, axes):
        return lax.psum_scatter(array, axes, scatter_dimension=0, tiled=True)

    x_rows, grad_rows = by_share(x_in), by_share(d_out)
    grads_in = [flat(around(grad_rows, k)) for k in range(seq_count)]
    input_wide = x_rows.astype(f32)
    scale_one = lax.rsqrt(jnp.mean(input_wide * input_wide, axis=-1, keepdims=True) + norm_eps)
    normed_one = (input_wide * scale_one * norm1_gain).astype(bf16)
    w_conv = jnp.concatenate([w_in_zx[1], w_in_bc], axis=-1)
    w_step = jnp.pad(w_in_dt, ((0, 0), (0, 128 - heads_dev)))
    w_late = jnp.concatenate([w_conv, w_step], axis=-1)
    conv_in = times(normed_one, w_conv).astype(bf16)
    step_raw = times(normed_one, w_step)[..., :heads_dev]
    gate_z = times(normed_one, w_in_zx[0])
    edge_rows = shifted(conv_in[head_count - 1, :, share_rows - 8 :].astype(f32), "seq", 1)
    taps = jnp.concatenate([conv_x, conv_bc], axis=1)
    bias = jnp.concatenate([conv_x_bias, conv_bc_bias])
    taps_bias = jnp.concatenate([taps, bias[None], jnp.zeros((7 - conv_taps, conv_width), f32)])
    decay_across = jnp.transpose(log_decay, (0, 2, 1))
    step_bias = dt_bias[None]
    totals = jnp.sum(log_decay.reshape(batch_size, -1, BLOCK, heads_dev), axis=2)
    before = [jnp.zeros_like(totals[:, 0])]
    for k in range(totals.shape[1]):
        before.append(before[-1] + totals[:, k])
    lead = jnp.repeat(jnp.exp(jnp.stack(before, axis=1)), head_size, axis=-1)
    device_decay, lead = lead[:, -1:], lead[:, :-1, None]
    skip = jnp.repeat(skip_d, head_size)[None]
    gate_gain = gate_norm_gain[None]

    conv_act, scanned, starts, leaving = scan_forward(
        conv_in, edge_rows, taps_bias, step_raw, step_bias, log_decay, decay_across, inner_dev, state_size
    )
    identity = (jnp.ones_like(device_decay), jnp.zeros_like(leaving))
    if seq_count == 2:
        entering = shifted(leaving, "seq", 1)
    else:
        _, entering = prefix((device_decay, leaving), "seq", chain_forward, identity)
    mixed, gated_low, squares, partial_out = gate_forward(
        scanned, conv_act, gate_z, log_decay, lead, entering, skip, gate_gain, w_out
    )

    got_mix, *grads_in = tie(swap_shares(partial_out), *grads_in)
    squares = own_share(add_over(squares[..., 0], "head"))
    expert_ids = jnp.arange(experts_all, dtype=jnp.int32)
    used = jnp.any(own_share(by_share(routes))[..., None] == expert_ids, axis=2).astype(f32)
    x_share, grad_share = own_share(x_rows), own_share(grad_rows)
    beside = -(-2 * experts_all // 128) * 128
    normed_share, hidden, mix_out, scales = on_share(
        lambda *refs: after_mix_kernel(inner_all, *refs),
        got_mix,
        [x_share, squares[..., None], used],
        [norm2_gain[None], router],
        [(model_width + beside, bf16), (model_width, f32), (model_width, f32), (128, f32)],
    )
    pieces = relay(normed_share)
    rows_in = [flat(laid([around(piece, k) for piece in pieces])) for k in range(seq_count)]

    first = (seq_rank * head_count + head_rank) * experts_dev
    mine = (jnp.arange(8)[:, None] + first == expert_ids) & (jnp.arange(8)[:, None] < experts_dev)
    mine = mine.astype(f32)
    turns = [*range(1, seq_count), 0]
    ffn_out, ffn_dx, logit_grad, before_act = [], [], [], []
    for k in turns:
        shared = (w_shared_gu, w_shared_down) if k == 0 else ()
        out, logit, both = experts_forward(rows_in[k], grads_in[k], mine, w_expert_gu, w_expert_down, shared)
        ffn_out.append(around(out, -k))
        logit_grad.append(around(logit, -k))
        before_act.append(both)
    ffn_low = sum(f.astype(f32) for f in ffn_out).astype(bf16)
    ffn_low = ffn_low.reshape(head_count, batch_size, share_rows, model_width)
    ffn_low, before_act[-1] = tie(ffn_low, before_act[-1])
    got_out = swap_shares(ffn_low)
    up_terms, down_terms = [], []
    for k, both in zip(turns, before_act):
        shared = (w_shared_gu, w_shared_down) if k == 0 else ()
        made_k = experts_backward(rows_in[k], grads_in[k], both, mine, w_expert_gu, w_expert_down, shared)
        ffn_dx.append(around(made_k[0], -k))
        down_terms.append((grads_in[k], made_k[1]))
        up_terms.append((rows_in[k], made_k[2]))
    shared_terms = [[(rows_in[0], made_k[4])], [(grads_in[0], made_k[3])]]
    logit_grad = sum(logit_grad).astype(bf16)
    ffn_dx = sum(d.astype(f32) for d in ffn_dx) + times_t(logit_grad, router)
    ffn_dx = ffn_dx.astype(bf16).reshape(ffn_low.shape)
    ffn_dx, *gu_grads = tie(ffn_dx, *[term[1] for term in up_terms])
    up_terms = [(term[0], gu_grad) for term, gu_grad in zip(up_terms, gu_grads)]
    ffn_dx, got_out = tie(ffn_dx, got_out)
    got_dx = swap_shares(ffn_dx)
    expert_grads = [
        weight_grads([up_terms[k : k + 2], down_terms[k : k + 2]], model_width, 512)
        for k in range(0, seq_count, 2)
    ]
    if len(expert_grads) > 1:
        expert_grads = [sum(g.astype(f32) for g in expert_grads).astype(bf16)]
    got_dx, expert_grads, logit_grad = tie(got_dx, expert_grads[0], logit_grad)
    expert_sum = scattered(expert_grads, "dp")
    grad_router = lax.dot_general(
        logit_grad, rows_in[0], (((0,), (0,)), ((), ())), preferred_element_type=f32
    )[:, :model_width]
    push_share, hidden_grad, norm_two_sums = on_share(
        lambda *refs: after_ffn_kernel(inner_all, *refs),
        got_dx,
        [hidden, mix_out, scales, grad_share],
        [norm2_gain[None]],
        [(model_width + 128, bf16), (model_width, f32)],
        [(8, model_width)],
    )
    out_push = relay_shares(push_share)

    layer_share, out_push = tie((hidden + summed(got_out)).astype(bf16), out_push)
    layer_out = gather_shares(layer_share)

    mixed_grad, z_grad, entering_grad, channel_sums = gate_backward(
        out_push, w_out, mixed, gate_z, conv_act, log_decay, lead, gate_gain
    )
    if seq_count == 2:
        leaving_grad = shifted(entering_grad.astype(bf16), "seq", -1).astype(f32)
    else:
        _, leaving_grad = prefix_2((device_decay, entering_grad), "seq", chain_backward, identity)
    in_grad, first_rows, last_rows, tap_sums = scan_backward(
        conv_in,
        edge_rows,
        taps_bias,
        step_raw,
        step_bias,
        log_decay,
        decay_across,
        conv_act,
        mixed_grad,
        starts,
        lead,
        entering,
        leaving_grad,
        skip,
    )
    early_dx = times_t(z_grad, w_in_zx[0])
    in_grad, layer_out, early_dx, expert_sum = tie(in_grad, layer_out, early_dx, expert_sum)
    in_grad = end_rows(in_grad, last_rows, shifted(first_rows, "seq", -1), taps_bias)
    normed_one_grad = early_dx + times_t(in_grad, w_late)
    grad_norm_one = jnp.sum(normed_one_grad * input_wide * scale_one, axis=(0, 1, 2))
    normed_one_grad = normed_one_grad.astype(bf16)
    normed_one_grad, in_grad = tie(normed_one_grad, in_grad)
    got_dn = swap_shares(normed_one_grad)

    def whole(array):
        return spread_last(array, head_rank, head_count).reshape(-1)

    small = [
        norm_two_sums[0],
        grad_router.reshape(-1),
        whole(tap_sums[:conv_taps, :inner_dev]),
        whole(tap_sums[conv_taps, :inner_dev]),
        whole(channel_sums[0]),
        grad_norm_one,
        tap_sums[:conv_taps, inner_dev:].reshape(-1),
        tap_sums[conv_taps, inner_dev:],
        whole(tap_sums[conv_taps + 1, :heads_dev]),
        whole(jnp.sum(channel_sums[1].reshape(heads_dev, head_size), axis=-1)),
    ]
    sizes = [a.shape[0] for a in small]
    small = jnp.concatenate(small + [jnp.zeros((128 * model_width - sum(sizes),), f32)])
    small = small.reshape(128, model_width).T.astype(bf16)
    grad_late = weight_grads([[(flat(normed_one), flat(in_grad))]], model_width, 128, small)
    early_terms = [[(flat(out_push), flat(gated_low))], [(flat(normed_one), flat(z_grad))]]
    grad_early = weight_grads(early_terms + shared_terms, model_width, 256)
    late_sum = scattered(grad_late, ("dp", "seq")).astype(f32)
    late_sum, got_dn = tie(late_sum, got_dn)
    input_grad = on_share(
        after_proj_kernel, got_dn, [x_share, hidden_grad], [norm1_gain[None]], [(model_width, bf16)]
    )[0]
    merged = jnp.concatenate([late_sum[:, inner_dev:conv_width], late_sum[:, conv_width + 128 :]], axis=1)
    for bit in bits_of("head"):
        merged = merged.astype(bf16)
        merged = merged.astype(f32) + across(merged, "head", bit).astype(f32)
    merged = merged.astype(bf16)
    input_grad, merged = tie(input_grad, merged)
    merged = join_over(merged[None], 0, "dp", "seq")
    merged = jnp.swapaxes(merged.reshape((seq_count, -1) + merged.shape[1:]), 0, 1)
    merged = merged.reshape(model_width, -1).astype(f32)
    layer_out = by_position(layer_out)
    late_sum, grad_early = tie(late_sum, grad_early)
    early_sum = scattered(grad_early, ("dp", "seq")).astype(f32)
    d_input = relay_shares(input_grad, 1).reshape(batch_size, tokens, model_width)

    grad_bc = merged[:, : 2 * state_size]
    small = merged[:, 2 * state_size :].T.reshape(-1)
    ends = [sum(sizes[:k]) for k in range(len(sizes) + 1)]
    small = [small[ends[k] : ends[k + 1]] for k in range(len(sizes))]
    expert_sum = expert_sum.astype(f32)
    double = w_expert_gu.shape[2]
    grad_gu = [expert_sum[:, e * double : (e + 1) * double] for e in range(experts_dev)]
    expert_sum = expert_sum[:, experts_dev * double :]
    width = double // 2
    grad_down = [expert_sum[:, e * width : (e + 1) * width].T for e in range(experts_dev)]
    shared_sum = early_sum[:, 2 * inner_dev :]
    ff_dev = w_shared_down.shape[0]
    return (
        layer_out,
        d_input,
        small[5],
        jnp.stack([early_sum[:, inner_dev : 2 * inner_dev], late_sum[:, :inner_dev]]),
        grad_bc,
        late_sum[:, conv_width : conv_width + heads_dev],
        small[8],
        small[2].reshape(conv_taps, inner_all),
        small[3],
        small[6].reshape(conv_taps, 2 * state_size),
        small[7],
        small[9],
        small[4],
        early_sum[:, :inner_dev].T,
        small[0],
        small[1].reshape(experts_all, model_width).T,
        jnp.stack(grad_gu),
        jnp.stack(grad_down),
        jnp.stack([shared_sum[:, :ff_dev], shared_sum[:, ff_dev : 2 * ff_dev]]),
        shared_sum[:, 2 * ff_dev :].T,
    )


def solution(mesh):
    placed = (
        P("dp", "seq", None),
        P("dp", "seq", None),
        P("dp", "seq", "head"),
        P("dp", "seq", None),
        P(),
        P(None, None, "head"),
        P(),
        P(None, "head"),
        P("head"),
        P(None, "head"),
        P("head"),
        P(),
        P(),
        P("head"),
        P("head"),
        P("head", None),
        P(),
        P(),
        P(("seq", "head"), None, None),
        P(("seq", "head"), None, None),
        P(None, None, "head"),
        P("head", None),
    )
    return jax.shard_map(
        local,
        mesh=mesh,
        in_specs=placed,
        out_specs=(
            P("dp", "seq", None),
            P("dp", "seq", None),
            P(),
            P(None, ("dp", "seq"), "head"),
            P(),
            P(("dp", "seq"), "head"),
            P(),
            P(),
            P(),
            P(),
            P(),
            P(),
            P(),
            P("head", ("dp", "seq")),
            P(),
            P(),
            P(("seq", "head"), "dp", None),
            P(("seq", "head"), None, "dp"),
            P(None, ("dp", "seq"), "head"),
            P("head", ("dp", "seq")),
        ),
        check_vma=False,
    )
```

```python
import jax
import jax.numpy as jnp
from jax import lax
from jax.experimental import pallas as pl
from jax.experimental.pallas import tpu as pltpu
from jax.sharding import PartitionSpec as P

BLOCK = 256
ROWS = 256

bf16, f32 = jnp.bfloat16, jnp.float32
norm_eps = 1e-05
highest = lax.Precision.HIGHEST


def dot_nn(a, b):
    return lax.dot_general(a, b, (((1,), (0,)), ((), ())), preferred_element_type=f32)


def dot_nt(a, b):
    return lax.dot_general(a, b, (((1,), (1,)), ((), ())), preferred_element_type=f32)


def dot_tn(a, b):
    return lax.dot_general(a, b, (((0,), (0,)), ((), ())), preferred_element_type=f32)


def lower_mask(count, flip=False):
    rows = lax.broadcasted_iota(jnp.int32, (count, count), 0)
    columns = lax.broadcasted_iota(jnp.int32, (count, count), 1)
    return columns >= rows if flip else rows >= columns


def sum_down(values):
    lower = lower_mask(values.shape[0]).astype(f32)
    return jnp.dot(lower, values, precision=highest, preferred_element_type=f32)


def sum_right(values):
    upper = lower_mask(values.shape[1], True).astype(f32)
    return jnp.dot(values, upper, precision=highest, preferred_element_type=f32)


def first_half(rows, width=128):
    return lax.broadcasted_iota(jnp.int32, (rows, width), 1) < width // 2


def per_channel(values, head_size):
    rows, heads = values.shape
    left = first_half(rows, 2 * head_size)
    return jnp.concatenate(
        [jnp.where(left, values[:, h : h + 1], values[:, h + 1 : h + 2]) for h in range(0, heads, 2)],
        axis=1,
    )


def joined(ref):
    return ref[...].reshape(-1, ref.shape[-1])


def softplus(v):
    return jnp.maximum(v, 0.0) + jnp.log1p(jnp.exp(-jnp.abs(v)))


def scan_kernel(cin, edge, taps, raw, bias, decay, decay_t, act_ref, y_ref, start_ref, leave_ref, buf, prev, state):
    heads = decay.shape[1]
    block = BLOCK
    inner = y_ref.shape[2]
    size = state.shape[0]
    head_size = inner // heads
    pair = 2 * head_size
    count = 4

    @pl.when(pl.program_id(1) == 0)
    def _():
        prev[...] = edge[...]
        state[...] = jnp.zeros_like(state)

    buf[0:8, :] = prev[...]
    buf[8 : 8 + block, :] = joined(cin).astype(f32)
    pre = taps[4:5, :] + sum(taps[k : k + 1, :] * buf[5 + k : 5 + k + block, :] for k in range(count))
    prev[...] = buf[block : block + 8, :]
    act = (pre * jax.nn.sigmoid(pre)).astype(bf16)
    act_ref[...] = act.reshape(act_ref.shape)
    map_b, map_c = act[:, inner : inner + size], act[:, inner + size :]
    step = softplus(joined(raw) + bias[...])
    scaled = act[:, :inner].astype(f32) * per_channel(step, head_size)
    within, across = sum_down(decay[...]), sum_right(decay_t[...])
    grown = per_channel(jnp.exp(within), head_size)
    tail = per_channel(jnp.exp(within[block - 1 :, :] - within), head_size)
    before = state[...]
    start_ref[...] = before
    carried = grown * dot_nn(map_c, before.astype(bf16))
    scores = dot_nt(map_c, map_b)
    causal = lower_mask(block)
    low = scaled.astype(bf16)
    left = first_half(block, pair)
    for h in range(0, heads, 2):
        columns = slice(h * head_size, h * head_size + pair)
        halves = []
        for a in (h, h + 1):
            gap = jnp.where(causal, within[:, a : a + 1] - across[a : a + 1, :], -1e30)
            halves.append(dot_nn((jnp.exp(gap) * scores).astype(bf16), low[:, columns]))
        y_pair = carried[:, columns] + jnp.where(left, halves[0], halves[1])
        y_ref[:, :, columns] = y_pair.reshape(y_ref.shape[:2] + (pair,))
    after = grown[block - 1 :, :] * before + dot_tn(map_b, (scaled * tail).astype(bf16))
    state[...] = after
    leave_ref[...] = after


def gate_kernel(y, act_in, z, decay, lead, entering, skip, gain, w_out, mixed_ref, low_ref, squares_ref, out_ref):
    heads = decay.shape[1]
    inner = y.shape[2]
    size = entering.shape[0]
    grown = per_channel(jnp.exp(sum_down(decay[...])), inner // heads) * lead[...]
    act = joined(act_in)
    map_c = act[:, inner + size :]
    carried = grown * dot_nn(map_c, entering[...].astype(bf16))
    mixed = joined(y) + carried + skip[...] * act[:, :inner].astype(f32)
    gate = joined(z)
    gated = mixed * (gate * jax.nn.sigmoid(gate))
    mixed_ref[...] = mixed.astype(bf16).reshape(mixed_ref.shape)
    low = (gated * gain[...]).astype(bf16)
    low_ref[...] = low.reshape(low_ref.shape)
    squares = jnp.sum(gated * gated, axis=1, keepdims=True)
    squares_ref[...] = jnp.broadcast_to(squares, (BLOCK, squares_ref.shape[2])).reshape(squares_ref.shape)
    out_ref[...] = dot_nn(low, w_out[...]).astype(bf16).reshape(out_ref.shape)


def gate_back_kernel(push, w_out, mixed_in, z, act_in, decay, lead, slope_in, gain, dy_ref, dz_ref, enter_ref, sums_ref):
    heads = decay.shape[1]
    inner = mixed_in.shape[2]
    size = enter_ref.shape[0]
    mixed = joined(mixed_in).astype(f32)
    act = joined(act_in)
    terms = joined(slope_in).astype(f32)
    slope = terms[:, 0:1] + terms[:, 1:2]
    gate = joined(z)
    sigma = jax.nn.sigmoid(gate)
    silu = gate * sigma
    gated = mixed * silu
    low_grad = dot_nt(joined(push), w_out[...])
    gated_grad = low_grad * gain[...] + 2.0 * gated * slope
    dy = gated_grad * silu
    dy_ref[...] = dy.astype(bf16).reshape(dy_ref.shape)
    dz_ref[...] = (gated_grad * mixed * (sigma + silu * (1.0 - sigma))).astype(bf16).reshape(dz_ref.shape)
    grown = per_channel(jnp.exp(sum_down(decay[...])), inner // heads) * lead[...]
    part = dot_tn(act[:, inner + size :], (grown * dy).astype(bf16))
    gain_sum = jnp.sum(low_grad * gated, axis=0, keepdims=True)
    skip_sum = jnp.sum(dy * act[:, :inner].astype(f32), axis=0, keepdims=True)

    @pl.when(pl.program_id(1) == 0)
    def _():
        enter_ref[...] = jnp.zeros_like(enter_ref)

    @pl.when((pl.program_id(0) == 0) & (pl.program_id(1) == 0))
    def _():
        sums_ref[...] = jnp.zeros_like(sums_ref)

    enter_ref[...] += part
    sums_ref[0:1, :] += gain_sum
    sums_ref[1:2, :] += skip_sum


def scan_back_kernel(cin, cin_before, edge, taps, raw, bias, decay, decay_t, act_in, dy_in, start, lead, entering, leave_grad, skip,
                     in_ref, head_ref, tail_ref, taps_ref, buf, nextp, state_grad):
    heads = decay.shape[1]
    block = BLOCK
    inner = dy_in.shape[2]
    width = taps.shape[1]
    size = state_grad.shape[0]
    head_size = inner // heads
    pair = 2 * head_size
    count = 4
    turn, turns = pl.program_id(1), pl.num_programs(1)

    @pl.when(turn == 0)
    def _():
        state_grad[...] = leave_grad[...]
        nextp[...] = jnp.zeros_like(nextp)

    @pl.when((pl.program_id(0) == 0) & (turn == 0))
    def _():
        taps_ref[...] = jnp.zeros_like(taps_ref)

    buf[8 : 8 + block, :] = joined(cin).astype(f32)

    @pl.when(turn == turns - 1)
    def _():
        buf[0:8, :] = edge[...]

    @pl.when(turn < turns - 1)
    def _():
        buf[0:8, :] = cin_before[...].astype(f32)[8:, :]

    pre = taps[4:5, :] + sum(taps[k : k + 1, :] * buf[5 + k : 5 + k + block, :] for k in range(count))
    sigma = jax.nn.sigmoid(pre)
    slope = sigma * (1.0 + pre * (1.0 - sigma))
    act = joined(act_in)
    map_b, map_c = act[:, inner : inner + size], act[:, inner + size :]
    value = act[:, :inner].astype(f32)
    raw_full = joined(raw) + bias[...]
    step = per_channel(softplus(raw_full), head_size)
    scaled = value * step
    low = scaled.astype(bf16)
    dy_low = joined(dy_in)
    dy = dy_low.astype(f32)
    within, across = sum_down(decay[...]), sum_right(decay_t[...])
    grown = per_channel(jnp.exp(within), head_size)
    tail = per_channel(jnp.exp(within[block - 1 :, :] - within), head_size)
    before = (start[...] + lead[...] * entering[...]).astype(bf16)
    after_grad = state_grad[...]
    after_low = after_grad.astype(bf16)
    grown_dy = (grown * dy).astype(bf16)
    c_grad = dot_nt(grown_dy, before)
    b_grad = dot_nt((tail * scaled).astype(bf16), after_low)
    scaled_grad = tail * dot_nn(map_b, after_low)
    state_grad[...] = grown[block - 1 :, :] * after_grad + dot_tn(map_c, grown_dy)
    scores_t = dot_nt(map_b, map_c)
    causal_t = lower_mask(block, True)
    left = first_half(block, pair)
    zero = jnp.zeros((block, pair), bf16)
    scores_grad_t = jnp.zeros((block, block), f32)
    parts = []
    for h in range(0, heads, 2):
        columns = slice(h * head_size, h * head_size + pair)
        dy_pair, low_pair = dy_low[:, columns], low[:, columns]
        halves = []
        for a in (h, h + 1):
            gap = jnp.where(causal_t, across[a : a + 1, :] - within[:, a : a + 1], -1e30)
            fade = jnp.exp(gap)
            own = jnp.where(left, low_pair, zero) if a == h else jnp.where(left, zero, low_pair)
            scores_grad_t = scores_grad_t + fade * dot_nt(own, dy_pair)
            halves.append(dot_nn((fade * scores_t).astype(bf16), dy_pair))
        parts.append(jnp.where(left, halves[0], halves[1]))
    scaled_grad = scaled_grad + jnp.concatenate(parts, axis=1)
    scores_low = scores_grad_t.astype(bf16)
    b_grad = b_grad + dot_nn(scores_low, map_c)
    c_grad = c_grad + dot_tn(scores_low, map_b)
    x_grad = scaled_grad * step + skip[...] * dy
    lanes = in_ref.shape[2] - width
    rows = lax.broadcasted_iota(jnp.int32, (inner, lanes), 0)
    columns = lax.broadcasted_iota(jnp.int32, (inner, lanes), 1)
    member = ((rows >= columns * head_size) & (rows < (columns + 1) * head_size)).astype(bf16)
    step_grad = dot_nn((scaled_grad * value).astype(bf16), member)
    raw_grad = step_grad[:, :heads] * jax.nn.sigmoid(raw_full)
    taps_ref[5:6, :heads] += jnp.sum(raw_grad, axis=0, keepdims=True)
    raw_grad = jnp.concatenate([raw_grad, jnp.zeros((block, lanes - heads), f32)], axis=1)
    in_ref[:, :, width:] = raw_grad.astype(bf16).reshape(in_ref.shape[:2] + (lanes,))
    pre_grad = jnp.concatenate([x_grad, b_grad, c_grad], axis=1) * slope
    for k in range(count):
        taps_ref[k : k + 1, :] += jnp.sum(pre_grad * buf[5 + k : 5 + k + block, :], axis=0, keepdims=True)
    taps_ref[4:5, :] += jnp.sum(pre_grad, axis=0, keepdims=True)
    buf[0:block, :] = pre_grad
    buf[block : block + 8, :] = nextp[...]
    nextp[...] = buf[0:8, :]
    head_ref[...] = buf[0:8, :]
    in_grad = sum(taps[k : k + 1, :] * buf[3 - k : 3 - k + block, :] for k in range(count))
    in_ref[:, :, :width] = in_grad.astype(bf16).reshape(in_ref.shape[:2] + (width,))

    @pl.when(turn == 0)
    def _():
        tail_ref[...] = in_grad[block - 8 :, :]


def params():
    return pltpu.CompilerParams(vmem_limit_bytes=56 * 2**20)


def cost(flops, moved, powers):
    return pl.CostEstimate(flops=int(flops), bytes_accessed=int(moved), transcendentals=int(powers))


def rows_of(share, width, flip=0):
    per = BLOCK // share
    if flip:
        return pl.BlockSpec((per, None, share, width), lambda b, k: (flip - 1 - k, b, 0, 0))
    return pl.BlockSpec((per, None, share, width), lambda b, k: (k, b, 0, 0))


def each(height, width):
    return pl.BlockSpec((None, height, width), lambda b, k: (b, 0, 0))


def only(height, width):
    return pl.BlockSpec((height, width), lambda b, k: (0, 0))


def at_block(height, width, flip=0):
    if flip:
        return pl.BlockSpec((None, None, height, width), lambda b, k: (b, flip - 1 - k, 0, 0))
    return pl.BlockSpec((None, None, height, width), lambda b, k: (b, k, 0, 0))


def in_order(width, flip=0):
    if flip:
        return pl.BlockSpec((None, BLOCK, width), lambda b, k: (b, flip - 1 - k, 0))
    return pl.BlockSpec((None, BLOCK, width), lambda b, k: (b, k, 0))


def made(*shape, kind=bf16):
    return jax.ShapeDtypeStruct(shape, kind)


def scan_forward(cin, edge, taps, raw, bias, decay, decay_t, inner, size):
    shares, batch, share, width = cin.shape
    heads = raw.shape[3]
    tokens = shares * share
    blocks = tokens // BLOCK
    return pl.pallas_call(
        scan_kernel,
        grid=(batch, blocks),
        in_specs=[
            rows_of(share, width),
            each(8, width),
            only(8, width),
            rows_of(share, heads),
            only(1, heads),
            in_order(heads),
            pl.BlockSpec((None, heads, BLOCK), lambda b, k: (b, 0, k)),
        ],
        out_specs=[rows_of(share, width), rows_of(share, inner), at_block(size, inner), each(size, inner)],
        out_shape=[
            made(shares, batch, share, width),
            made(shares, batch, share, inner, kind=f32),
            made(batch, blocks, size, inner, kind=f32),
            made(batch, size, inner, kind=f32),
        ],
        scratch_shapes=[
            pltpu.VMEM((BLOCK + 8, width), f32),
            pltpu.VMEM((8, width), f32),
            pltpu.VMEM((size, inner), f32),
        ],
        compiler_params=params(),
        cost_estimate=cost(
            batch * tokens * inner * (4 * BLOCK + 4 * size), 10 * batch * tokens * inner, batch * tokens * heads * BLOCK
        ),
    )(cin, edge, taps, raw, bias, decay, decay_t)


def gate_forward(y, act, z, decay, lead, entering, skip, gain, w_out):
    shares, batch, share, inner = y.shape
    width, heads, size = act.shape[3], decay.shape[2], entering.shape[1]
    model = w_out.shape[1]
    tokens = shares * share
    return pl.pallas_call(
        gate_kernel,
        grid=(batch, tokens // BLOCK),
        in_specs=[
            rows_of(share, inner),
            rows_of(share, width),
            rows_of(share, inner),
            in_order(heads),
            at_block(1, inner),
            each(size, inner),
            only(1, inner),
            only(1, inner),
            only(inner, model),
        ],
        out_specs=[rows_of(share, inner), rows_of(share, inner), rows_of(share, 128), rows_of(share, model)],
        out_shape=[
            made(shares, batch, share, inner),
            made(shares, batch, share, inner),
            made(shares, batch, share, 128, kind=f32),
            made(shares, batch, share, model),
        ],
        compiler_params=params(),
        cost_estimate=cost(
            2 * batch * tokens * inner * (model + size), batch * tokens * inner * 18, batch * tokens * inner
        ),
    )(y, act, z, decay, lead, entering, skip, gain, w_out)


def gate_backward(push, w_out, mixed, z, act, decay, lead, gain):
    shares, batch, share, inner = mixed.shape
    width, heads, model = act.shape[3], decay.shape[2], w_out.shape[1]
    size = (width - inner) // 2
    tokens = shares * share
    return pl.pallas_call(
        gate_back_kernel,
        grid=(batch, tokens // BLOCK),
        in_specs=[
            rows_of(share, model),
            only(inner, model),
            rows_of(share, inner),
            rows_of(share, inner),
            rows_of(share, width),
            in_order(heads),
            at_block(1, inner),
            pl.BlockSpec((BLOCK // share, None, share, 128), lambda b, k: (k, b, 0, model // 128)),
            only(1, inner),
        ],
        out_specs=[rows_of(share, inner), rows_of(share, inner), each(size, inner), only(8, inner)],
        out_shape=[
            made(shares, batch, share, inner),
            made(shares, batch, share, inner),
            made(batch, size, inner, kind=f32),
            made(8, inner, kind=f32),
        ],
        compiler_params=params(),
        cost_estimate=cost(
            2 * batch * tokens * inner * (model + size), batch * tokens * inner * 18, batch * tokens * inner
        ),
    )(push, w_out, mixed, z, act, decay, lead, push, gain)


def scan_backward(cin, edge, taps, raw, bias, decay, decay_t, act, dy, start, lead, entering, leave_grad, skip):
    shares, batch, share, width = cin.shape
    heads, inner, size = raw.shape[3], dy.shape[3], entering.shape[1]
    tokens = shares * share
    blocks = tokens // BLOCK
    per = BLOCK // share
    return pl.pallas_call(
        scan_back_kernel,
        grid=(batch, blocks),
        in_specs=[
            rows_of(share, width, blocks),
            pl.BlockSpec(
                (None, None, 16, width),
                lambda b, k: (jnp.maximum((blocks - 1 - k) * per - 1, 0), b, share // 16 - 1, 0),
            ),
            each(8, width),
            only(8, width),
            rows_of(share, heads, blocks),
            only(1, heads),
            in_order(heads, blocks),
            pl.BlockSpec((None, heads, BLOCK), lambda b, k: (b, 0, blocks - 1 - k)),
            rows_of(share, width, blocks),
            rows_of(share, inner, blocks),
            at_block(size, inner, blocks),
            at_block(1, inner, blocks),
            each(size, inner),
            each(size, inner),
            only(1, inner),
        ],
        out_specs=[rows_of(share, width + 128, blocks), each(8, width), each(8, width), only(8, width)],
        out_shape=[
            made(shares, batch, share, width + 128),
            made(batch, 8, width, kind=f32),
            made(batch, 8, width, kind=f32),
            made(8, width, kind=f32),
        ],
        scratch_shapes=[
            pltpu.VMEM((BLOCK + 8, width), f32),
            pltpu.VMEM((8, width), f32),
            pltpu.VMEM((size, inner), f32),
        ],
        compiler_params=params(),
        cost_estimate=cost(
            batch * tokens * inner * (8 * BLOCK + 10 * size), 15 * batch * tokens * inner, batch * tokens * heads * BLOCK
        ),
    )(cin, cin, edge, taps, raw, bias, decay, decay_t, act, dy, start, lead, entering, leave_grad, skip)


def end_rows(in_grad, last, following, taps):
    shares, batch, share, width = in_grad.shape
    columns = last.shape[2]

    def kernel(rows, last_ref, next_ref, taps_ref, out_ref, buf):
        for b in range(batch):
            buf[0:8, :] = jnp.zeros((8, columns), f32)
            buf[8:16, :] = next_ref[b]
            added = sum(taps_ref[k : k + 1, :] * buf[3 - k : 11 - k, :] for k in range(4))
            old = rows[b].astype(f32)
            end = jnp.concatenate([last_ref[b] + added, old[8:, columns:]], axis=1)
            out_ref[b] = jnp.concatenate([old[:8], end], axis=0).astype(bf16)

    block = pl.BlockSpec((None, batch, 16, width), lambda i: (shares - 1, 0, share // 16 - 1, 0))

    def whole(array):
        zeros = (0,) * array.ndim
        return pl.BlockSpec(array.shape, lambda i: zeros)

    return pl.pallas_call(
        kernel,
        grid=(1,),
        in_specs=[block, whole(last), whole(following), whole(taps)],
        out_specs=block,
        out_shape=made(*in_grad.shape),
        input_output_aliases={0: 0},
        scratch_shapes=[pltpu.VMEM((16, columns), f32)],
        compiler_params=params(),
        cost_estimate=cost(16 * width * batch, 200 * width * batch, 0),
    )(in_grad, last, following, taps)


def weight_grads(groups, depth, tile, extra=None):
    rows = groups[0][0][0].shape[0]
    tiles = [group[0][1].shape[1] // tile for group in groups]
    starts = [sum(tiles[:g]) for g in range(len(groups) + 1)]
    terms = max(len(group) for group in groups)
    flat = [array for group in groups for term in group for array in term]
    count = len(flat)

    def kernel(*refs):
        out, turned = refs[-2], refs[-1]
        j = pl.program_id(0)
        place = 0
        for g, group in enumerate(groups):
            mine = refs[place : place + 2 * len(group)]
            place += 2 * len(group)

            @pl.when(j == starts[g])
            def _(mine=mine):
                for t in range(len(mine) // 2):
                    turned[t] = mine[2 * t][...].T

            @pl.when((j >= starts[g]) & (j < starts[g + 1]))
            def _(mine=mine):
                total = sum(dot_nn(turned[t], mine[2 * t + 1][...]) for t in range(len(mine) // 2))
                out[...] = total.astype(bf16)

        if extra is not None:

            @pl.when(j == starts[-1] - 1)
            def _():
                added = refs[count]
                room = tile - added.shape[1]
                out[:, room:] = (out[:, room:].astype(f32) + added[...].astype(f32)).astype(bf16)

    specs = []
    for g, group in enumerate(groups):
        for _ in group:
            specs.append(pl.BlockSpec((rows, depth), lambda j: (0, 0), pipeline_mode=pl.Buffered(1)))
            specs.append(
                pl.BlockSpec((rows, tile), lambda j, a=starts[g], n=tiles[g]: (0, jnp.clip(j - a, 0, n - 1)))
            )
    steps = starts[-1]
    if extra is not None:
        flat = flat + [extra]
        specs.append(pl.BlockSpec(extra.shape, lambda j: (0, 0)))
    return pl.pallas_call(
        kernel,
        grid=(steps,),
        in_specs=specs,
        out_specs=pl.BlockSpec((depth, tile), lambda j: (0, j)),
        out_shape=jax.ShapeDtypeStruct((depth, steps * tile), bf16),
        scratch_shapes=[pltpu.VMEM((terms, depth, rows), bf16)],
        compiler_params=params(),
        cost_estimate=cost(2 * terms * rows * depth * tile * steps, 2 * (count * rows * depth + depth * tile * steps), 0),
    )(*flat)


def gates_of(gates_ref, mine):
    terms = gates_ref[...].astype(f32)
    every = mine.shape[1]
    return terms[:, :every] + terms[:, every : 2 * every]


def expert_forward_kernel(shared, x_ref, grad_ref, gates_ref, mine, w_gu, w_down, *refs):
    out_ref, logit_ref, both_ref = refs[-3:]
    x = x_ref[...]
    gates = gates_of(gates_ref, mine)
    wide = grad_ref[...].astype(f32)
    out = own = total = 0.0
    width = w_down.shape[1]
    for e in range(w_gu.shape[0]):
        weight = jnp.sum(gates * mine[e : e + 1, :], axis=1, keepdims=True)
        both = dot_nn(x, w_gu[e])
        both_ref[:, 2 * e * width : 2 * (e + 1) * width] = both
        gate, up = both[:, :width], both[:, width:]
        act = (gate * jax.nn.sigmoid(gate) * up).astype(bf16)
        result = dot_nn(act, w_down[e]).astype(bf16).astype(f32)
        push = jnp.sum(wide * result, axis=1, keepdims=True)
        own = own + push * mine[e : e + 1, :]
        total = total + weight * push
        out = out + weight * result
    if shared:
        ws_gu, ws_down = refs[:2]
        first, ff = 2 * w_gu.shape[0] * width, ws_down.shape[0]
        gate, up = dot_nn(x, ws_gu[0]), dot_nn(x, ws_gu[1])
        both_ref[:, first : first + ff] = gate
        both_ref[:, first + ff :] = up
        act = (gate * jax.nn.sigmoid(gate) * up).astype(bf16)
        out = out + dot_nn(act, ws_down[...])
    out_ref[...] = out.astype(bf16)
    logit_ref[...] = gates * (own - total)


def expert_backward_kernel(shared, grad_ref, gates_ref, both_ref, mine, w_gu, w_down, *refs):
    grad = grad_ref[...]
    gates = gates_of(gates_ref, mine)
    wide = grad.astype(f32)
    dx_ref, act_ref, gu_ref = refs[2:5] if shared else refs

    def back(gate, up, act_push):
        sigma = jax.nn.sigmoid(gate)
        silu = gate * sigma
        slope = sigma + silu * (1.0 - sigma)
        gu_grad = jnp.concatenate([act_push * up * slope, act_push * silu], axis=1).astype(bf16)
        return (silu * up).astype(bf16), gu_grad

    dx = 0.0
    width = w_down.shape[1]
    for e in range(w_gu.shape[0]):
        weight = jnp.sum(gates * mine[e : e + 1, :], axis=1, keepdims=True)
        act_push = dot_nt((weight * wide).astype(bf16), w_down[e])
        middle = (2 * e + 1) * width
        gate, up = both_ref[:, middle - width : middle], both_ref[:, middle : middle + width]
        act, gu_grad = back(gate, up, act_push)
        act_ref[:, e * width : (e + 1) * width] = (weight * act.astype(f32)).astype(bf16)
        gu_ref[:, middle - width : middle + width] = gu_grad
        dx = dx + dot_nt(gu_grad, w_gu[e]).astype(bf16).astype(f32)
    if shared:
        ws_gu, ws_down = refs[:2]
        s_act_ref, s_gu_ref = refs[5:]
        first, ff = 2 * w_gu.shape[0] * width, ws_down.shape[0]
        gate, up = both_ref[:, first : first + ff], both_ref[:, first + ff :]
        act, gu_grad = back(gate, up, dot_nt(grad, ws_down[...]))
        s_act_ref[...] = act
        s_gu_ref[...] = gu_grad
        dx = dx + dot_nt(gu_grad[:, :ff], ws_gu[0]) + dot_nt(gu_grad[:, ff:], ws_gu[1])
    dx_ref[...] = dx.astype(bf16)


def by_rows(columns, at=0):
    return pl.BlockSpec((ROWS, columns), lambda i: (i, at))


def kept(array):
    zeros = (0,) * array.ndim
    return pl.BlockSpec(array.shape, lambda i: zeros, pipeline_mode=pl.Buffered(1))


def experts_forward(x, grad, mine, w_gu, w_down, shared=()):
    rows = x.shape[0]
    count, model, double = w_gu.shape
    beside = x.shape[1] - model
    every = mine.shape[1]
    hidden = count * double + (2 * shared[1].shape[0] if shared else 0)
    return pl.pallas_call(
        lambda *refs: expert_forward_kernel(bool(shared), *refs),
        grid=(rows // ROWS,),
        in_specs=[by_rows(model), by_rows(model), by_rows(beside, model // beside)]
        + [kept(w) for w in (mine, w_gu, w_down, *shared)],
        out_specs=[by_rows(model), by_rows(every), by_rows(hidden)],
        out_shape=[made(rows, model), made(rows, every, kind=f32), made(rows, hidden, kind=f32)],
        compiler_params=params(),
        cost_estimate=cost(3 * rows * hidden * model, 3 * hidden * model + rows * (6 * model + 4 * hidden), rows * hidden),
    )(x, grad, x, mine, w_gu, w_down, *shared)


def experts_backward(x, grad, both, mine, w_gu, w_down, shared=()):
    rows = x.shape[0]
    count, model, double = w_gu.shape
    beside = x.shape[1] - model
    hidden = both.shape[1]
    widths = [model, count * double // 2, count * double]
    if shared:
        widths += [shared[1].shape[0], 2 * shared[1].shape[0]]
    return pl.pallas_call(
        lambda *refs: expert_backward_kernel(bool(shared), *refs),
        grid=(rows // ROWS,),
        in_specs=[by_rows(model), by_rows(beside, model // beside), by_rows(hidden)]
        + [kept(w) for w in (mine, w_gu, w_down, *shared)],
        out_specs=[by_rows(w) for w in widths],
        out_shape=[made(rows, w) for w in widths],
        compiler_params=params(),
        cost_estimate=cost(3 * rows * hidden * model, 3 * hidden * model + rows * (4 * model + 7 * hidden), rows * hidden),
    )(grad, x, both, mine, w_gu, w_down, *shared)


def summed(got):
    return sum(got[i].astype(f32) for i in range(got.shape[0]))


def two_terms(values, width):
    high = values.astype(bf16)
    low = (values - high.astype(f32)).astype(bf16)
    terms, room = [high, low], width - 2 * values.shape[1]
    if room:
        terms.append(jnp.zeros((values.shape[0], room), bf16))
    return jnp.concatenate(terms, axis=1)


def after_mix_kernel(inner, got, x, squares, used, gain, router, packed_ref, hidden_ref, mix_ref, scale_ref):
    model = x.shape[1]
    mix = summed(got)
    gate_scale = lax.rsqrt(squares[...] / inner + norm_eps)
    hidden = x[...].astype(f32) + mix * gate_scale
    scale = lax.rsqrt(jnp.mean(hidden * hidden, axis=1, keepdims=True) + norm_eps)
    normed = (hidden * scale * gain[...]).astype(bf16)
    mask = used[...] > 0.0
    logits = jnp.where(mask, dot_nn(normed, router[...]), -1e30)
    powers = jnp.where(mask, jnp.exp(logits - jnp.max(logits, axis=1, keepdims=True)), 0.0)
    gates = powers / jnp.sum(powers, axis=1, keepdims=True)
    packed_ref[:, :model] = normed
    packed_ref[:, model:] = two_terms(gates, packed_ref.shape[1] - model)
    hidden_ref[...] = hidden
    mix_ref[...] = mix
    lane = lax.broadcasted_iota(jnp.int32, scale_ref.shape, 1)
    scale_ref[...] = jnp.where(lane == 0, gate_scale, scale)


def after_ffn_kernel(inner, got, hidden_in, mix, scales, grad, gain, packed_ref, grad_ref, sum_ref):
    model = grad.shape[1]
    dx, hidden = summed(got), hidden_in[...]
    gate_scale, scale = scales[:, 0:1], scales[:, 1:2]
    gained = dx * gain[...]
    mean = jnp.mean(gained * hidden, axis=1, keepdims=True)
    hidden_grad = grad[...].astype(f32) + scale * (gained - hidden * (scale * scale * mean))
    grad_ref[...] = hidden_grad
    push = jnp.sum(hidden_grad * mix[...], axis=1, keepdims=True)
    slope = (-0.5 / inner) * push * gate_scale * gate_scale * gate_scale
    packed_ref[:, :model] = (hidden_grad * gate_scale).astype(bf16)
    packed_ref[:, model:] = two_terms(slope, packed_ref.shape[1] - model)

    @pl.when(pl.program_id(0) == 0)
    def _():
        sum_ref[...] = jnp.zeros_like(sum_ref)

    sum_ref[0:1, :] += jnp.sum(dx * hidden * scale, axis=0, keepdims=True)


def after_proj_kernel(got, x_in, hidden_grad, gain, out_ref):
    dn, x = summed(got), x_in[...].astype(f32)
    scale = lax.rsqrt(jnp.mean(x * x, axis=1, keepdims=True) + norm_eps)
    gained = dn * gain[...]
    mean = jnp.mean(gained * x, axis=1, keepdims=True)
    out_ref[...] = (hidden_grad[...] + scale * (gained - x * (scale * scale * mean))).astype(bf16)


def on_share(kernel, got, rows, wholes, outs, sums=()):
    shares, batch, share, model = got.shape

    def rows_at(width):
        return pl.BlockSpec((None, share, width), lambda b: (b, 0, 0))

    def kept_at(shape):
        return pl.BlockSpec(shape, lambda b: (0, 0))

    return pl.pallas_call(
        kernel,
        grid=(batch,),
        in_specs=[pl.BlockSpec((shares, None, share, model), lambda b: (0, b, 0, 0))]
        + [rows_at(r.shape[2]) for r in rows]
        + [kept_at(w.shape) for w in wholes],
        out_specs=[rows_at(width) for width, _ in outs] + [kept_at(shape) for shape in sums],
        out_shape=[made(batch, share, width, kind=kind) for width, kind in outs]
        + [made(*shape, kind=f32) for shape in sums],
        compiler_params=params(),
        cost_estimate=cost(40 * batch * share * model, 30 * batch * share * model, batch * share),
    )(got, *rows, *wholes)


def shifted(array, axis, by):
    count = lax.axis_size(axis)
    pairs = [(i, i + by) for i in range(count) if 0 <= i + by < count]
    return lax.ppermute(array, axis, pairs)


def prefix(part, axis, combine, identity):
    place = lax.axis_index(axis)
    gathered = jax.tree.map(lambda a: lax.all_gather(a, axis), part)
    state = jax.tree.map(lambda a, e: jnp.zeros_like(a) + jnp.asarray(e, a.dtype), part, identity)

    def one(lap, state):
        return combine(
            state, jax.tree.map(lambda a: lax.dynamic_index_in_dim(a, lap, 0, False), gathered)
        )

    return lax.fori_loop(0, place, one, state)


def prefix_2(array, axis, combine, identity):
    count, place = (lax.axis_size(axis), lax.axis_index(axis))
    everything = jax.tree.map(
        lambda part, kind: lax.all_gather(part.astype(kind), axis),
        array,
        jax.tree.map(lambda a: jnp.bfloat16 if a.dtype == jnp.float32 else a.dtype, array),
    )
    start = jax.tree.map(
        lambda part, zero: jnp.broadcast_to(jnp.asarray(zero, part.dtype), part.shape),
        array,
        identity,
    )

    def lap(k, before):
        at = count - 1 - k
        reached = at > place
        new = combine(
            before, jax.tree.map(lambda part, own: part[at].astype(own.dtype), everything, array)
        )
        return jax.tree.map(lambda a, b: jnp.where(reached, a, b), new, before)

    return lax.fori_loop(0, count, lap, start)


def swap_shares(part):
    return lax.all_to_all(part, "head", split_axis=0, concat_axis=0, tiled=True)


def gather_shares(share):
    copies = jnp.broadcast_to(share[None], (lax.axis_size("head"),) + share.shape)
    return lax.all_to_all(copies, "head", split_axis=0, concat_axis=0, tiled=True)


def relay(part, *beside):
    count, place = lax.axis_size("head"), lax.axis_index("head")

    def passed(array, by, start=0):
        pairs = [(i, i + by) for i in range(count) if 0 <= i + by < count]
        pairs = [(i, j) for i, j in pairs if 0 <= i - start * by < count]
        return lax.ppermute(array, "head", pairs)

    if count == 4:
        up, down = passed(part, 1), passed(part, -1)
        far = lax.ppermute(part, "head", [(0, 3), (3, 0)])
        up_two, down_two = passed(up, 1, 1), passed(down, -1, 1)
        if beside:
            far, *beside = tie(far, *beside)
        pieces = [
            part,
            jnp.where(place >= 1, up, far),
            jnp.where(place >= 2, up_two, down_two),
            jnp.where(place >= 3, far, down),
        ]
        return (pieces, *beside) if beside else pieces
    up, down = [part], [part]
    for _ in range(count - 1):
        up.append(passed(up[-1], 1))
        down.append(passed(down[-1], -1))
    pieces = [part] + [jnp.where(place >= d, up[d], down[count - d]) for d in range(1, count)]
    return (pieces, *beside) if beside else pieces


def laid(pieces, axis=0):
    count, place = lax.axis_size("head"), lax.axis_index("head")
    shape = pieces[0].shape[:axis] + (count,) + pieces[0].shape[axis:]
    out = jnp.zeros(shape, pieces[0].dtype)
    for d, piece in enumerate(pieces):
        out = lax.dynamic_update_index_in_dim(out, piece, (place + count - d) % count, axis)
    return out


def relay_shares(share, axis=0):
    return laid(relay(share), axis)


def bits_of(axis):
    count = lax.axis_size(axis)
    return [(1 << k) for k in range(count.bit_length() - 1)]


def across(array, axis, bit):
    return lax.ppermute(array, axis, [(i, i ^ bit) for i in range(lax.axis_size(axis))])


def add_over(array, *axes):
    for axis in axes:
        for bit in bits_of(axis):
            array = array + across(array, axis, bit)
    return array


def join_over(array, dimension, *axes):
    for axis in axes:
        place = lax.axis_index(axis)
        for bit in bits_of(axis):
            other = across(array, axis, bit)
            array = jnp.where(
                (place & bit) == 0,
                jnp.concatenate([array, other], axis=dimension),
                jnp.concatenate([other, array], axis=dimension),
            )
    return array


def tie(*arrays):
    return lax.optimization_barrier(arrays)


def around(array, by):
    count = lax.axis_size("seq")
    if by % count == 0:
        return array
    return lax.ppermute(array, "seq", [(i, (i + by) % count) for i in range(count)])


def spread_last(local_part, rank_index, part_count):
    local_width = local_part.shape[-1]
    full_array = jnp.zeros(local_part.shape[:-1] + (local_width * part_count,), jnp.float32)
    return lax.dynamic_update_slice_in_dim(
        full_array, local_part, rank_index * local_width, local_part.ndim - 1
    )


def chain_forward(earlier, later):
    return (earlier[0] * later[0], later[0] * earlier[1] + later[1])


def chain_backward(earlier, later):
    return (earlier[0] * later[0], later[1] + later[0] * earlier[1])


def local(
    x_in,
    d_out,
    log_decay,
    routes,
    norm1_gain,
    w_in_zx,
    w_in_bc,
    w_in_dt,
    dt_bias,
    conv_x,
    conv_x_bias,
    conv_bc,
    conv_bc_bias,
    skip_d,
    gate_norm_gain,
    w_out,
    norm2_gain,
    router,
    w_expert_gu,
    w_expert_down,
    w_shared_gu,
    w_shared_down,
):
    batch_size, tokens, model_width = x_in.shape
    inner_dev = w_in_zx.shape[2]
    heads_dev = w_in_dt.shape[1]
    head_size = inner_dev // heads_dev
    state_size = w_in_bc.shape[1] // 2
    conv_taps = conv_x.shape[0]
    experts_dev = w_expert_gu.shape[0]
    head_count = lax.axis_size("head")
    seq_count = lax.axis_size("seq")
    head_rank = lax.axis_index("head")
    seq_rank = lax.axis_index("seq")
    inner_all = inner_dev * head_count
    experts_all = experts_dev * seq_count * head_count
    share_rows = tokens // head_count
    rows_all = batch_size * tokens
    conv_width = inner_dev + 2 * state_size

    def by_share(array):
        array = array.reshape((batch_size, head_count, share_rows) + array.shape[2:])
        return jnp.swapaxes(array, 0, 1)

    def by_position(array):
        return jnp.swapaxes(array, 0, 1).reshape(batch_size, tokens, array.shape[-1])

    def own_share(array):
        return lax.dynamic_index_in_dim(array, head_rank, 0, keepdims=False)

    def flat(array):
        return array.reshape(-1, array.shape[-1])

    def times(a, b):
        return lax.dot_general(a, b, (((a.ndim - 1,), (0,)), ((), ())), preferred_element_type=f32)

    def times_t(a, b):
        return lax.dot_general(a, b, (((a.ndim - 1,), (1,)), ((), ())), preferred_element_type=f32)

    def scattered(array, axes):
        return lax.psum_scatter(array, axes, scatter_dimension=0, tiled=True)

    x_rows, grad_rows = by_share(x_in), by_share(d_out)
    grads_in = [flat(around(grad_rows, k)) for k in range(seq_count)]
    input_wide = x_rows.astype(f32)
    scale_one = lax.rsqrt(jnp.mean(input_wide * input_wide, axis=-1, keepdims=True) + norm_eps)
    normed_one = (input_wide * scale_one * norm1_gain).astype(bf16)
    w_conv = jnp.concatenate([w_in_zx[1], w_in_bc], axis=-1)
    w_step = jnp.pad(w_in_dt, ((0, 0), (0, 128 - heads_dev)))
    w_late = jnp.concatenate([w_conv, w_step], axis=-1)
    conv_in = times(normed_one, w_conv).astype(bf16)
    step_raw = times(normed_one, w_step)[..., :heads_dev]
    gate_z = times(normed_one, w_in_zx[0])
    edge_rows = shifted(conv_in[head_count - 1, :, share_rows - 8 :].astype(f32), "seq", 1)
    edge_rows, gate_z = tie(edge_rows, gate_z)
    taps = jnp.concatenate([conv_x, conv_bc], axis=1)
    bias = jnp.concatenate([conv_x_bias, conv_bc_bias])
    taps_bias = jnp.concatenate([taps, bias[None], jnp.zeros((7 - conv_taps, conv_width), f32)])
    decay_across = jnp.transpose(log_decay, (0, 2, 1))
    step_bias = dt_bias[None]
    totals = jnp.sum(log_decay.reshape(batch_size, -1, BLOCK, heads_dev), axis=2)
    before = [jnp.zeros_like(totals[:, 0])]
    for k in range(totals.shape[1]):
        before.append(before[-1] + totals[:, k])
    lead = jnp.repeat(jnp.exp(jnp.stack(before, axis=1)), head_size, axis=-1)
    device_decay, lead = lead[:, -1:], lead[:, :-1, None]
    skip = jnp.repeat(skip_d, head_size)[None]
    gate_gain = gate_norm_gain[None]

    conv_act, scanned, starts, leaving = scan_forward(
        conv_in, edge_rows, taps_bias, step_raw, step_bias, log_decay, decay_across, inner_dev, state_size
    )
    identity = (jnp.ones_like(device_decay), jnp.zeros_like(leaving))
    if seq_count == 2:
        entering = shifted(leaving, "seq", 1)
    else:
        _, entering = prefix((device_decay, leaving), "seq", chain_forward, identity)
    mixed, gated_low, squares, partial_out = gate_forward(
        scanned, conv_act, gate_z, log_decay, lead, entering, skip, gate_gain, w_out
    )

    got_mix, *grads_in = tie(swap_shares(partial_out), *grads_in)
    squares = own_share(add_over(squares[..., 0], "head"))
    expert_ids = jnp.arange(experts_all, dtype=jnp.int32)
    used = jnp.any(own_share(by_share(routes))[..., None] == expert_ids, axis=2).astype(f32)
    x_share, grad_share = own_share(x_rows), own_share(grad_rows)
    beside = -(-2 * experts_all // 128) * 128
    normed_share, hidden, mix_out, scales = on_share(
        lambda *refs: after_mix_kernel(inner_all, *refs),
        got_mix,
        [x_share, squares[..., None], used],
        [norm2_gain[None], router],
        [(model_width + beside, bf16), (model_width, f32), (model_width, f32), (128, f32)],
    )
    pieces = relay(normed_share)
    rows_in = [flat(laid([around(piece, k) for piece in pieces])) for k in range(seq_count)]

    first = (seq_rank * head_count + head_rank) * experts_dev
    mine = (jnp.arange(8)[:, None] + first == expert_ids) & (jnp.arange(8)[:, None] < experts_dev)
    mine = mine.astype(f32)
    turns = [*range(1, seq_count), 0]
    ffn_out, ffn_dx, logit_grad, before_act = [], [], [], []
    for k in turns:
        shared = (w_shared_gu, w_shared_down) if k == 0 else ()
        out, logit, both = experts_forward(rows_in[k], grads_in[k], mine, w_expert_gu, w_expert_down, shared)
        ffn_out.append(around(out, -k))
        logit_grad.append(around(logit, -k))
        before_act.append(both)
    ffn_low = sum(f.astype(f32) for f in ffn_out).astype(bf16)
    ffn_low = ffn_low.reshape(head_count, batch_size, share_rows, model_width)
    ffn_low, before_act[-1] = tie(ffn_low, before_act[-1])
    got_out = swap_shares(ffn_low)
    up_terms, down_terms = [], []
    for k, both in zip(turns, before_act):
        shared = (w_shared_gu, w_shared_down) if k == 0 else ()
        made_k = experts_backward(rows_in[k], grads_in[k], both, mine, w_expert_gu, w_expert_down, shared)
        ffn_dx.append(around(made_k[0], -k))
        down_terms.append((grads_in[k], made_k[1]))
        up_terms.append((rows_in[k], made_k[2]))
    shared_terms = [[(rows_in[0], made_k[4])], [(grads_in[0], made_k[3])]]
    logit_grad = sum(logit_grad).astype(bf16)
    ffn_dx = sum(d.astype(f32) for d in ffn_dx) + times_t(logit_grad, router)
    ffn_dx = ffn_dx.astype(bf16).reshape(ffn_low.shape)
    ffn_dx, *gu_grads = tie(ffn_dx, *[term[1] for term in up_terms])
    up_terms = [(term[0], gu_grad) for term, gu_grad in zip(up_terms, gu_grads)]
    ffn_dx, got_out = tie(ffn_dx, got_out)
    got_dx = swap_shares(ffn_dx)
    expert_grads = [
        weight_grads([up_terms[k : k + 2], down_terms[k : k + 2]], model_width, 512)
        for k in range(0, seq_count, 2)
    ]
    if len(expert_grads) > 1:
        expert_grads = [sum(g.astype(f32) for g in expert_grads).astype(bf16)]
    got_dx, expert_grads, logit_grad = tie(got_dx, expert_grads[0], logit_grad)
    expert_sum = scattered(expert_grads, "dp")
    grad_router = lax.dot_general(
        logit_grad, rows_in[0], (((0,), (0,)), ((), ())), preferred_element_type=f32
    )[:, :model_width]
    push_share, hidden_grad, norm_two_sums = on_share(
        lambda *refs: after_ffn_kernel(inner_all, *refs),
        got_dx,
        [hidden, mix_out, scales, grad_share],
        [norm2_gain[None]],
        [(model_width + 128, bf16), (model_width, f32)],
        [(8, model_width)],
    )
    out_push = relay_shares(push_share)

    layer_share, out_push = tie((hidden + summed(got_out)).astype(bf16), out_push)
    layer_out = gather_shares(layer_share)

    mixed_grad, z_grad, entering_grad, channel_sums = gate_backward(
        out_push, w_out, mixed, gate_z, conv_act, log_decay, lead, gate_gain
    )
    if seq_count == 2:
        leaving_grad = shifted(entering_grad.astype(bf16), "seq", -1).astype(f32)
    else:
        _, leaving_grad = prefix_2((device_decay, entering_grad), "seq", chain_backward, identity)
    in_grad, first_rows, last_rows, tap_sums = scan_backward(
        conv_in,
        edge_rows,
        taps_bias,
        step_raw,
        step_bias,
        log_decay,
        decay_across,
        conv_act,
        mixed_grad,
        starts,
        lead,
        entering,
        leaving_grad,
        skip,
    )
    early_dx = times_t(z_grad, w_in_zx[0])
    in_grad, layer_out, early_dx, expert_sum = tie(in_grad, layer_out, early_dx, expert_sum)
    in_grad = end_rows(in_grad, last_rows, shifted(first_rows, "seq", -1), taps_bias)
    normed_one_grad = early_dx + times_t(in_grad, w_late)
    grad_norm_one = jnp.sum(normed_one_grad * input_wide * scale_one, axis=(0, 1, 2))
    normed_one_grad = normed_one_grad.astype(bf16)
    normed_one_grad, in_grad = tie(normed_one_grad, in_grad)
    got_dn = swap_shares(normed_one_grad)

    def whole(array):
        return spread_last(array, head_rank, head_count).reshape(-1)

    small = [
        norm_two_sums[0],
        grad_router.reshape(-1),
        whole(tap_sums[:conv_taps, :inner_dev]),
        whole(tap_sums[conv_taps, :inner_dev]),
        whole(channel_sums[0]),
        grad_norm_one,
        tap_sums[:conv_taps, inner_dev:].reshape(-1),
        tap_sums[conv_taps, inner_dev:],
        whole(tap_sums[conv_taps + 1, :heads_dev]),
        whole(jnp.sum(channel_sums[1].reshape(heads_dev, head_size), axis=-1)),
    ]
    sizes = [a.shape[0] for a in small]
    skipped = 16 * model_width
    small = [jnp.zeros((skipped,), f32)] + small
    small = jnp.concatenate(small + [jnp.zeros((128 * model_width - skipped - sum(sizes),), f32)])
    small = small.reshape(128, model_width).T.astype(bf16)
    grad_late = weight_grads([[(flat(normed_one), flat(in_grad))]], model_width, 384, small)
    early_terms = [[(flat(out_push), flat(gated_low))], [(flat(normed_one), flat(z_grad))]]
    grad_early = weight_grads(early_terms + shared_terms, model_width, 256)
    late_sum = scattered(grad_late, ("dp", "seq"))
    late_sum, got_dn = tie(late_sum, got_dn)
    input_grad = on_share(
        after_proj_kernel, got_dn, [x_share, hidden_grad], [norm1_gain[None]], [(model_width, bf16)]
    )[0]
    merged = late_sum[:, inner_dev:]
    for bit in bits_of("head"):
        merged = merged.astype(bf16)
        merged = merged.astype(f32) + across(merged, "head", bit).astype(f32)
    merged = merged.astype(bf16)
    input_grad, merged = tie(input_grad, merged)
    late_sum, grad_early = tie(late_sum, grad_early)
    early_sum = scattered(grad_early, ("dp", "seq")).astype(f32)
    pieces, merged, layer_out, late_sum, expert_sum = relay(
        input_grad, merged, layer_out, late_sum, expert_sum
    )
    late_sum = late_sum.astype(f32)
    merged = join_over(merged[None], 0, "dp", "seq")
    merged = jnp.swapaxes(merged.reshape((seq_count, -1) + merged.shape[1:]), 0, 1)
    merged = merged.reshape(model_width, -1).astype(f32)
    layer_out = by_position(layer_out)
    d_input = laid(pieces, 1).reshape(batch_size, tokens, model_width)

    grad_bc = merged[:, : 2 * state_size]
    small = merged[:, 2 * state_size + 16 :].T.reshape(-1)
    ends = [sum(sizes[:k]) for k in range(len(sizes) + 1)]
    small = [small[ends[k] : ends[k + 1]] for k in range(len(sizes))]
    expert_sum = expert_sum.astype(f32)
    double = w_expert_gu.shape[2]
    grad_gu = [expert_sum[:, e * double : (e + 1) * double] for e in range(experts_dev)]
    expert_sum = expert_sum[:, experts_dev * double :]
    width = double // 2
    grad_down = [expert_sum[:, e * width : (e + 1) * width].T for e in range(experts_dev)]
    shared_sum = early_sum[:, 2 * inner_dev :]
    ff_dev = w_shared_down.shape[0]
    return (
        layer_out,
        d_input,
        small[5],
        jnp.stack([early_sum[:, inner_dev : 2 * inner_dev], late_sum[:, :inner_dev]]),
        grad_bc,
        late_sum[:, conv_width : conv_width + heads_dev],
        small[8],
        small[2].reshape(conv_taps, inner_all),
        small[3],
        small[6].reshape(conv_taps, 2 * state_size),
        small[7],
        small[9],
        small[4],
        early_sum[:, :inner_dev].T,
        small[0],
        small[1].reshape(experts_all, model_width).T,
        jnp.stack(grad_gu),
        jnp.stack(grad_down),
        jnp.stack([shared_sum[:, :ff_dev], shared_sum[:, ff_dev : 2 * ff_dev]]),
        shared_sum[:, 2 * ff_dev :].T,
    )


def solution(mesh):
    placed = (
        P("dp", "seq", None),
        P("dp", "seq", None),
        P("dp", "seq", "head"),
        P("dp", "seq", None),
        P(),
        P(None, None, "head"),
        P(),
        P(None, "head"),
        P("head"),
        P(None, "head"),
        P("head"),
        P(),
        P(),
        P("head"),
        P("head"),
        P("head", None),
        P(),
        P(),
        P(("seq", "head"), None, None),
        P(("seq", "head"), None, None),
        P(None, None, "head"),
        P("head", None),
    )
    return jax.shard_map(
        local,
        mesh=mesh,
        in_specs=placed,
        out_specs=(
            P("dp", "seq", None),
            P("dp", "seq", None),
            P(),
            P(None, ("dp", "seq"), "head"),
            P(),
            P(("dp", "seq"), "head"),
            P(),
            P(),
            P(),
            P(),
            P(),
            P(),
            P(),
            P("head", ("dp", "seq")),
            P(),
            P(),
            P(("seq", "head"), "dp", None),
            P(("seq", "head"), None, "dp"),
            P(None, ("dp", "seq"), "head"),
            P("head", ("dp", "seq")),
        ),
        check_vma=False,
    )
```

```python
import jax
import jax.numpy as jnp
from jax import lax
from jax.experimental import pallas as pl
from jax.experimental.pallas import tpu as pltpu
from jax.sharding import PartitionSpec as P

BLOCK = 256
ROWS = 256

bf16, f32 = jnp.bfloat16, jnp.float32
norm_eps = 1e-05
highest = lax.Precision.HIGHEST


def dot_nn(a, b):
    return lax.dot_general(a, b, (((1,), (0,)), ((), ())), preferred_element_type=f32)


def dot_nt(a, b):
    return lax.dot_general(a, b, (((1,), (1,)), ((), ())), preferred_element_type=f32)


def dot_tn(a, b):
    return lax.dot_general(a, b, (((0,), (0,)), ((), ())), preferred_element_type=f32)


def lower_mask(count, flip=False):
    rows = lax.broadcasted_iota(jnp.int32, (count, count), 0)
    columns = lax.broadcasted_iota(jnp.int32, (count, count), 1)
    return columns >= rows if flip else rows >= columns


def sum_down(values):
    lower = lower_mask(values.shape[0]).astype(f32)
    return jnp.dot(lower, values, precision=highest, preferred_element_type=f32)


def sum_right(values):
    upper = lower_mask(values.shape[1], True).astype(f32)
    return jnp.dot(values, upper, precision=highest, preferred_element_type=f32)


def first_half(rows, width=128):
    return lax.broadcasted_iota(jnp.int32, (rows, width), 1) < width // 2


def per_channel(values, head_size):
    rows, heads = values.shape
    left = first_half(rows, 2 * head_size)
    return jnp.concatenate(
        [jnp.where(left, values[:, h : h + 1], values[:, h + 1 : h + 2]) for h in range(0, heads, 2)],
        axis=1,
    )


def joined(ref):
    return ref[...].reshape(-1, ref.shape[-1])


def softplus(v):
    return jnp.maximum(v, 0.0) + jnp.log1p(jnp.exp(-jnp.abs(v)))


def scan_kernel(cin, edge, taps, raw, bias, decay, decay_t, act_ref, y_ref, start_ref, leave_ref, buf, prev, state):
    heads = decay.shape[1]
    block = BLOCK
    inner = y_ref.shape[2]
    size = state.shape[0]
    head_size = inner // heads
    pair = 2 * head_size
    count = 4

    @pl.when(pl.program_id(1) == 0)
    def _():
        prev[...] = edge[...]
        state[...] = jnp.zeros_like(state)

    buf[0:8, :] = prev[...]
    buf[8 : 8 + block, :] = joined(cin).astype(f32)
    pre = taps[4:5, :] + sum(taps[k : k + 1, :] * buf[5 + k : 5 + k + block, :] for k in range(count))
    prev[...] = buf[block : block + 8, :]
    act = (pre * jax.nn.sigmoid(pre)).astype(bf16)
    act_ref[...] = act.reshape(act_ref.shape)
    map_b, map_c = act[:, inner : inner + size], act[:, inner + size :]
    step = softplus(joined(raw) + bias[...])
    scaled = act[:, :inner].astype(f32) * per_channel(step, head_size)
    within, across = sum_down(decay[...]), sum_right(decay_t[...])
    grown = per_channel(jnp.exp(within), head_size)
    tail = per_channel(jnp.exp(within[block - 1 :, :] - within), head_size)
    before = state[...]
    start_ref[...] = before
    carried = grown * dot_nn(map_c, before.astype(bf16))
    scores = dot_nt(map_c, map_b)
    causal = lower_mask(block)
    low = scaled.astype(bf16)
    left = first_half(block, pair)
    for h in range(0, heads, 2):
        columns = slice(h * head_size, h * head_size + pair)
        halves = []
        for a in (h, h + 1):
            gap = jnp.where(causal, within[:, a : a + 1] - across[a : a + 1, :], -1e30)
            halves.append(dot_nn((jnp.exp(gap) * scores).astype(bf16), low[:, columns]))
        y_pair = carried[:, columns] + jnp.where(left, halves[0], halves[1])
        y_ref[:, :, columns] = y_pair.reshape(y_ref.shape[:2] + (pair,))
    after = grown[block - 1 :, :] * before + dot_tn(map_b, (scaled * tail).astype(bf16))
    state[...] = after
    leave_ref[...] = after


def gate_kernel(y, act_in, z, decay, lead, entering, skip, gain, w_out, mixed_ref, low_ref, squares_ref, out_ref):
    heads = decay.shape[1]
    inner = y.shape[2]
    size = entering.shape[0]
    grown = per_channel(jnp.exp(sum_down(decay[...])), inner // heads) * lead[...]
    act = joined(act_in)
    map_c = act[:, inner + size :]
    carried = grown * dot_nn(map_c, entering[...].astype(bf16))
    mixed = joined(y) + carried + skip[...] * act[:, :inner].astype(f32)
    gate = joined(z)
    gated = mixed * (gate * jax.nn.sigmoid(gate))
    mixed_ref[...] = mixed.astype(bf16).reshape(mixed_ref.shape)
    low = (gated * gain[...]).astype(bf16)
    low_ref[...] = low.reshape(low_ref.shape)
    squares = jnp.sum(gated * gated, axis=1, keepdims=True)
    squares_ref[...] = jnp.broadcast_to(squares, (BLOCK, squares_ref.shape[2])).reshape(squares_ref.shape)
    out_ref[...] = dot_nn(low, w_out[...]).astype(bf16).reshape(out_ref.shape)


def gate_back_kernel(push, w_out, mixed_in, z, act_in, decay, lead, slope_in, gain, dy_ref, dz_ref, enter_ref, sums_ref):
    heads = decay.shape[1]
    inner = mixed_in.shape[2]
    size = enter_ref.shape[0]
    mixed = joined(mixed_in).astype(f32)
    act = joined(act_in)
    terms = joined(slope_in).astype(f32)
    slope = terms[:, 0:1] + terms[:, 1:2]
    gate = joined(z)
    sigma = jax.nn.sigmoid(gate)
    silu = gate * sigma
    gated = mixed * silu
    low_grad = dot_nt(joined(push), w_out[...])
    gated_grad = low_grad * gain[...] + 2.0 * gated * slope
    dy = gated_grad * silu
    dy_ref[...] = dy.astype(bf16).reshape(dy_ref.shape)
    dz_ref[...] = (gated_grad * mixed * (sigma + silu * (1.0 - sigma))).astype(bf16).reshape(dz_ref.shape)
    grown = per_channel(jnp.exp(sum_down(decay[...])), inner // heads) * lead[...]
    part = dot_tn(act[:, inner + size :], (grown * dy).astype(bf16))
    gain_sum = jnp.sum(low_grad * gated, axis=0, keepdims=True)
    skip_sum = jnp.sum(dy * act[:, :inner].astype(f32), axis=0, keepdims=True)

    @pl.when(pl.program_id(1) == 0)
    def _():
        enter_ref[...] = jnp.zeros_like(enter_ref)

    @pl.when((pl.program_id(0) == 0) & (pl.program_id(1) == 0))
    def _():
        sums_ref[...] = jnp.zeros_like(sums_ref)

    enter_ref[...] += part
    sums_ref[0:1, :] += gain_sum
    sums_ref[1:2, :] += skip_sum


def scan_back_kernel(cin, cin_before, edge, taps, raw, bias, decay, decay_t, act_in, dy_in, start, lead, entering, leave_grad, skip,
                     in_ref, head_ref, tail_ref, taps_ref, buf, nextp, state_grad):
    heads = decay.shape[1]
    block = BLOCK
    inner = dy_in.shape[2]
    width = taps.shape[1]
    size = state_grad.shape[0]
    head_size = inner // heads
    pair = 2 * head_size
    count = 4
    turn, turns = pl.program_id(1), pl.num_programs(1)

    @pl.when(turn == 0)
    def _():
        state_grad[...] = leave_grad[...]
        nextp[...] = jnp.zeros_like(nextp)

    @pl.when((pl.program_id(0) == 0) & (turn == 0))
    def _():
        taps_ref[...] = jnp.zeros_like(taps_ref)

    buf[8 : 8 + block, :] = joined(cin).astype(f32)

    @pl.when(turn == turns - 1)
    def _():
        buf[0:8, :] = edge[...]

    @pl.when(turn < turns - 1)
    def _():
        buf[0:8, :] = cin_before[...].astype(f32)[8:, :]

    pre = taps[4:5, :] + sum(taps[k : k + 1, :] * buf[5 + k : 5 + k + block, :] for k in range(count))
    sigma = jax.nn.sigmoid(pre)
    slope = sigma * (1.0 + pre * (1.0 - sigma))
    act = joined(act_in)
    map_b, map_c = act[:, inner : inner + size], act[:, inner + size :]
    value = act[:, :inner].astype(f32)
    raw_full = joined(raw) + bias[...]
    step = per_channel(softplus(raw_full), head_size)
    scaled = value * step
    low = scaled.astype(bf16)
    dy_low = joined(dy_in)
    dy = dy_low.astype(f32)
    within, across = sum_down(decay[...]), sum_right(decay_t[...])
    grown = per_channel(jnp.exp(within), head_size)
    tail = per_channel(jnp.exp(within[block - 1 :, :] - within), head_size)
    before = (start[...] + lead[...] * entering[...]).astype(bf16)
    after_grad = state_grad[...]
    after_low = after_grad.astype(bf16)
    grown_dy = (grown * dy).astype(bf16)
    c_grad = dot_nt(grown_dy, before)
    b_grad = dot_nt((tail * scaled).astype(bf16), after_low)
    scaled_grad = tail * dot_nn(map_b, after_low)
    state_grad[...] = grown[block - 1 :, :] * after_grad + dot_tn(map_c, grown_dy)
    scores_t = dot_nt(map_b, map_c)
    causal_t = lower_mask(block, True)
    left = first_half(block, pair)
    zero = jnp.zeros((block, pair), bf16)
    scores_grad_t = jnp.zeros((block, block), f32)
    parts = []
    for h in range(0, heads, 2):
        columns = slice(h * head_size, h * head_size + pair)
        dy_pair, low_pair = dy_low[:, columns], low[:, columns]
        halves = []
        for a in (h, h + 1):
            gap = jnp.where(causal_t, across[a : a + 1, :] - within[:, a : a + 1], -1e30)
            fade = jnp.exp(gap)
            own = jnp.where(left, low_pair, zero) if a == h else jnp.where(left, zero, low_pair)
            scores_grad_t = scores_grad_t + fade * dot_nt(own, dy_pair)
            halves.append(dot_nn((fade * scores_t).astype(bf16), dy_pair))
        parts.append(jnp.where(left, halves[0], halves[1]))
    scaled_grad = scaled_grad + jnp.concatenate(parts, axis=1)
    scores_low = scores_grad_t.astype(bf16)
    b_grad = b_grad + dot_nn(scores_low, map_c)
    c_grad = c_grad + dot_tn(scores_low, map_b)
    x_grad = scaled_grad * step + skip[...] * dy
    lanes = in_ref.shape[2] - width
    rows = lax.broadcasted_iota(jnp.int32, (inner, lanes), 0)
    columns = lax.broadcasted_iota(jnp.int32, (inner, lanes), 1)
    member = ((rows >= columns * head_size) & (rows < (columns + 1) * head_size)).astype(bf16)
    step_grad = dot_nn((scaled_grad * value).astype(bf16), member)
    raw_grad = step_grad[:, :heads] * jax.nn.sigmoid(raw_full)
    taps_ref[5:6, :heads] += jnp.sum(raw_grad, axis=0, keepdims=True)
    raw_grad = jnp.concatenate([raw_grad, jnp.zeros((block, lanes - heads), f32)], axis=1)
    in_ref[:, :, width:] = raw_grad.astype(bf16).reshape(in_ref.shape[:2] + (lanes,))
    pre_grad = jnp.concatenate([x_grad, b_grad, c_grad], axis=1) * slope
    for k in range(count):
        taps_ref[k : k + 1, :] += jnp.sum(pre_grad * buf[5 + k : 5 + k + block, :], axis=0, keepdims=True)
    taps_ref[4:5, :] += jnp.sum(pre_grad, axis=0, keepdims=True)
    buf[0:block, :] = pre_grad
    buf[block : block + 8, :] = nextp[...]
    nextp[...] = buf[0:8, :]
    head_ref[...] = buf[0:8, :]
    in_grad = sum(taps[k : k + 1, :] * buf[3 - k : 3 - k + block, :] for k in range(count))
    in_ref[:, :, :width] = in_grad.astype(bf16).reshape(in_ref.shape[:2] + (width,))

    @pl.when(turn == 0)
    def _():
        tail_ref[...] = in_grad[block - 8 :, :]


def params():
    return pltpu.CompilerParams(vmem_limit_bytes=56 * 2**20)


def cost(flops, moved, powers):
    return pl.CostEstimate(flops=int(flops), bytes_accessed=int(moved), transcendentals=int(powers))


def rows_of(share, width, flip=0):
    per = BLOCK // share
    if flip:
        return pl.BlockSpec((per, None, share, width), lambda b, k: (flip - 1 - k, b, 0, 0))
    return pl.BlockSpec((per, None, share, width), lambda b, k: (k, b, 0, 0))


def each(height, width):
    return pl.BlockSpec((None, height, width), lambda b, k: (b, 0, 0))


def only(height, width):
    return pl.BlockSpec((height, width), lambda b, k: (0, 0))


def at_block(height, width, flip=0):
    if flip:
        return pl.BlockSpec((None, None, height, width), lambda b, k: (b, flip - 1 - k, 0, 0))
    return pl.BlockSpec((None, None, height, width), lambda b, k: (b, k, 0, 0))


def in_order(width, flip=0):
    if flip:
        return pl.BlockSpec((None, BLOCK, width), lambda b, k: (b, flip - 1 - k, 0))
    return pl.BlockSpec((None, BLOCK, width), lambda b, k: (b, k, 0))


def made(*shape, kind=bf16):
    return jax.ShapeDtypeStruct(shape, kind)


def scan_forward(cin, edge, taps, raw, bias, decay, decay_t, inner, size):
    shares, batch, share, width = cin.shape
    heads = raw.shape[3]
    tokens = shares * share
    blocks = tokens // BLOCK
    return pl.pallas_call(
        scan_kernel,
        grid=(batch, blocks),
        in_specs=[
            rows_of(share, width),
            each(8, width),
            only(8, width),
            rows_of(share, heads),
            only(1, heads),
            in_order(heads),
            pl.BlockSpec((None, heads, BLOCK), lambda b, k: (b, 0, k)),
        ],
        out_specs=[rows_of(share, width), rows_of(share, inner), at_block(size, inner), each(size, inner)],
        out_shape=[
            made(shares, batch, share, width),
            made(shares, batch, share, inner, kind=f32),
            made(batch, blocks, size, inner, kind=f32),
            made(batch, size, inner, kind=f32),
        ],
        scratch_shapes=[
            pltpu.VMEM((BLOCK + 8, width), f32),
            pltpu.VMEM((8, width), f32),
            pltpu.VMEM((size, inner), f32),
        ],
        compiler_params=params(),
        cost_estimate=cost(
            batch * tokens * inner * (4 * BLOCK + 4 * size), 10 * batch * tokens * inner, batch * tokens * heads * BLOCK
        ),
    )(cin, edge, taps, raw, bias, decay, decay_t)


def gate_forward(y, act, z, decay, lead, entering, skip, gain, w_out):
    shares, batch, share, inner = y.shape
    width, heads, size = act.shape[3], decay.shape[2], entering.shape[1]
    model = w_out.shape[1]
    tokens = shares * share
    return pl.pallas_call(
        gate_kernel,
        grid=(batch, tokens // BLOCK),
        in_specs=[
            rows_of(share, inner),
            rows_of(share, width),
            rows_of(share, inner),
            in_order(heads),
            at_block(1, inner),
            each(size, inner),
            only(1, inner),
            only(1, inner),
            only(inner, model),
        ],
        out_specs=[rows_of(share, inner), rows_of(share, inner), rows_of(share, 128), rows_of(share, model)],
        out_shape=[
            made(shares, batch, share, inner),
            made(shares, batch, share, inner),
            made(shares, batch, share, 128, kind=f32),
            made(shares, batch, share, model),
        ],
        compiler_params=params(),
        cost_estimate=cost(
            2 * batch * tokens * inner * (model + size), batch * tokens * inner * 18, batch * tokens * inner
        ),
    )(y, act, z, decay, lead, entering, skip, gain, w_out)


def gate_backward(push, w_out, mixed, z, act, decay, lead, gain):
    shares, batch, share, inner = mixed.shape
    width, heads, model = act.shape[3], decay.shape[2], w_out.shape[1]
    size = (width - inner) // 2
    tokens = shares * share
    return pl.pallas_call(
        gate_back_kernel,
        grid=(batch, tokens // BLOCK),
        in_specs=[
            rows_of(share, model),
            only(inner, model),
            rows_of(share, inner),
            rows_of(share, inner),
            rows_of(share, width),
            in_order(heads),
            at_block(1, inner),
            pl.BlockSpec((BLOCK // share, None, share, 128), lambda b, k: (k, b, 0, model // 128)),
            only(1, inner),
        ],
        out_specs=[rows_of(share, inner), rows_of(share, inner), each(size, inner), only(8, inner)],
        out_shape=[
            made(shares, batch, share, inner),
            made(shares, batch, share, inner),
            made(batch, size, inner, kind=f32),
            made(8, inner, kind=f32),
        ],
        compiler_params=params(),
        cost_estimate=cost(
            2 * batch * tokens * inner * (model + size), batch * tokens * inner * 18, batch * tokens * inner
        ),
    )(push, w_out, mixed, z, act, decay, lead, push, gain)


def scan_backward(cin, edge, taps, raw, bias, decay, decay_t, act, dy, start, lead, entering, leave_grad, skip):
    shares, batch, share, width = cin.shape
    heads, inner, size = raw.shape[3], dy.shape[3], entering.shape[1]
    tokens = shares * share
    blocks = tokens // BLOCK
    per = BLOCK // share
    return pl.pallas_call(
        scan_back_kernel,
        grid=(batch, blocks),
        in_specs=[
            rows_of(share, width, blocks),
            pl.BlockSpec(
                (None, None, 16, width),
                lambda b, k: (jnp.maximum((blocks - 1 - k) * per - 1, 0), b, share // 16 - 1, 0),
            ),
            each(8, width),
            only(8, width),
            rows_of(share, heads, blocks),
            only(1, heads),
            in_order(heads, blocks),
            pl.BlockSpec((None, heads, BLOCK), lambda b, k: (b, 0, blocks - 1 - k)),
            rows_of(share, width, blocks),
            rows_of(share, inner, blocks),
            at_block(size, inner, blocks),
            at_block(1, inner, blocks),
            each(size, inner),
            each(size, inner),
            only(1, inner),
        ],
        out_specs=[rows_of(share, width + 128, blocks), each(8, width), each(8, width), only(8, width)],
        out_shape=[
            made(shares, batch, share, width + 128),
            made(batch, 8, width, kind=f32),
            made(batch, 8, width, kind=f32),
            made(8, width, kind=f32),
        ],
        scratch_shapes=[
            pltpu.VMEM((BLOCK + 8, width), f32),
            pltpu.VMEM((8, width), f32),
            pltpu.VMEM((size, inner), f32),
        ],
        compiler_params=params(),
        cost_estimate=cost(
            batch * tokens * inner * (8 * BLOCK + 10 * size), 15 * batch * tokens * inner, batch * tokens * heads * BLOCK
        ),
    )(cin, cin, edge, taps, raw, bias, decay, decay_t, act, dy, start, lead, entering, leave_grad, skip)


def end_rows(in_grad, last, following, taps):
    shares, batch, share, width = in_grad.shape
    columns = last.shape[2]

    def kernel(rows, last_ref, next_ref, taps_ref, out_ref, buf):
        for b in range(batch):
            buf[0:8, :] = jnp.zeros((8, columns), f32)
            buf[8:16, :] = next_ref[b]
            added = sum(taps_ref[k : k + 1, :] * buf[3 - k : 11 - k, :] for k in range(4))
            old = rows[b].astype(f32)
            end = jnp.concatenate([last_ref[b] + added, old[8:, columns:]], axis=1)
            out_ref[b] = jnp.concatenate([old[:8], end], axis=0).astype(bf16)

    block = pl.BlockSpec((None, batch, 16, width), lambda i: (shares - 1, 0, share // 16 - 1, 0))

    def whole(array):
        zeros = (0,) * array.ndim
        return pl.BlockSpec(array.shape, lambda i: zeros)

    return pl.pallas_call(
        kernel,
        grid=(1,),
        in_specs=[block, whole(last), whole(following), whole(taps)],
        out_specs=block,
        out_shape=made(*in_grad.shape),
        input_output_aliases={0: 0},
        scratch_shapes=[pltpu.VMEM((16, columns), f32)],
        compiler_params=params(),
        cost_estimate=cost(16 * width * batch, 200 * width * batch, 0),
    )(in_grad, last, following, taps)


def weight_grads(groups, depth, tile, extra=None):
    rows = groups[0][0][0].shape[0]
    tiles = [group[0][1].shape[1] // tile for group in groups]
    starts = [sum(tiles[:g]) for g in range(len(groups) + 1)]
    terms = max(len(group) for group in groups)
    flat = [array for group in groups for term in group for array in term]
    count = len(flat)

    def kernel(*refs):
        out, turned = refs[-2], refs[-1]
        j = pl.program_id(0)
        place = 0
        for g, group in enumerate(groups):
            mine = refs[place : place + 2 * len(group)]
            place += 2 * len(group)

            @pl.when(j == starts[g])
            def _(mine=mine):
                for t in range(len(mine) // 2):
                    turned[t] = mine[2 * t][...].T

            @pl.when((j >= starts[g]) & (j < starts[g + 1]))
            def _(mine=mine):
                total = sum(dot_nn(turned[t], mine[2 * t + 1][...]) for t in range(len(mine) // 2))
                out[...] = total.astype(bf16)

        if extra is not None:

            @pl.when(j == starts[-1] - 1)
            def _():
                added = refs[count]
                room = tile - added.shape[1]
                out[:, room:] = (out[:, room:].astype(f32) + added[...].astype(f32)).astype(bf16)

    specs = []
    for g, group in enumerate(groups):
        for _ in group:
            specs.append(pl.BlockSpec((rows, depth), lambda j: (0, 0), pipeline_mode=pl.Buffered(1)))
            specs.append(
                pl.BlockSpec((rows, tile), lambda j, a=starts[g], n=tiles[g]: (0, jnp.clip(j - a, 0, n - 1)))
            )
    steps = starts[-1]
    if extra is not None:
        flat = flat + [extra]
        specs.append(pl.BlockSpec(extra.shape, lambda j: (0, 0)))
    return pl.pallas_call(
        kernel,
        grid=(steps,),
        in_specs=specs,
        out_specs=pl.BlockSpec((depth, tile), lambda j: (0, j)),
        out_shape=jax.ShapeDtypeStruct((depth, steps * tile), bf16),
        scratch_shapes=[pltpu.VMEM((terms, depth, rows), bf16)],
        compiler_params=params(),
        cost_estimate=cost(2 * terms * rows * depth * tile * steps, 2 * (count * rows * depth + depth * tile * steps), 0),
    )(*flat)


def gates_of(gates_ref, mine):
    terms = gates_ref[...].astype(f32)
    every = mine.shape[1]
    return terms[:, :every] + terms[:, every : 2 * every]


def expert_forward_kernel(shared, x_ref, grad_ref, gates_ref, mine, w_gu, w_down, *refs):
    out_ref, logit_ref, both_ref = refs[-3:]
    x = x_ref[...]
    gates = gates_of(gates_ref, mine)
    wide = grad_ref[...].astype(f32)
    out = own = total = 0.0
    width = w_down.shape[1]
    for e in range(w_gu.shape[0]):
        weight = jnp.sum(gates * mine[e : e + 1, :], axis=1, keepdims=True)
        both = dot_nn(x, w_gu[e])
        both_ref[:, 2 * e * width : 2 * (e + 1) * width] = both
        gate, up = both[:, :width], both[:, width:]
        act = (gate * jax.nn.sigmoid(gate) * up).astype(bf16)
        result = dot_nn(act, w_down[e]).astype(bf16).astype(f32)
        push = jnp.sum(wide * result, axis=1, keepdims=True)
        own = own + push * mine[e : e + 1, :]
        total = total + weight * push
        out = out + weight * result
    if shared:
        ws_gu, ws_down = refs[:2]
        first, ff = 2 * w_gu.shape[0] * width, ws_down.shape[0]
        gate, up = dot_nn(x, ws_gu[0]), dot_nn(x, ws_gu[1])
        both_ref[:, first : first + ff] = gate
        both_ref[:, first + ff :] = up
        act = (gate * jax.nn.sigmoid(gate) * up).astype(bf16)
        out = out + dot_nn(act, ws_down[...])
    out_ref[...] = out.astype(bf16)
    logit_ref[...] = gates * (own - total)


def expert_backward_kernel(shared, grad_ref, gates_ref, both_ref, mine, w_gu, w_down, *refs):
    grad = grad_ref[...]
    gates = gates_of(gates_ref, mine)
    wide = grad.astype(f32)
    dx_ref, act_ref, gu_ref = refs[2:5] if shared else refs

    def back(gate, up, act_push):
        sigma = jax.nn.sigmoid(gate)
        silu = gate * sigma
        slope = sigma + silu * (1.0 - sigma)
        gu_grad = jnp.concatenate([act_push * up * slope, act_push * silu], axis=1).astype(bf16)
        return (silu * up).astype(bf16), gu_grad

    dx = 0.0
    width = w_down.shape[1]
    for e in range(w_gu.shape[0]):
        weight = jnp.sum(gates * mine[e : e + 1, :], axis=1, keepdims=True)
        act_push = dot_nt((weight * wide).astype(bf16), w_down[e])
        middle = (2 * e + 1) * width
        gate, up = both_ref[:, middle - width : middle], both_ref[:, middle : middle + width]
        act, gu_grad = back(gate, up, act_push)
        act_ref[:, e * width : (e + 1) * width] = (weight * act.astype(f32)).astype(bf16)
        gu_ref[:, middle - width : middle + width] = gu_grad
        dx = dx + dot_nt(gu_grad, w_gu[e]).astype(bf16).astype(f32)
    if shared:
        ws_gu, ws_down = refs[:2]
        s_act_ref, s_gu_ref = refs[5:]
        first, ff = 2 * w_gu.shape[0] * width, ws_down.shape[0]
        gate, up = both_ref[:, first : first + ff], both_ref[:, first + ff :]
        act, gu_grad = back(gate, up, dot_nt(grad, ws_down[...]))
        s_act_ref[...] = act
        s_gu_ref[...] = gu_grad
        dx = dx + dot_nt(gu_grad[:, :ff], ws_gu[0]) + dot_nt(gu_grad[:, ff:], ws_gu[1])
    dx_ref[...] = dx.astype(bf16)


def by_rows(columns, at=0):
    return pl.BlockSpec((ROWS, columns), lambda i: (i, at))


def kept(array):
    zeros = (0,) * array.ndim
    return pl.BlockSpec(array.shape, lambda i: zeros, pipeline_mode=pl.Buffered(1))


def experts_forward(x, grad, mine, w_gu, w_down, shared=()):
    rows = x.shape[0]
    count, model, double = w_gu.shape
    beside = x.shape[1] - model
    every = mine.shape[1]
    hidden = count * double + (2 * shared[1].shape[0] if shared else 0)
    return pl.pallas_call(
        lambda *refs: expert_forward_kernel(bool(shared), *refs),
        grid=(rows // ROWS,),
        in_specs=[by_rows(model), by_rows(model), by_rows(beside, model // beside)]
        + [kept(w) for w in (mine, w_gu, w_down, *shared)],
        out_specs=[by_rows(model), by_rows(every), by_rows(hidden)],
        out_shape=[made(rows, model), made(rows, every, kind=f32), made(rows, hidden, kind=f32)],
        compiler_params=params(),
        cost_estimate=cost(3 * rows * hidden * model, 3 * hidden * model + rows * (6 * model + 4 * hidden), rows * hidden),
    )(x, grad, x, mine, w_gu, w_down, *shared)


def experts_backward(x, grad, both, mine, w_gu, w_down, shared=()):
    rows = x.shape[0]
    count, model, double = w_gu.shape
    beside = x.shape[1] - model
    hidden = both.shape[1]
    widths = [model, count * double // 2, count * double]
    if shared:
        widths += [shared[1].shape[0], 2 * shared[1].shape[0]]
    return pl.pallas_call(
        lambda *refs: expert_backward_kernel(bool(shared), *refs),
        grid=(rows // ROWS,),
        in_specs=[by_rows(model), by_rows(beside, model // beside), by_rows(hidden)]
        + [kept(w) for w in (mine, w_gu, w_down, *shared)],
        out_specs=[by_rows(w) for w in widths],
        out_shape=[made(rows, w) for w in widths],
        compiler_params=params(),
        cost_estimate=cost(3 * rows * hidden * model, 3 * hidden * model + rows * (4 * model + 7 * hidden), rows * hidden),
    )(grad, x, both, mine, w_gu, w_down, *shared)


def summed(got):
    return sum(got[i].astype(f32) for i in range(got.shape[0]))


def two_terms(values, width):
    high = values.astype(bf16)
    low = (values - high.astype(f32)).astype(bf16)
    terms, room = [high, low], width - 2 * values.shape[1]
    if room:
        terms.append(jnp.zeros((values.shape[0], room), bf16))
    return jnp.concatenate(terms, axis=1)


def after_mix_kernel(inner, got, x, squares, used, gain, router, packed_ref, hidden_ref, mix_ref, scale_ref):
    model = x.shape[1]
    mix = summed(got)
    gate_scale = lax.rsqrt(squares[...] / inner + norm_eps)
    hidden = x[...].astype(f32) + mix * gate_scale
    scale = lax.rsqrt(jnp.mean(hidden * hidden, axis=1, keepdims=True) + norm_eps)
    normed = (hidden * scale * gain[...]).astype(bf16)
    mask = used[...] > 0.0
    logits = jnp.where(mask, dot_nn(normed, router[...]), -1e30)
    powers = jnp.where(mask, jnp.exp(logits - jnp.max(logits, axis=1, keepdims=True)), 0.0)
    gates = powers / jnp.sum(powers, axis=1, keepdims=True)
    packed_ref[:, :model] = normed
    packed_ref[:, model:] = two_terms(gates, packed_ref.shape[1] - model)
    hidden_ref[...] = hidden
    mix_ref[...] = mix
    lane = lax.broadcasted_iota(jnp.int32, scale_ref.shape, 1)
    scale_ref[...] = jnp.where(lane == 0, gate_scale, scale)


def after_ffn_kernel(inner, got, hidden_in, mix, scales, grad, gain, packed_ref, grad_ref, sum_ref):
    model = grad.shape[1]
    dx, hidden = summed(got), hidden_in[...]
    gate_scale, scale = scales[:, 0:1], scales[:, 1:2]
    gained = dx * gain[...]
    mean = jnp.mean(gained * hidden, axis=1, keepdims=True)
    hidden_grad = grad[...].astype(f32) + scale * (gained - hidden * (scale * scale * mean))
    grad_ref[...] = hidden_grad
    push = jnp.sum(hidden_grad * mix[...], axis=1, keepdims=True)
    slope = (-0.5 / inner) * push * gate_scale * gate_scale * gate_scale
    packed_ref[:, :model] = (hidden_grad * gate_scale).astype(bf16)
    packed_ref[:, model:] = two_terms(slope, packed_ref.shape[1] - model)

    @pl.when(pl.program_id(0) == 0)
    def _():
        sum_ref[...] = jnp.zeros_like(sum_ref)

    sum_ref[0:1, :] += jnp.sum(dx * hidden * scale, axis=0, keepdims=True)


def after_proj_kernel(got, x_in, hidden_grad, gain, out_ref):
    dn, x = summed(got), x_in[...].astype(f32)
    scale = lax.rsqrt(jnp.mean(x * x, axis=1, keepdims=True) + norm_eps)
    gained = dn * gain[...]
    mean = jnp.mean(gained * x, axis=1, keepdims=True)
    out_ref[...] = (hidden_grad[...] + scale * (gained - x * (scale * scale * mean))).astype(bf16)


def on_share(kernel, got, rows, wholes, outs, sums=()):
    shares, batch, share, model = got.shape

    def rows_at(width):
        return pl.BlockSpec((None, share, width), lambda b: (b, 0, 0))

    def kept_at(shape):
        return pl.BlockSpec(shape, lambda b: (0, 0))

    return pl.pallas_call(
        kernel,
        grid=(batch,),
        in_specs=[pl.BlockSpec((shares, None, share, model), lambda b: (0, b, 0, 0))]
        + [rows_at(r.shape[2]) for r in rows]
        + [kept_at(w.shape) for w in wholes],
        out_specs=[rows_at(width) for width, _ in outs] + [kept_at(shape) for shape in sums],
        out_shape=[made(batch, share, width, kind=kind) for width, kind in outs]
        + [made(*shape, kind=f32) for shape in sums],
        compiler_params=params(),
        cost_estimate=cost(40 * batch * share * model, 30 * batch * share * model, batch * share),
    )(got, *rows, *wholes)


def shifted(array, axis, by):
    count = lax.axis_size(axis)
    pairs = [(i, i + by) for i in range(count) if 0 <= i + by < count]
    return lax.ppermute(array, axis, pairs)


def prefix(part, axis, combine, identity):
    place = lax.axis_index(axis)
    gathered = jax.tree.map(lambda a: lax.all_gather(a, axis), part)
    state = jax.tree.map(lambda a, e: jnp.zeros_like(a) + jnp.asarray(e, a.dtype), part, identity)

    def one(lap, state):
        return combine(
            state, jax.tree.map(lambda a: lax.dynamic_index_in_dim(a, lap, 0, False), gathered)
        )

    return lax.fori_loop(0, place, one, state)


def prefix_2(array, axis, combine, identity):
    count, place = (lax.axis_size(axis), lax.axis_index(axis))
    everything = jax.tree.map(
        lambda part, kind: lax.all_gather(part.astype(kind), axis),
        array,
        jax.tree.map(lambda a: jnp.bfloat16 if a.dtype == jnp.float32 else a.dtype, array),
    )
    start = jax.tree.map(
        lambda part, zero: jnp.broadcast_to(jnp.asarray(zero, part.dtype), part.shape),
        array,
        identity,
    )

    def lap(k, before):
        at = count - 1 - k
        reached = at > place
        new = combine(
            before, jax.tree.map(lambda part, own: part[at].astype(own.dtype), everything, array)
        )
        return jax.tree.map(lambda a, b: jnp.where(reached, a, b), new, before)

    return lax.fori_loop(0, count, lap, start)


def swap_shares(part):
    return lax.all_to_all(part, "head", split_axis=0, concat_axis=0, tiled=True)


def gather_shares(share):
    copies = jnp.broadcast_to(share[None], (lax.axis_size("head"),) + share.shape)
    return lax.all_to_all(copies, "head", split_axis=0, concat_axis=0, tiled=True)


def relay(part, *beside):
    count, place = lax.axis_size("head"), lax.axis_index("head")

    def passed(array, by, start=0):
        pairs = [(i, i + by) for i in range(count) if 0 <= i + by < count]
        pairs = [(i, j) for i, j in pairs if 0 <= i - start * by < count]
        return lax.ppermute(array, "head", pairs)

    if count == 4:
        up, down = passed(part, 1), passed(part, -1)
        far = lax.ppermute(part, "head", [(0, 3), (3, 0)])
        up_two, down_two = passed(up, 1, 1), passed(down, -1, 1)
        if beside:
            far, *beside = tie(far, *beside)
        pieces = [
            part,
            jnp.where(place >= 1, up, far),
            jnp.where(place >= 2, up_two, down_two),
            jnp.where(place >= 3, far, down),
        ]
        return (pieces, *beside) if beside else pieces
    up, down = [part], [part]
    for _ in range(count - 1):
        up.append(passed(up[-1], 1))
        down.append(passed(down[-1], -1))
    pieces = [part] + [jnp.where(place >= d, up[d], down[count - d]) for d in range(1, count)]
    return (pieces, *beside) if beside else pieces


def laid(pieces, axis=0):
    count, place = lax.axis_size("head"), lax.axis_index("head")
    shape = pieces[0].shape[:axis] + (count,) + pieces[0].shape[axis:]
    out = jnp.zeros(shape, pieces[0].dtype)
    for d, piece in enumerate(pieces):
        out = lax.dynamic_update_index_in_dim(out, piece, (place + count - d) % count, axis)
    return out


def relay_shares(share, axis=0):
    return laid(relay(share), axis)


def bits_of(axis):
    count = lax.axis_size(axis)
    return [(1 << k) for k in range(count.bit_length() - 1)]


def across(array, axis, bit):
    return lax.ppermute(array, axis, [(i, i ^ bit) for i in range(lax.axis_size(axis))])


def add_over(array, *axes):
    for axis in axes:
        for bit in bits_of(axis):
            array = array + across(array, axis, bit)
    return array


def join_over(array, dimension, *axes):
    for axis in axes:
        place = lax.axis_index(axis)
        for bit in bits_of(axis):
            other = across(array, axis, bit)
            array = jnp.where(
                (place & bit) == 0,
                jnp.concatenate([array, other], axis=dimension),
                jnp.concatenate([other, array], axis=dimension),
            )
    return array


def tie(*arrays):
    return lax.optimization_barrier(arrays)


def around(array, by):
    count = lax.axis_size("seq")
    if by % count == 0:
        return array
    return lax.ppermute(array, "seq", [(i, (i + by) % count) for i in range(count)])


def spread_last(local_part, rank_index, part_count):
    local_width = local_part.shape[-1]
    full_array = jnp.zeros(local_part.shape[:-1] + (local_width * part_count,), jnp.float32)
    return lax.dynamic_update_slice_in_dim(
        full_array, local_part, rank_index * local_width, local_part.ndim - 1
    )


def chain_forward(earlier, later):
    return (earlier[0] * later[0], later[0] * earlier[1] + later[1])


def chain_backward(earlier, later):
    return (earlier[0] * later[0], later[1] + later[0] * earlier[1])


def local(
    x_in,
    d_out,
    log_decay,
    routes,
    norm1_gain,
    w_in_zx,
    w_in_bc,
    w_in_dt,
    dt_bias,
    conv_x,
    conv_x_bias,
    conv_bc,
    conv_bc_bias,
    skip_d,
    gate_norm_gain,
    w_out,
    norm2_gain,
    router,
    w_expert_gu,
    w_expert_down,
    w_shared_gu,
    w_shared_down,
):
    batch_size, tokens, model_width = x_in.shape
    inner_dev = w_in_zx.shape[2]
    heads_dev = w_in_dt.shape[1]
    head_size = inner_dev // heads_dev
    state_size = w_in_bc.shape[1] // 2
    conv_taps = conv_x.shape[0]
    experts_dev = w_expert_gu.shape[0]
    head_count = lax.axis_size("head")
    seq_count = lax.axis_size("seq")
    head_rank = lax.axis_index("head")
    seq_rank = lax.axis_index("seq")
    inner_all = inner_dev * head_count
    experts_all = experts_dev * seq_count * head_count
    share_rows = tokens // head_count
    rows_all = batch_size * tokens
    conv_width = inner_dev + 2 * state_size

    def by_share(array):
        array = array.reshape((batch_size, head_count, share_rows) + array.shape[2:])
        return jnp.swapaxes(array, 0, 1)

    def by_position(array):
        return jnp.swapaxes(array, 0, 1).reshape(batch_size, tokens, array.shape[-1])

    def own_share(array):
        return lax.dynamic_index_in_dim(array, head_rank, 0, keepdims=False)

    def flat(array):
        return array.reshape(-1, array.shape[-1])

    def times(a, b):
        return lax.dot_general(a, b, (((a.ndim - 1,), (0,)), ((), ())), preferred_element_type=f32)

    def times_t(a, b):
        return lax.dot_general(a, b, (((a.ndim - 1,), (1,)), ((), ())), preferred_element_type=f32)

    def scattered(array, axes):
        return lax.psum_scatter(array, axes, scatter_dimension=0, tiled=True)

    x_rows, grad_rows = by_share(x_in), by_share(d_out)
    grads_in = [flat(around(grad_rows, k)) for k in range(seq_count)]
    input_wide = x_rows.astype(f32)
    scale_one = lax.rsqrt(jnp.mean(input_wide * input_wide, axis=-1, keepdims=True) + norm_eps)
    normed_one = (input_wide * scale_one * norm1_gain).astype(bf16)
    w_conv = jnp.concatenate([w_in_zx[1], w_in_bc], axis=-1)
    w_step = jnp.pad(w_in_dt, ((0, 0), (0, 128 - heads_dev)))
    w_late = jnp.concatenate([w_conv, w_step], axis=-1)
    conv_in = times(normed_one, w_conv).astype(bf16)
    step_raw = times(normed_one, w_step)[..., :heads_dev]
    gate_z = times(normed_one, w_in_zx[0])
    edge_rows = shifted(conv_in[head_count - 1, :, share_rows - 8 :].astype(f32), "seq", 1)
    edge_rows, gate_z = tie(edge_rows, gate_z)
    taps = jnp.concatenate([conv_x, conv_bc], axis=1)
    bias = jnp.concatenate([conv_x_bias, conv_bc_bias])
    taps_bias = jnp.concatenate([taps, bias[None], jnp.zeros((7 - conv_taps, conv_width), f32)])
    decay_across = jnp.transpose(log_decay, (0, 2, 1))
    step_bias = dt_bias[None]
    totals = jnp.sum(log_decay.reshape(batch_size, -1, BLOCK, heads_dev), axis=2)
    before = [jnp.zeros_like(totals[:, 0])]
    for k in range(totals.shape[1]):
        before.append(before[-1] + totals[:, k])
    lead = jnp.repeat(jnp.exp(jnp.stack(before, axis=1)), head_size, axis=-1)
    device_decay, lead = lead[:, -1:], lead[:, :-1, None]
    skip = jnp.repeat(skip_d, head_size)[None]
    gate_gain = gate_norm_gain[None]

    conv_act, scanned, starts, leaving = scan_forward(
        conv_in, edge_rows, taps_bias, step_raw, step_bias, log_decay, decay_across, inner_dev, state_size
    )
    identity = (jnp.ones_like(device_decay), jnp.zeros_like(leaving))
    if seq_count == 2:
        entering = shifted(leaving, "seq", 1)
    else:
        _, entering = prefix((device_decay, leaving), "seq", chain_forward, identity)
    mixed, gated_low, squares, partial_out = gate_forward(
        scanned, conv_act, gate_z, log_decay, lead, entering, skip, gate_gain, w_out
    )

    got_mix, *grads_in = tie(swap_shares(partial_out), *grads_in)
    squares = own_share(add_over(squares[..., 0], "head"))
    expert_ids = jnp.arange(experts_all, dtype=jnp.int32)
    used = jnp.any(own_share(by_share(routes))[..., None] == expert_ids, axis=2).astype(f32)
    x_share, grad_share = own_share(x_rows), own_share(grad_rows)
    beside = -(-2 * experts_all // 128) * 128
    normed_share, hidden, mix_out, scales = on_share(
        lambda *refs: after_mix_kernel(inner_all, *refs),
        got_mix,
        [x_share, squares[..., None], used],
        [norm2_gain[None], router],
        [(model_width + beside, bf16), (model_width, f32), (model_width, f32), (128, f32)],
    )
    pieces = relay(normed_share)
    rows_in = [flat(laid([around(piece, k) for piece in pieces])) for k in range(seq_count)]

    first = (seq_rank * head_count + head_rank) * experts_dev
    mine = (jnp.arange(8)[:, None] + first == expert_ids) & (jnp.arange(8)[:, None] < experts_dev)
    mine = mine.astype(f32)
    turns = [*range(1, seq_count), 0]
    ffn_out, ffn_dx, logit_grad, before_act = [], [], [], []
    for k in turns:
        shared = (w_shared_gu, w_shared_down) if k == 0 else ()
        out, logit, both = experts_forward(rows_in[k], grads_in[k], mine, w_expert_gu, w_expert_down, shared)
        ffn_out.append(around(out, -k))
        logit_grad.append(around(logit, -k))
        before_act.append(both)
    ffn_low = sum(f.astype(f32) for f in ffn_out).astype(bf16)
    ffn_low = ffn_low.reshape(head_count, batch_size, share_rows, model_width)
    ffn_low, before_act[-1] = tie(ffn_low, before_act[-1])
    got_out = swap_shares(ffn_low)
    up_terms, down_terms = [], []
    for k, both in zip(turns, before_act):
        shared = (w_shared_gu, w_shared_down) if k == 0 else ()
        made_k = experts_backward(rows_in[k], grads_in[k], both, mine, w_expert_gu, w_expert_down, shared)
        ffn_dx.append(around(made_k[0], -k))
        down_terms.append((grads_in[k], made_k[1]))
        up_terms.append((rows_in[k], made_k[2]))
    shared_terms = [[(rows_in[0], made_k[4])], [(grads_in[0], made_k[3])]]
    logit_grad = sum(logit_grad).astype(bf16)
    ffn_dx = sum(d.astype(f32) for d in ffn_dx) + times_t(logit_grad, router)
    ffn_dx = ffn_dx.astype(bf16).reshape(ffn_low.shape)
    ffn_dx, *gu_grads = tie(ffn_dx, *[term[1] for term in up_terms])
    up_terms = [(term[0], gu_grad) for term, gu_grad in zip(up_terms, gu_grads)]
    ffn_dx, got_out = tie(ffn_dx, got_out)
    got_dx = swap_shares(ffn_dx)
    expert_grads = [
        weight_grads([up_terms[k : k + 2], down_terms[k : k + 2]], model_width, 512)
        for k in range(0, seq_count, 2)
    ]
    if len(expert_grads) > 1:
        expert_grads = [sum(g.astype(f32) for g in expert_grads).astype(bf16)]
    got_dx, expert_grads, logit_grad = tie(got_dx, expert_grads[0], logit_grad)
    expert_sum = scattered(expert_grads, "dp")
    grad_router = lax.dot_general(
        logit_grad, rows_in[0], (((0,), (0,)), ((), ())), preferred_element_type=f32
    )[:, :model_width]
    push_share, hidden_grad, norm_two_sums = on_share(
        lambda *refs: after_ffn_kernel(inner_all, *refs),
        got_dx,
        [hidden, mix_out, scales, grad_share],
        [norm2_gain[None]],
        [(model_width + 128, bf16), (model_width, f32)],
        [(8, model_width)],
    )
    out_push = relay_shares(push_share)

    layer_share, out_push = tie((hidden + summed(got_out)).astype(bf16), out_push)
    layer_out = gather_shares(layer_share)

    mixed_grad, z_grad, entering_grad, channel_sums = gate_backward(
        out_push, w_out, mixed, gate_z, conv_act, log_decay, lead, gate_gain
    )
    if seq_count == 2:
        leaving_grad = shifted(entering_grad.astype(bf16), "seq", -1).astype(f32)
    else:
        _, leaving_grad = prefix_2((device_decay, entering_grad), "seq", chain_backward, identity)
    in_grad, first_rows, last_rows, tap_sums = scan_backward(
        conv_in,
        edge_rows,
        taps_bias,
        step_raw,
        step_bias,
        log_decay,
        decay_across,
        conv_act,
        mixed_grad,
        starts,
        lead,
        entering,
        leaving_grad,
        skip,
    )
    early_dx = times_t(z_grad, w_in_zx[0])
    in_grad, early_dx, expert_sum = tie(in_grad, early_dx, expert_sum)
    in_grad = end_rows(in_grad, last_rows, shifted(first_rows, "seq", -1), taps_bias)
    normed_one_grad = early_dx + times_t(in_grad, w_late)
    grad_norm_one = jnp.sum(normed_one_grad * input_wide * scale_one, axis=(0, 1, 2))
    normed_one_grad = normed_one_grad.astype(bf16)
    normed_one_grad, in_grad, layer_out = tie(normed_one_grad, in_grad, layer_out)
    got_dn = swap_shares(normed_one_grad)

    def whole(array):
        return spread_last(array, head_rank, head_count).reshape(-1)

    small = [
        norm_two_sums[0],
        grad_router.reshape(-1),
        whole(tap_sums[:conv_taps, :inner_dev]),
        whole(tap_sums[conv_taps, :inner_dev]),
        whole(channel_sums[0]),
        grad_norm_one,
        tap_sums[:conv_taps, inner_dev:].reshape(-1),
        tap_sums[conv_taps, inner_dev:],
        whole(tap_sums[conv_taps + 1, :heads_dev]),
        whole(jnp.sum(channel_sums[1].reshape(heads_dev, head_size), axis=-1)),
    ]
    sizes = [a.shape[0] for a in small]
    skipped = 16 * model_width
    small = [jnp.zeros((skipped,), f32)] + small
    small = jnp.concatenate(small + [jnp.zeros((128 * model_width - skipped - sum(sizes),), f32)])
    small = small.reshape(128, model_width).T.astype(bf16)
    grad_late = weight_grads([[(flat(normed_one), flat(in_grad))]], model_width, 384, small)
    early_terms = [[(flat(out_push), flat(gated_low))], [(flat(normed_one), flat(z_grad))]]
    grad_early = weight_grads(early_terms + shared_terms, model_width, 256)
    late_sum = scattered(grad_late, ("dp", "seq"))
    late_sum, got_dn = tie(late_sum, got_dn)
    input_grad = on_share(
        after_proj_kernel, got_dn, [x_share, hidden_grad], [norm1_gain[None]], [(model_width, bf16)]
    )[0]
    merged = late_sum[:, inner_dev:]
    for bit in bits_of("head"):
        merged = merged.astype(bf16)
        merged = merged.astype(f32) + across(merged, "head", bit).astype(f32)
    merged = merged.astype(bf16)
    input_grad, merged = tie(input_grad, merged)
    late_sum, grad_early = tie(late_sum, grad_early)
    early_sum = scattered(grad_early, ("dp", "seq")).astype(f32)
    pieces, merged, layer_out, late_sum, expert_sum = relay(
        input_grad, merged, layer_out, late_sum, expert_sum
    )
    late_sum = late_sum.astype(f32)
    merged = join_over(merged[None], 0, "dp", "seq")
    merged = jnp.swapaxes(merged.reshape((seq_count, -1) + merged.shape[1:]), 0, 1)
    merged = merged.reshape(model_width, -1).astype(f32)
    layer_out = by_position(layer_out)
    d_input = laid(pieces, 1).reshape(batch_size, tokens, model_width)

    grad_bc = merged[:, : 2 * state_size]
    small = merged[:, 2 * state_size + 16 :].T.reshape(-1)
    ends = [sum(sizes[:k]) for k in range(len(sizes) + 1)]
    small = [small[ends[k] : ends[k + 1]] for k in range(len(sizes))]
    expert_sum = expert_sum.astype(f32)
    double = w_expert_gu.shape[2]
    grad_gu = [expert_sum[:, e * double : (e + 1) * double] for e in range(experts_dev)]
    expert_sum = expert_sum[:, experts_dev * double :]
    width = double // 2
    grad_down = [expert_sum[:, e * width : (e + 1) * width].T for e in range(experts_dev)]
    shared_sum = early_sum[:, 2 * inner_dev :]
    ff_dev = w_shared_down.shape[0]
    return (
        layer_out,
        d_input,
        small[5],
        jnp.stack([early_sum[:, inner_dev : 2 * inner_dev], late_sum[:, :inner_dev]]),
        grad_bc,
        late_sum[:, conv_width : conv_width + heads_dev],
        small[8],
        small[2].reshape(conv_taps, inner_all),
        small[3],
        small[6].reshape(conv_taps, 2 * state_size),
        small[7],
        small[9],
        small[4],
        early_sum[:, :inner_dev].T,
        small[0],
        small[1].reshape(experts_all, model_width).T,
        jnp.stack(grad_gu),
        jnp.stack(grad_down),
        jnp.stack([shared_sum[:, :ff_dev], shared_sum[:, ff_dev : 2 * ff_dev]]),
        shared_sum[:, 2 * ff_dev :].T,
    )


def solution(mesh):
    placed = (
        P("dp", "seq", None),
        P("dp", "seq", None),
        P("dp", "seq", "head"),
        P("dp", "seq", None),
        P(),
        P(None, None, "head"),
        P(),
        P(None, "head"),
        P("head"),
        P(None, "head"),
        P("head"),
        P(),
        P(),
        P("head"),
        P("head"),
        P("head", None),
        P(),
        P(),
        P(("seq", "head"), None, None),
        P(("seq", "head"), None, None),
        P(None, None, "head"),
        P("head", None),
    )
    return jax.shard_map(
        local,
        mesh=mesh,
        in_specs=placed,
        out_specs=(
            P("dp", "seq", None),
            P("dp", "seq", None),
            P(),
            P(None, ("dp", "seq"), "head"),
            P(),
            P(("dp", "seq"), "head"),
            P(),
            P(),
            P(),
            P(),
            P(),
            P(),
            P(),
            P("head", ("dp", "seq")),
            P(),
            P(),
            P(("seq", "head"), "dp", None),
            P(("seq", "head"), None, "dp"),
            P(None, ("dp", "seq"), "head"),
            P("head", ("dp", "seq")),
        ),
        check_vma=False,
    )
```
